32 devices in a mesh: groups: 2 (over x), dp: 8 (over z, y), tensor: 2 (over core).
Axes of the slice: x: 2, y: 2, z: 4, core: 2. Of those that a mesh axis runs over, the one named last changes fastest.
Arguments:
- grads: bfloat16 [16, 2, 2048, 512], P(('groups', 'dp'), None, 'tensor'), parts along dimension 0, may hold values from -144 to 144
- errors: float32 [16, 2, 2048, 512], P(('groups', 'dp'), None, 'tensor'), parts along dimension 0, may hold values from -4 to 4
- seeds: int32 [2], replicated, may hold values from 0 to 999999
Outputs:
- update: bfloat16 [4, 2048, 512], P('groups', 'tensor'), parts along dimension 0
- new_errors: float32 [16, 2, 2048, 512], P(('groups', 'dp'), None, 'tensor'), parts along dimension 0
The draws below stay inside these ranges and needn't reach their ends.
There are 2 independent parts, one for each index of `groups`. The reference program is written for one: setup_inputs(seed, part) draws one part's arguments, and reference() takes and returns one part's arrays. A program takes and returns all parts, laid end to end along the dimension named above; an argument that names none is the same for every part. Nothing has to cross between parts.
All inputs are finite; a program needn't handle non-finite values.
Results may differ from the reference program's by a relative error of at most 0.001.
Values sent between devices are 32-bit elements; how exact they have to be, the bound alone decides.
No kernel may reach another device: no remote copies, remote signals or barrier semaphores. Data moves between devices by JAX's collectives and lax.ppermute only.
A program may use at most 64 MiB of HBM per device.

```python
import math
import jax
import jax.numpy as jnp
from jax import lax

ROWS = 2048
COLS = 512
RANK = 4
MATS = 2
N_DP = 8


def draw_grads(key, part):
    key = jax.random.fold_in(key, 11)
    keys = jax.random.split(key, 4)
    common = jax.random.truncated_normal(keys[0], -4.0, 4.0, (MATS, ROWS, COLS), jnp.float32)
    owned = jax.random.truncated_normal(keys[1], -4.0, 4.0, (N_DP, MATS, ROWS, COLS), jnp.float32)
    lowest = 0.3
    row_scale = jnp.exp(jax.random.uniform(keys[2], (MATS, ROWS, 1), jnp.float32, math.log(lowest), math.log(lowest * 10.0)))
    col_scale = jnp.exp(jax.random.uniform(keys[3], (MATS, 1, COLS), jnp.float32, math.log(lowest), math.log(lowest * 10.0)))
    levels = 1.0 + 2.0 * jnp.arange(N_DP, dtype=jnp.float32) / max(N_DP - 1, 1)
    values = row_scale[None] * col_scale[None] * (common[None] + levels[:, None, None, None] * owned)
    return values.astype(jnp.bfloat16)


def level_of(key, extent, shards, least, high):
    level, own = 1.0, jax.random.fold_in(key, 6)
    for axis_at, parts in shards:
        heights = jnp.exp(jax.random.uniform(jax.random.fold_in(own, axis_at), (parts,), jnp.float32, least / len(shards), high / len(shards)))
        level = level * jnp.repeat(heights, extent[axis_at] // parts).reshape([-1 if axis == axis_at else 1 for axis in range(len(extent))])
    return level


def scatter_about(stream_key, shape, scale, bound, cuts=(), held_as=jnp.bfloat16):
    drawn = scale * jax.random.normal(stream_key, shape, jnp.float32)
    if cuts:
        drawn = drawn * level_of(stream_key, shape, cuts, -0.22, 0.18)
    return jnp.clip(drawn, -bound, bound).astype(held_as)


def setup_inputs(seed: int = 0, part: int = 0) -> dict:
    splits = jax.random.split(jax.random.key(seed), 4)
    own_keys = jax.random.split(jax.random.fold_in(splits[3], part), 4)
    return {
        "grads": draw_grads(jax.random.fold_in(jax.random.fold_in(splits[3], part), 71), part),
        "errors": scatter_about(own_keys[1], (N_DP, MATS, ROWS, COLS), 0.5, 4.0, ((0, 8), (2, 2)), jnp.float32),
        "seeds": jax.random.randint(splits[2], (MATS,), 0, 1000000).astype(jnp.int32),
    }


EPSILON = 1e-08

def initial_factor(seeds):
    index = (jnp.arange(RANK, dtype=jnp.int32)[:, None] * COLS + jnp.arange(COLS, dtype=jnp.int32)[None, :]).astype(jnp.int32)
    mixed = index[None, :, :] * 747796405 + seeds.astype(jnp.int32)[:, None, None] * 277803737 + 12345
    mixed = mixed.astype(jnp.int32)
    mixed = mixed ^ mixed >> 15
    mixed = (mixed * 1274126177).astype(jnp.int32)
    mixed = mixed ^ mixed >> 13
    lowbits = jnp.bitwise_and(mixed, 65535)
    return (lowbits.astype(jnp.float32) - 32767.5) / 32768.0

def orthogonalize(factor):
    columns = [factor[:, index] for index in range(RANK)]
    for index in range(RANK):
        current = columns[index]
        length = jnp.sqrt(lax.optimization_barrier(jnp.sum(current * current, axis=-1, keepdims=True))) + EPSILON
        current = current / length
        columns[index] = current
        for other in range(index + 1, RANK):
            inner = lax.optimization_barrier(jnp.sum(current * columns[other], axis=-1, keepdims=True))
            columns[other] = columns[other] - inner * current
    return jnp.stack(columns, axis=1)

def reference(grads, errors, seeds):
    merged = grads.astype(jnp.float32) + errors
    start_factor = initial_factor(seeds)
    left_sum = jnp.einsum('wmrc,mkc->mkr', merged, start_factor, precision=lax.Precision.HIGHEST) / N_DP
    left_factor = orthogonalize(left_sum)
    right_factor = jnp.einsum('wmrc,mkr->mkc', merged, left_factor, precision=lax.Precision.HIGHEST) / N_DP
    approx = jnp.einsum('mkr,mkc->mrc', left_factor, right_factor, precision=lax.Precision.HIGHEST)
    update = approx.astype(jnp.bfloat16)
    new_errors = merged - approx[None]
    return (update, new_errors)
```

```python
import jax
import jax.numpy as jnp
from jax import lax
from jax.sharding import PartitionSpec as P

RANK = 4


EPSILON = 1e-08


def initial_factor(seeds, rank_count, col_count):
    index = (
        jnp.arange(rank_count, dtype=jnp.int32)[:, None] * col_count
        + jnp.arange(col_count, dtype=jnp.int32)[None, :]
    )
    mixed = index[None, :, :] * 747796405 + seeds[:, None, None] * 277803737 + 12345
    mixed = mixed ^ mixed >> 15
    mixed = mixed * 1274126177
    mixed = mixed ^ mixed >> 13
    lowbits = jnp.bitwise_and(mixed, 65535)
    return (lowbits.astype(jnp.float32) - 32767.5) / 32768.0


def orthogonal(factor):
    rank_count = factor.shape[1]
    columns = [factor[:, index] for index in range(rank_count)]
    for index in range(rank_count):
        current = columns[index]
        length = jnp.sqrt(jnp.sum(current * current, axis=-1, keepdims=True)) + EPSILON
        current = current / length
        columns[index] = current
        for other in range(index + 1, rank_count):
            inner = jnp.sum(current * columns[other], axis=-1, keepdims=True)
            columns[other] = columns[other] - inner * current
    return jnp.stack(columns, axis=1)


def swap_sum(value, axis):
    count = lax.axis_size(axis)
    step = 1
    while step < count:
        pairs = [(index, index ^ step) for index in range(count)]
        value = value + lax.ppermute(value, axis, pairs)
        step *= 2
    return value


def body(grads, errors, seeds):
    merged = grads[0].astype(jnp.float32) + errors[0]
    replicas = lax.axis_size("dp")
    half = lax.axis_index("tensor")
    rows = merged.shape[1]
    start_factor = initial_factor(seeds, RANK, merged.shape[2])
    partial_value = jnp.einsum(
        "mrc,mkc->mkr", merged, start_factor, precision=lax.Precision.HIGHEST
    )
    summed = swap_sum(partial_value, "dp") / replicas
    other = lax.ppermute(summed, "tensor", [(0, 1), (1, 0)])
    first = jnp.where(half == 0, summed, other)
    second = jnp.where(half == 0, other, summed)
    whole = orthogonal(jnp.concatenate([first, second], axis=-1))
    left_factor = lax.dynamic_slice_in_dim(whole, half * rows, rows, axis=2)
    right_part = jnp.einsum("mrc,mkr->mkc", merged, left_factor, precision=lax.Precision.HIGHEST)
    right_factor = swap_sum(swap_sum(right_part, "tensor"), "dp") / replicas
    approx = jnp.einsum("mkr,mkc->mrc", left_factor, right_factor, precision=lax.Precision.HIGHEST)
    return (approx.astype(jnp.bfloat16), (merged - approx)[None])


def solution(mesh):
    in_specs = (
        P(("groups", "dp"), None, "tensor", None),
        P(("groups", "dp"), None, "tensor", None),
        P(),
    )
    out_specs = (P("groups", "tensor", None), P(("groups", "dp"), None, "tensor", None))
    return jax.shard_map(body, mesh=mesh, in_specs=in_specs, out_specs=out_specs, check_vma=False)
```

```python
import jax
import jax.numpy as jnp
from jax import lax
from jax.sharding import PartitionSpec as P

RANK = 4


EPSILON = 1e-08


def initial_factor(seeds, rank_count, col_count):
    index = (
        jnp.arange(rank_count, dtype=jnp.int32)[:, None] * col_count
        + jnp.arange(col_count, dtype=jnp.int32)[None, :]
    )
    mixed = index[None, :, :] * 747796405 + seeds[:, None, None] * 277803737 + 12345
    mixed = mixed ^ mixed >> 15
    mixed = mixed * 1274126177
    mixed = mixed ^ mixed >> 13
    lowbits = jnp.bitwise_and(mixed, 65535)
    return (lowbits.astype(jnp.float32) - 32767.5) / 32768.0


def orthogonal(factor):
    rank_count = factor.shape[1]
    columns = [factor[:, index] for index in range(rank_count)]
    for index in range(rank_count):
        current = columns[index]
        length = jnp.sqrt(jnp.sum(current * current, axis=-1, keepdims=True)) + EPSILON
        current = current / length
        columns[index] = current
        for other in range(index + 1, rank_count):
            inner = jnp.sum(current * columns[other], axis=-1, keepdims=True)
            columns[other] = columns[other] - inner * current
    return jnp.stack(columns, axis=1)


def body(grads, errors, seeds):
    merged = grads[0].astype(jnp.float32) + errors[0]
    replicas = lax.axis_size("dp")
    half = lax.axis_index("tensor")
    rows = merged.shape[1]
    start_factor = initial_factor(seeds, RANK, merged.shape[2])
    partial_value = jnp.einsum(
        "mrc,mkc->mkr", merged, start_factor, precision=lax.Precision.HIGHEST
    )
    mats, ranks = partial_value.shape[:2]
    pieces = partial_value.reshape(mats, ranks, replicas, rows // replicas)
    pieces = lax.all_to_all(pieces.transpose(2, 0, 1, 3), "dp", 0, 0)
    summed = jnp.sum(pieces, axis=0) / replicas
    parts = lax.all_gather(summed, ("tensor", "dp"))
    whole = orthogonal(parts.transpose(1, 2, 0, 3).reshape(mats, ranks, 2 * rows))
    left_factor = lax.dynamic_slice_in_dim(whole, half * rows, rows, axis=2)
    right_part = jnp.einsum("mrc,mkr->mkc", merged, left_factor, precision=lax.Precision.HIGHEST)
    right_factor = jnp.sum(lax.all_gather(right_part, ("dp", "tensor")), axis=0) / replicas
    approx = jnp.einsum("mkr,mkc->mrc", left_factor, right_factor, precision=lax.Precision.HIGHEST)
    return (approx.astype(jnp.bfloat16), (merged - approx)[None])


def solution(mesh):
    in_specs = (
        P(("groups", "dp"), None, "tensor", None),
        P(("groups", "dp"), None, "tensor", None),
        P(),
    )
    out_specs = (P("groups", "tensor", None), P(("groups", "dp"), None, "tensor", None))
    return jax.shard_map(body, mesh=mesh, in_specs=in_specs, out_specs=out_specs, check_vma=False)
```

```python
import functools

import jax
import jax.numpy as jnp
from jax import lax
from jax.experimental import pallas as pl
from jax.experimental.pallas import tpu as pltpu
from jax.sharding import PartitionSpec as P

RANK = 4
EPSILON = 1e-08
CHUNKS = 4
BF16 = jnp.bfloat16
F32 = jnp.float32


def halves(value):
    high = value.astype(BF16).astype(F32)
    return high, value - high


def start_rows(seeds_ref, mats, cols):
    shape = (mats * RANK, cols)
    row = lax.broadcasted_iota(jnp.int32, shape, 0)
    col = lax.broadcasted_iota(jnp.int32, shape, 1)
    mat = row // RANK
    seed = jnp.full(shape, seeds_ref[0], jnp.int32)
    for index in range(1, mats):
        seed = jnp.where(mat == index, seeds_ref[index], seed)
    mixed = ((row - mat * RANK) * cols + col) * 747796405 + seed * 277803737 + 12345
    mixed = mixed ^ (mixed >> 15)
    mixed = mixed * 1274126177
    mixed = mixed ^ (mixed >> 13)
    lowbits = jnp.bitwise_and(mixed, 65535)
    return (lowbits.astype(F32) - 32767.5) / 32768.0


def fold(mat, value, product):
    part = product[: value.shape[0]] + product[value.shape[0] :]
    row = lax.broadcasted_iota(jnp.int32, value.shape, 0)
    return jnp.where(row // RANK == mat, part, value)


def project_body(seeds_ref, grads_ref, errors_ref, left_ref, merged_ref, high_ref, low_ref, seed, gbuf, ebuf, seed_sem, sems):
    _, mats, rows, cols = grads_ref.shape
    size = rows // CHUNKS
    seed_copy = pltpu.make_async_copy(seeds_ref, seed, seed_sem)
    seed_copy.start()
    copies = []
    for mat in range(mats):
        for chunk in range(CHUNKS):
            at = pl.ds(chunk * size, size)
            slot = mat * CHUNKS + chunk
            pair = (
                pltpu.make_async_copy(grads_ref.at[0, mat, at], gbuf.at[mat, at], sems.at[0, slot]),
                pltpu.make_async_copy(errors_ref.at[0, mat, at], ebuf.at[mat, at], sems.at[1, slot]),
            )
            for copy in pair:
                copy.start()
            copies.append(pair)
    seed_copy.wait()
    start = start_rows(seed, mats, cols)
    weights = jnp.concatenate(halves(start), axis=0).astype(BF16)
    dims = (((1,), (1,)), ((), ()))
    for chunk in range(CHUNKS):
        at = pl.ds(chunk * size, size)
        left = jnp.zeros((mats * RANK, size), F32)
        for mat in range(mats):
            for copy in copies[mat * CHUNKS + chunk]:
                copy.wait()
            value = gbuf[mat, at].astype(F32) + ebuf[mat, at]
            high = value.astype(BF16)
            low = (value - high.astype(F32)).astype(BF16)
            merged_ref[mat, at] = value
            high_ref[mat, at] = high
            low_ref[mat, at] = low
            product = lax.dot_general(weights, high, dims, preferred_element_type=F32)
            product = product + lax.dot_general(weights, low, dims, preferred_element_type=F32)
            left = fold(mat, left, product)
        left_ref[:, at] = left


def project(seeds, grads, errors):
    _, mats, rows, cols = grads.shape
    return pl.pallas_call(
        project_body,
        out_shape=(
            jax.ShapeDtypeStruct((mats * RANK, rows), F32),
            pltpu.VMEM((mats, rows, cols), F32),
            pltpu.VMEM((mats, rows, cols), BF16),
            pltpu.VMEM((mats, rows, cols), BF16),
        ),
        in_specs=[pl.BlockSpec(memory_space=pltpu.HBM)] * 3,
        out_specs=[pl.BlockSpec(memory_space=pltpu.VMEM)] * 4,
        scratch_shapes=[
            pltpu.SMEM(seeds.shape, seeds.dtype),
            pltpu.VMEM((mats, rows, cols), BF16),
            pltpu.VMEM((mats, rows, cols), F32),
            pltpu.SemaphoreType.DMA,
            pltpu.SemaphoreType.DMA((2, mats * CHUNKS)),
        ],
        compiler_params=pltpu.CompilerParams(vmem_limit_bytes=24 * 2**20),
        name="project",
    )(*[pltpu.with_memory_space_constraint(value, pltpu.HBM) for value in (seeds, grads, errors)])


def spread(column, count):
    picked = jnp.concatenate(
        [jnp.broadcast_to(column[row : row + 1], (RANK, column.shape[1])) for row in range(0, count, RANK)],
        axis=0,
    )
    return picked


def orthogonal(mine, other):
    count = mine.shape[0]
    lane = lax.broadcasted_iota(jnp.int32, (count, 1), 0) % RANK
    for index in range(RANK):
        current = spread(mine[index : count - RANK + index + 1], count - RANK + 1)
        partner = spread(other[index : count - RANK + index + 1], count - RANK + 1)
        products = jnp.sum(mine * current, axis=1, keepdims=True) + jnp.sum(
            other * partner, axis=1, keepdims=True
        )
        square = spread(products[index : count - RANK + index + 1], count - RANK + 1)
        length = jnp.sqrt(square) + EPSILON
        current = current / length
        partner = partner / length
        inner = products / length
        mine = jnp.where(lane == index, current, jnp.where(lane > index, mine - inner * current, mine))
        other = jnp.where(lane == index, partner, jnp.where(lane > index, other - inner * partner, other))
    return mine


def reflect_body(mine_ref, other_ref, high_ref, low_ref, left_ref, right_ref):
    mats, rows, cols = high_ref.shape
    left = orthogonal(mine_ref[...], other_ref[...])
    left_ref[...] = left
    weights = jnp.concatenate(halves(left), axis=0).astype(BF16)
    right = jnp.zeros((mats * RANK, cols), F32)
    for mat in range(mats):
        product = jnp.dot(weights, high_ref[mat], preferred_element_type=F32)
        product = product + jnp.dot(weights, low_ref[mat], preferred_element_type=F32)
        right = fold(mat, right, product)
    right_ref[...] = right


def reflect(mine, other, high, low):
    mats, rows, cols = high.shape
    return pl.pallas_call(
        reflect_body,
        out_shape=(
            jax.ShapeDtypeStruct((mats * RANK, rows), F32),
            jax.ShapeDtypeStruct((mats * RANK, cols), F32),
        ),
        in_specs=[pl.BlockSpec(memory_space=pltpu.VMEM)] * 4,
        out_specs=[pl.BlockSpec(memory_space=pltpu.VMEM)] * 2,
        compiler_params=pltpu.CompilerParams(vmem_limit_bytes=24 * 2**20),
        name="reflect",
    )(mine, other, pltpu.with_memory_space_constraint(high, pltpu.VMEM), pltpu.with_memory_space_constraint(low, pltpu.VMEM))


def finish_body(scale, left_ref, right_ref, merged_ref, update_ref, errors_ref, ubuf, ebuf, sems):
    mats, rows, cols = merged_ref.shape
    size = rows // CHUNKS
    left_high, left_low = halves(left_ref[...])
    right_high, right_low = halves(right_ref[...] * scale)
    left = jnp.concatenate([left_high, left_low, left_high, left_low], axis=0).T.astype(BF16)
    right = jnp.concatenate([right_high, right_high, right_low, right_low], axis=0)
    row = lax.broadcasted_iota(jnp.int32, right.shape, 0) % (mats * RANK)
    copies = []
    for mat in range(mats):
        weights = jnp.where(row // RANK == mat, right, 0.0).astype(BF16)
        for chunk in range(CHUNKS):
            at = pl.ds(chunk * size, size)
            slot = mat * CHUNKS + chunk
            approx = jnp.dot(left[chunk * size : (chunk + 1) * size], weights, preferred_element_type=F32)
            ubuf[mat, at] = approx.astype(BF16)
            ebuf[mat, at] = merged_ref[mat, at] - approx
            for copy in (
                pltpu.make_async_copy(ubuf.at[mat, at], update_ref.at[mat, at], sems.at[0, slot]),
                pltpu.make_async_copy(ebuf.at[mat, at], errors_ref.at[0, mat, at], sems.at[1, slot]),
            ):
                copy.start()
                copies.append(copy)
    for copy in copies:
        copy.wait()


def finish(left, right, merged, scale):
    mats, rows, cols = merged.shape
    return pl.pallas_call(
        functools.partial(finish_body, scale),
        out_shape=(
            jax.ShapeDtypeStruct((mats, rows, cols), BF16),
            jax.ShapeDtypeStruct((1, mats, rows, cols), F32),
        ),
        in_specs=[pl.BlockSpec(memory_space=pltpu.VMEM)] * 3,
        out_specs=[pl.BlockSpec(memory_space=pltpu.HBM)] * 2,
        scratch_shapes=[
            pltpu.VMEM((mats, rows, cols), BF16),
            pltpu.VMEM((mats, rows, cols), F32),
            pltpu.SemaphoreType.DMA((2, mats * CHUNKS)),
        ],
        compiler_params=pltpu.CompilerParams(vmem_limit_bytes=24 * 2**20),
        name="finish",
    )(left, right, pltpu.with_memory_space_constraint(merged, pltpu.VMEM))


def swap_sum(value, axis):
    count = lax.axis_size(axis)
    step = 1
    while step < count:
        pairs = [(index, index ^ step) for index in range(count)]
        value = value + lax.ppermute(value, axis, pairs)
        step *= 2
    return value


def body(grads, errors, seeds):
    replicas = lax.axis_size("dp")
    left_part, merged, high, low = project(seeds, grads, errors)
    mine = swap_sum(left_part, "dp") / replicas
    other = lax.ppermute(mine, "tensor", [(0, 1), (1, 0)])
    left, right_part = reflect(mine, other, high, low)
    right = swap_sum(swap_sum(right_part, "tensor"), "dp")
    return finish(left, right, merged, 1.0 / replicas)


def solution(mesh):
    in_specs = (
        P(("groups", "dp"), None, "tensor", None),
        P(("groups", "dp"), None, "tensor", None),
        P(),
    )
    out_specs = (P("groups", "tensor", None), P(("groups", "dp"), None, "tensor", None))
    return jax.shard_map(body, mesh=mesh, in_specs=in_specs, out_specs=out_specs, check_vma=False)
```

```python
import functools

import jax
import jax.numpy as jnp
from jax import lax
from jax.experimental import pallas as pl
from jax.experimental.pallas import tpu as pltpu
from jax.sharding import PartitionSpec as P

RANK = 4
EPSILON = 1e-08
CHUNKS = 4
BF16 = jnp.bfloat16
F32 = jnp.float32


def halves(value):
    high = value.astype(BF16).astype(F32)
    return high, value - high


def start_rows(seeds_ref, mats, cols):
    shape = (mats * RANK, cols)
    row = lax.broadcasted_iota(jnp.int32, shape, 0)
    col = lax.broadcasted_iota(jnp.int32, shape, 1)
    mat = row // RANK
    seed = jnp.full(shape, seeds_ref[0], jnp.int32)
    for index in range(1, mats):
        seed = jnp.where(mat == index, seeds_ref[index], seed)
    mixed = ((row - mat * RANK) * cols + col) * 747796405 + seed * 277803737 + 12345
    mixed = mixed ^ (mixed >> 15)
    mixed = mixed * 1274126177
    mixed = mixed ^ (mixed >> 13)
    lowbits = jnp.bitwise_and(mixed, 65535)
    return (lowbits.astype(F32) - 32767.5) / 32768.0


def fold(mat, value, product):
    part = product[: value.shape[0]] + product[value.shape[0] :]
    row = lax.broadcasted_iota(jnp.int32, value.shape, 0)
    return jnp.where(row // RANK == mat, part, value)


def project_body(seeds_ref, grads_ref, errors_ref, left_ref, merged_ref, high_ref, low_ref, seed, gbuf, ebuf, seed_sem, sems):
    _, mats, rows, cols = grads_ref.shape
    size = rows // CHUNKS
    seed_copy = pltpu.make_async_copy(seeds_ref, seed, seed_sem)
    seed_copy.start()
    copies = []
    for mat in range(mats):
        for chunk in range(CHUNKS):
            at = pl.ds(chunk * size, size)
            slot = mat * CHUNKS + chunk
            pair = (
                pltpu.make_async_copy(grads_ref.at[0, mat, at], gbuf.at[mat, at], sems.at[0, slot]),
                pltpu.make_async_copy(errors_ref.at[0, mat, at], ebuf.at[mat, at], sems.at[1, slot]),
            )
            for copy in pair:
                copy.start()
            copies.append(pair)
    seed_copy.wait()
    start = start_rows(seed, mats, cols)
    weights = jnp.concatenate(halves(start), axis=0).astype(BF16)
    dims = (((1,), (1,)), ((), ()))
    for chunk in range(CHUNKS):
        at = pl.ds(chunk * size, size)
        left = jnp.zeros((mats * RANK, size), F32)
        for mat in range(mats):
            for copy in copies[mat * CHUNKS + chunk]:
                copy.wait()
            value = gbuf[mat, at].astype(F32) + ebuf[mat, at]
            high = value.astype(BF16)
            low = (value - high.astype(F32)).astype(BF16)
            merged_ref[mat, at] = value
            high_ref[mat, at] = high
            low_ref[mat, at] = low
            product = lax.dot_general(weights, high, dims, preferred_element_type=F32)
            product = product + lax.dot_general(weights, low, dims, preferred_element_type=F32)
            left = fold(mat, left, product)
        left_ref[:, at] = left


def project(seeds, grads, errors):
    _, mats, rows, cols = grads.shape
    return pl.pallas_call(
        project_body,
        out_shape=(
            jax.ShapeDtypeStruct((mats * RANK, rows), F32),
            pltpu.VMEM((mats, rows, cols), F32),
            pltpu.VMEM((mats, rows, cols), BF16),
            pltpu.VMEM((mats, rows, cols), BF16),
        ),
        in_specs=[pl.BlockSpec(memory_space=pltpu.HBM)] * 3,
        out_specs=[pl.BlockSpec(memory_space=pltpu.VMEM)] * 4,
        scratch_shapes=[
            pltpu.SMEM(seeds.shape, seeds.dtype),
            pltpu.VMEM((mats, rows, cols), BF16),
            pltpu.VMEM((mats, rows, cols), F32),
            pltpu.SemaphoreType.DMA,
            pltpu.SemaphoreType.DMA((2, mats * CHUNKS)),
        ],
        compiler_params=pltpu.CompilerParams(vmem_limit_bytes=24 * 2**20),
        name="project",
    )(*[pltpu.with_memory_space_constraint(value, pltpu.HBM) for value in (seeds, grads, errors)])


def spread(column, count):
    picked = jnp.concatenate(
        [jnp.broadcast_to(column[row : row + 1], (RANK, column.shape[1])) for row in range(0, count, RANK)],
        axis=0,
    )
    return picked


def orthogonal(mine, other):
    count = mine.shape[0]
    lane = lax.broadcasted_iota(jnp.int32, (count, 1), 0) % RANK
    for index in range(RANK):
        current = spread(mine[index : count - RANK + index + 1], count - RANK + 1)
        partner = spread(other[index : count - RANK + index + 1], count - RANK + 1)
        products = jnp.sum(mine * current, axis=1, keepdims=True) + jnp.sum(
            other * partner, axis=1, keepdims=True
        )
        square = spread(products[index : count - RANK + index + 1], count - RANK + 1)
        length = jnp.sqrt(square) + EPSILON
        current = current / length
        partner = partner / length
        inner = products / length
        mine = jnp.where(lane == index, current, jnp.where(lane > index, mine - inner * current, mine))
        other = jnp.where(lane == index, partner, jnp.where(lane > index, other - inner * partner, other))
    return mine


def reflect_body(scale, core_ref, whole_ref, high_ref, low_ref, left_ref, right_ref):
    mats, rows, cols = high_ref.shape
    upper = whole_ref[: mats * RANK] * scale
    lower = whole_ref[mats * RANK :] * scale
    first = core_ref[0] == 0
    left = orthogonal(jnp.where(first, lower, upper), jnp.where(first, upper, lower))
    left_ref[...] = left
    weights = jnp.concatenate(halves(left), axis=0).astype(BF16)
    right = jnp.zeros((mats * RANK, cols), F32)
    for mat in range(mats):
        product = jnp.dot(weights, high_ref[mat], preferred_element_type=F32)
        product = product + jnp.dot(weights, low_ref[mat], preferred_element_type=F32)
        right = fold(mat, right, product)
    right_ref[...] = right


def reflect(core, whole, high, low, scale):
    mats, rows, cols = high.shape
    return pl.pallas_call(
        functools.partial(reflect_body, scale),
        out_shape=(
            jax.ShapeDtypeStruct((mats * RANK, rows), F32),
            jax.ShapeDtypeStruct((mats * RANK, cols), F32),
        ),
        in_specs=[pl.BlockSpec(memory_space=pltpu.SMEM)] + [pl.BlockSpec(memory_space=pltpu.VMEM)] * 3,
        out_specs=[pl.BlockSpec(memory_space=pltpu.VMEM)] * 2,
        compiler_params=pltpu.CompilerParams(vmem_limit_bytes=24 * 2**20),
        name="reflect",
    )(core, whole, pltpu.with_memory_space_constraint(high, pltpu.VMEM), pltpu.with_memory_space_constraint(low, pltpu.VMEM))


def finish_body(scale, left_ref, right_ref, merged_ref, update_ref, errors_ref, ubuf, ebuf, sems):
    mats, rows, cols = merged_ref.shape
    size = rows // CHUNKS
    left_high, left_low = halves(left_ref[...])
    right_high, right_low = halves(right_ref[...] * scale)
    left = jnp.concatenate([left_high, left_low, left_high, left_low], axis=0).T.astype(BF16)
    right = jnp.concatenate([right_high, right_high, right_low, right_low], axis=0)
    row = lax.broadcasted_iota(jnp.int32, right.shape, 0) % (mats * RANK)
    copies = []
    for mat in range(mats):
        weights = jnp.where(row // RANK == mat, right, 0.0).astype(BF16)
        for chunk in range(CHUNKS):
            at = pl.ds(chunk * size, size)
            slot = mat * CHUNKS + chunk
            approx = jnp.dot(left[chunk * size : (chunk + 1) * size], weights, preferred_element_type=F32)
            ubuf[mat, at] = approx.astype(BF16)
            ebuf[mat, at] = merged_ref[mat, at] - approx
            for copy in (
                pltpu.make_async_copy(ubuf.at[mat, at], update_ref.at[mat, at], sems.at[0, slot]),
                pltpu.make_async_copy(ebuf.at[mat, at], errors_ref.at[0, mat, at], sems.at[1, slot]),
            ):
                copy.start()
                copies.append(copy)
    for copy in copies:
        copy.wait()


def finish(left, right, merged, scale):
    mats, rows, cols = merged.shape
    return pl.pallas_call(
        functools.partial(finish_body, scale),
        out_shape=(
            jax.ShapeDtypeStruct((mats, rows, cols), BF16),
            jax.ShapeDtypeStruct((1, mats, rows, cols), F32),
        ),
        in_specs=[pl.BlockSpec(memory_space=pltpu.VMEM)] * 3,
        out_specs=[pl.BlockSpec(memory_space=pltpu.HBM)] * 2,
        scratch_shapes=[
            pltpu.VMEM((mats, rows, cols), BF16),
            pltpu.VMEM((mats, rows, cols), F32),
            pltpu.SemaphoreType.DMA((2, mats * CHUNKS)),
        ],
        compiler_params=pltpu.CompilerParams(vmem_limit_bytes=24 * 2**20),
        name="finish",
    )(left, right, pltpu.with_memory_space_constraint(merged, pltpu.VMEM))


def spread_sum(value):
    count = lax.axis_size("dp")
    axes = ("dp", "tensor")
    terms = [
        lax.ppermute(value, axes, [(2 * at + 1, 2 * (at ^ step)) for at in range(count)])
        for step in range(count)
    ]
    while len(terms) > 1:
        terms = [terms[at] + terms[at + 1] for at in range(0, len(terms), 2)]
    return terms[0] + lax.ppermute(terms[0], "tensor", [(0, 1)])


def body(grads, errors, seeds):
    replicas = lax.axis_size("dp")
    left_part, merged, high, low = project(seeds, grads, errors)
    partner = lax.ppermute(left_part, "tensor", [(0, 1)])
    whole = spread_sum(jnp.concatenate([left_part, partner], axis=0))
    left, right_part = reflect(lax.axis_index("tensor").reshape(1), whole, high, low, 1.0 / replicas)
    right = spread_sum(right_part + lax.ppermute(right_part, "tensor", [(0, 1)]))
    return finish(left, right, merged, 1.0 / replicas)


def solution(mesh):
    in_specs = (
        P(("groups", "dp"), None, "tensor", None),
        P(("groups", "dp"), None, "tensor", None),
        P(),
    )
    out_specs = (P("groups", "tensor", None), P(("groups", "dp"), None, "tensor", None))
    return jax.shard_map(body, mesh=mesh, in_specs=in_specs, out_specs=out_specs, check_vma=False)
```

```python
import functools

import jax
import jax.numpy as jnp
from jax import lax
from jax.experimental import pallas as pl
from jax.experimental.pallas import tpu as pltpu
from jax.sharding import PartitionSpec as P

RANK = 4
EPSILON = 1e-08
CHUNKS = 4
BF16 = jnp.bfloat16
F32 = jnp.float32


def halves(value):
    high = value.astype(BF16).astype(F32)
    return high, value - high


def start_rows(seeds_ref, mats, cols):
    shape = (mats * RANK, cols)
    row = lax.broadcasted_iota(jnp.int32, shape, 0)
    col = lax.broadcasted_iota(jnp.int32, shape, 1)
    mat = row // RANK
    seed = jnp.full(shape, seeds_ref[0], jnp.int32)
    for index in range(1, mats):
        seed = jnp.where(mat == index, seeds_ref[index], seed)
    mixed = ((row - mat * RANK) * cols + col) * 747796405 + seed * 277803737 + 12345
    mixed = mixed ^ (mixed >> 15)
    mixed = mixed * 1274126177
    mixed = mixed ^ (mixed >> 13)
    lowbits = jnp.bitwise_and(mixed, 65535)
    return (lowbits.astype(F32) - 32767.5) / 32768.0


def fold(mat, value, product):
    part = product[: value.shape[0]] + product[value.shape[0] :]
    row = lax.broadcasted_iota(jnp.int32, value.shape, 0)
    return jnp.where(row // RANK == mat, part, value)


def project_body(seeds_ref, grads_ref, errors_ref, left_ref, merged_ref, high_ref, low_ref, seed, gbuf, ebuf, seed_sem, sems):
    _, mats, rows, cols = grads_ref.shape
    size = rows // CHUNKS
    seed_copy = pltpu.make_async_copy(seeds_ref, seed, seed_sem)
    seed_copy.start()
    copies = []
    for mat in range(mats):
        for chunk in range(CHUNKS):
            at = pl.ds(chunk * size, size)
            slot = mat * CHUNKS + chunk
            pair = (
                pltpu.make_async_copy(grads_ref.at[0, mat, at], gbuf.at[mat, at], sems.at[0, slot]),
                pltpu.make_async_copy(errors_ref.at[0, mat, at], ebuf.at[mat, at], sems.at[1, slot]),
            )
            for copy in pair:
                copy.start()
            copies.append(pair)
    seed_copy.wait()
    start = start_rows(seed, mats, cols)
    weights = jnp.concatenate(halves(start), axis=0).astype(BF16)
    dims = (((1,), (1,)), ((), ()))
    for chunk in range(CHUNKS):
        at = pl.ds(chunk * size, size)
        left = jnp.zeros((mats * RANK, size), F32)
        for mat in range(mats):
            for copy in copies[mat * CHUNKS + chunk]:
                copy.wait()
            value = gbuf[mat, at].astype(F32) + ebuf[mat, at]
            high = value.astype(BF16)
            low = (value - high.astype(F32)).astype(BF16)
            merged_ref[mat, at] = value
            high_ref[mat, at] = high
            low_ref[mat, at] = low
            product = lax.dot_general(weights, high, dims, preferred_element_type=F32)
            product = product + lax.dot_general(weights, low, dims, preferred_element_type=F32)
            left = fold(mat, left, product)
        left_ref[:, at] = left


def project(seeds, grads, errors):
    _, mats, rows, cols = grads.shape
    return pl.pallas_call(
        project_body,
        out_shape=(
            jax.ShapeDtypeStruct((mats * RANK, rows), F32),
            pltpu.VMEM((mats, rows, cols), F32),
            pltpu.VMEM((mats, rows, cols), BF16),
            pltpu.VMEM((mats, rows, cols), BF16),
        ),
        in_specs=[pl.BlockSpec(memory_space=pltpu.HBM)] * 3,
        out_specs=[pl.BlockSpec(memory_space=pltpu.VMEM)] * 4,
        scratch_shapes=[
            pltpu.SMEM(seeds.shape, seeds.dtype),
            pltpu.VMEM((mats, rows, cols), BF16),
            pltpu.VMEM((mats, rows, cols), F32),
            pltpu.SemaphoreType.DMA,
            pltpu.SemaphoreType.DMA((2, mats * CHUNKS)),
        ],
        compiler_params=pltpu.CompilerParams(vmem_limit_bytes=24 * 2**20),
        name="project",
    )(*[pltpu.with_memory_space_constraint(value, pltpu.HBM) for value in (seeds, grads, errors)])


def spread(column, count):
    picked = jnp.concatenate(
        [jnp.broadcast_to(column[row : row + 1], (RANK, column.shape[1])) for row in range(0, count, RANK)],
        axis=0,
    )
    return picked


def orthogonal(mine, other):
    count = mine.shape[0]
    lane = lax.broadcasted_iota(jnp.int32, (count, 1), 0) % RANK
    for index in range(RANK):
        current = spread(mine[index : count - RANK + index + 1], count - RANK + 1)
        partner = spread(other[index : count - RANK + index + 1], count - RANK + 1)
        products = jnp.sum(mine * current, axis=1, keepdims=True) + jnp.sum(
            other * partner, axis=1, keepdims=True
        )
        square = spread(products[index : count - RANK + index + 1], count - RANK + 1)
        length = jnp.sqrt(square) + EPSILON
        current = current / length
        partner = partner / length
        inner = products / length
        mine = jnp.where(lane == index, current, jnp.where(lane > index, mine - inner * current, mine))
        other = jnp.where(lane == index, partner, jnp.where(lane > index, other - inner * partner, other))
    return mine


def reflect_body(scale, core_ref, kept_ref, given_ref, high_ref, low_ref, left_ref, right_ref):
    mats, rows, cols = high_ref.shape
    half = mats * RANK
    first = core_ref[0] == 0
    mine = jnp.where(first, kept_ref[half:], given_ref[:half]) * scale
    other = jnp.where(first, kept_ref[:half], given_ref[half:]) * scale
    left = orthogonal(mine, other)
    left_ref[...] = left
    weights = jnp.concatenate(halves(left), axis=0).astype(BF16)
    right = jnp.zeros((mats * RANK, cols), F32)
    for mat in range(mats):
        product = jnp.dot(weights, high_ref[mat], preferred_element_type=F32)
        product = product + jnp.dot(weights, low_ref[mat], preferred_element_type=F32)
        right = fold(mat, right, product)
    right_ref[...] = right


def reflect(core, kept, given, high, low, scale):
    mats, rows, cols = high.shape
    return pl.pallas_call(
        functools.partial(reflect_body, scale),
        out_shape=(
            jax.ShapeDtypeStruct((mats * RANK, rows), F32),
            jax.ShapeDtypeStruct((mats * RANK, cols), F32),
        ),
        in_specs=[pl.BlockSpec(memory_space=pltpu.SMEM)] + [pl.BlockSpec(memory_space=pltpu.VMEM)] * 4,
        out_specs=[pl.BlockSpec(memory_space=pltpu.VMEM)] * 2,
        compiler_params=pltpu.CompilerParams(vmem_limit_bytes=24 * 2**20),
        name="reflect",
    )(core, kept, given, pltpu.with_memory_space_constraint(high, pltpu.VMEM), pltpu.with_memory_space_constraint(low, pltpu.VMEM))


def finish_body(scale, core_ref, left_ref, kept_ref, given_ref, merged_ref, update_ref, errors_ref, ubuf, ebuf, sems):
    mats, rows, cols = merged_ref.shape
    size = rows // CHUNKS
    left_high, left_low = halves(left_ref[...])
    right = jnp.where(core_ref[0] == 0, kept_ref[...], given_ref[...])
    right_high, right_low = halves(right * scale)
    left = jnp.concatenate([left_high, left_low, left_high, left_low], axis=0).T.astype(BF16)
    right = jnp.concatenate([right_high, right_high, right_low, right_low], axis=0)
    row = lax.broadcasted_iota(jnp.int32, right.shape, 0) % (mats * RANK)
    copies = []
    for mat in range(mats):
        weights = jnp.where(row // RANK == mat, right, 0.0).astype(BF16)
        for chunk in range(CHUNKS):
            at = pl.ds(chunk * size, size)
            slot = mat * CHUNKS + chunk
            approx = jnp.dot(left[chunk * size : (chunk + 1) * size], weights, preferred_element_type=F32)
            ubuf[mat, at] = approx.astype(BF16)
            ebuf[mat, at] = merged_ref[mat, at] - approx
            for copy in (
                pltpu.make_async_copy(ubuf.at[mat, at], update_ref.at[mat, at], sems.at[0, slot]),
                pltpu.make_async_copy(ebuf.at[mat, at], errors_ref.at[0, mat, at], sems.at[1, slot]),
            ):
                copy.start()
                copies.append(copy)
    for copy in copies:
        copy.wait()


def finish(core, left, kept, given, merged, scale):
    mats, rows, cols = merged.shape
    return pl.pallas_call(
        functools.partial(finish_body, scale),
        out_shape=(
            jax.ShapeDtypeStruct((mats, rows, cols), BF16),
            jax.ShapeDtypeStruct((1, mats, rows, cols), F32),
        ),
        in_specs=[pl.BlockSpec(memory_space=pltpu.SMEM)] + [pl.BlockSpec(memory_space=pltpu.VMEM)] * 4,
        out_specs=[pl.BlockSpec(memory_space=pltpu.HBM)] * 2,
        scratch_shapes=[
            pltpu.VMEM((mats, rows, cols), BF16),
            pltpu.VMEM((mats, rows, cols), F32),
            pltpu.SemaphoreType.DMA((2, mats * CHUNKS)),
        ],
        compiler_params=pltpu.CompilerParams(vmem_limit_bytes=24 * 2**20),
        name="finish",
    )(core, left, kept, given, pltpu.with_memory_space_constraint(merged, pltpu.VMEM))


def swap(value):
    return lax.ppermute(value, "tensor", [(0, 1), (1, 0)])


def spread_sum(value):
    count = lax.axis_size("dp")
    axes = ("dp", "tensor")
    last = max(count // 4, 1)
    step = 1
    while step < last:
        pairs = []
        for at in range(count):
            pairs += [(2 * at, 2 * at), (2 * at + 1, 2 * (at ^ step) + 1)]
        value = value + lax.ppermute(value, axes, pairs)
        step *= 2
    terms = []
    for offset in range(0, count, last):
        pairs = []
        for at in range(count):
            pairs += [(2 * at, 2 * at + 1), (2 * at + 1, 2 * (at ^ offset))]
        terms.append(lax.ppermute(value, axes, pairs))
    while len(terms) > 1:
        terms = [terms[at] + terms[at + 1] for at in range(0, len(terms), 2)]
    return terms[0], swap(terms[0])


def body(grads, errors, seeds):
    replicas = lax.axis_size("dp")
    core = lax.axis_index("tensor").reshape(1)
    left_part, merged, high, low = project(seeds, grads, errors)
    kept, given = spread_sum(jnp.concatenate([left_part, swap(left_part)], axis=0))
    left, right_part = reflect(core, kept, given, high, low, 1.0 / replicas)
    kept, given = spread_sum(right_part + swap(right_part))
    return finish(core, left, kept, given, merged, 1.0 / replicas)


def solution(mesh):
    in_specs = (
        P(("groups", "dp"), None, "tensor", None),
        P(("groups", "dp"), None, "tensor", None),
        P(),
    )
    out_specs = (P("groups", "tensor", None), P(("groups", "dp"), None, "tensor", None))
    return jax.shard_map(body, mesh=mesh, in_specs=in_specs, out_specs=out_specs, check_vma=False)
```

```python
import functools

import jax
import jax.numpy as jnp
from jax import lax
from jax.experimental import pallas as pl
from jax.experimental.pallas import tpu as pltpu
from jax.sharding import PartitionSpec as P

RANK = 4
EPSILON = 1e-08
CHUNKS = 4
BF16 = jnp.bfloat16
F32 = jnp.float32


def halves(value):
    high = value.astype(BF16).astype(F32)
    return high, value - high


def start_rows(seeds_ref, mats, cols):
    shape = (mats * RANK, cols)
    row = lax.broadcasted_iota(jnp.int32, shape, 0)
    col = lax.broadcasted_iota(jnp.int32, shape, 1)
    mat = row // RANK
    seed = jnp.full(shape, seeds_ref[0], jnp.int32)
    for index in range(1, mats):
        seed = jnp.where(mat == index, seeds_ref[index], seed)
    mixed = ((row - mat * RANK) * cols + col) * 747796405 + seed * 277803737 + 12345
    mixed = mixed ^ (mixed >> 15)
    mixed = mixed * 1274126177
    mixed = mixed ^ (mixed >> 13)
    lowbits = jnp.bitwise_and(mixed, 65535)
    return (lowbits.astype(F32) - 32767.5) / 32768.0


def fold(mat, value, product):
    part = product[: value.shape[0]] + product[value.shape[0] :]
    row = lax.broadcasted_iota(jnp.int32, value.shape, 0)
    return jnp.where(row // RANK == mat, part, value)


def project_body(seeds_ref, grads_ref, errors_ref, left_ref, merged_ref, high_ref, low_ref, seed, gbuf, ebuf, seed_sem, sems):
    _, mats, rows, cols = grads_ref.shape
    size = rows // CHUNKS
    seed_copy = pltpu.make_async_copy(seeds_ref, seed, seed_sem)
    seed_copy.start()
    copies = []
    for mat in range(mats):
        for chunk in range(CHUNKS):
            at = pl.ds(chunk * size, size)
            slot = mat * CHUNKS + chunk
            pair = (
                pltpu.make_async_copy(grads_ref.at[0, mat, at], gbuf.at[mat, at], sems.at[0, slot]),
                pltpu.make_async_copy(errors_ref.at[0, mat, at], ebuf.at[mat, at], sems.at[1, slot]),
            )
            for copy in pair:
                copy.start()
            copies.append(pair)
    seed_copy.wait()
    start = start_rows(seed, mats, cols)
    weights = jnp.concatenate(halves(start), axis=0).astype(BF16)
    dims = (((1,), (1,)), ((), ()))
    for chunk in range(CHUNKS):
        at = pl.ds(chunk * size, size)
        left = jnp.zeros((mats * RANK, size), F32)
        for mat in range(mats):
            for copy in copies[mat * CHUNKS + chunk]:
                copy.wait()
            value = gbuf[mat, at].astype(F32) + ebuf[mat, at]
            high = value.astype(BF16)
            low = (value - high.astype(F32)).astype(BF16)
            merged_ref[mat, at] = value
            high_ref[mat, at] = high
            low_ref[mat, at] = low
            product = lax.dot_general(weights, high, dims, preferred_element_type=F32)
            product = product + lax.dot_general(weights, low, dims, preferred_element_type=F32)
            left = fold(mat, left, product)
        left_ref[:, at] = left


def project(seeds, grads, errors):
    _, mats, rows, cols = grads.shape
    return pl.pallas_call(
        project_body,
        out_shape=(
            jax.ShapeDtypeStruct((mats * RANK, rows), F32),
            pltpu.VMEM((mats, rows, cols), F32),
            pltpu.VMEM((mats, rows, cols), BF16),
            pltpu.VMEM((mats, rows, cols), BF16),
        ),
        in_specs=[pl.BlockSpec(memory_space=pltpu.HBM)] * 3,
        out_specs=[pl.BlockSpec(memory_space=pltpu.VMEM)] * 4,
        scratch_shapes=[
            pltpu.SMEM(seeds.shape, seeds.dtype),
            pltpu.VMEM((mats, rows, cols), BF16),
            pltpu.VMEM((mats, rows, cols), F32),
            pltpu.SemaphoreType.DMA,
            pltpu.SemaphoreType.DMA((2, mats * CHUNKS)),
        ],
        compiler_params=pltpu.CompilerParams(vmem_limit_bytes=24 * 2**20),
        name="project",
    )(*[pltpu.with_memory_space_constraint(value, pltpu.HBM) for value in (seeds, grads, errors)])


def spread(column, count):
    picked = jnp.concatenate(
        [jnp.broadcast_to(column[row : row + 1], (RANK, column.shape[1])) for row in range(0, count, RANK)],
        axis=0,
    )
    return picked


def orthogonal(mine, other):
    count = mine.shape[0]
    lane = lax.broadcasted_iota(jnp.int32, (count, 1), 0) % RANK
    for index in range(RANK):
        current = spread(mine[index : count - RANK + index + 1], count - RANK + 1)
        partner = spread(other[index : count - RANK + index + 1], count - RANK + 1)
        products = jnp.sum(mine * current, axis=1, keepdims=True) + jnp.sum(
            other * partner, axis=1, keepdims=True
        )
        square = spread(products[index : count - RANK + index + 1], count - RANK + 1)
        length = jnp.sqrt(square) + EPSILON
        current = current / length
        partner = partner / length
        inner = products / length
        mine = jnp.where(lane == index, current, jnp.where(lane > index, mine - inner * current, mine))
        other = jnp.where(lane == index, partner, jnp.where(lane > index, other - inner * partner, other))
    return mine


def reflect_body(scale, both_ref, high_ref, low_ref, left_ref, right_ref):
    mats, rows, cols = high_ref.shape
    left = orthogonal(both_ref[0] * scale, both_ref[1] * scale)
    left_ref[...] = left
    weights = jnp.concatenate(halves(left), axis=0).astype(BF16)
    right = jnp.zeros((mats * RANK, cols), F32)
    for mat in range(mats):
        product = jnp.dot(weights, high_ref[mat], preferred_element_type=F32)
        product = product + jnp.dot(weights, low_ref[mat], preferred_element_type=F32)
        right = fold(mat, right, product)
    right_ref[...] = right


def reflect(both, high, low, scale):
    mats, rows, cols = high.shape
    return pl.pallas_call(
        functools.partial(reflect_body, scale),
        out_shape=(
            jax.ShapeDtypeStruct((mats * RANK, rows), F32),
            jax.ShapeDtypeStruct((mats * RANK, cols), F32),
        ),
        in_specs=[pl.BlockSpec(memory_space=pltpu.VMEM)] * 3,
        out_specs=[pl.BlockSpec(memory_space=pltpu.VMEM)] * 2,
        compiler_params=pltpu.CompilerParams(vmem_limit_bytes=24 * 2**20),
        name="reflect",
    )(both, pltpu.with_memory_space_constraint(high, pltpu.VMEM), pltpu.with_memory_space_constraint(low, pltpu.VMEM))


def finish_body(scale, left_ref, right_ref, merged_ref, update_ref, errors_ref, ubuf, ebuf, sems):
    mats, rows, cols = merged_ref.shape
    size = rows // CHUNKS
    left_high, left_low = halves(left_ref[...])
    right_high, right_low = halves(right_ref[...] * scale)
    left = jnp.concatenate([left_high, left_low, left_high, left_low], axis=0).T.astype(BF16)
    right = jnp.concatenate([right_high, right_high, right_low, right_low], axis=0)
    row = lax.broadcasted_iota(jnp.int32, right.shape, 0) % (mats * RANK)
    copies = []
    for mat in range(mats):
        weights = jnp.where(row // RANK == mat, right, 0.0).astype(BF16)
        for chunk in range(CHUNKS):
            at = pl.ds(chunk * size, size)
            slot = mat * CHUNKS + chunk
            approx = jnp.dot(left[chunk * size : (chunk + 1) * size], weights, preferred_element_type=F32)
            ubuf[mat, at] = approx.astype(BF16)
            ebuf[mat, at] = merged_ref[mat, at] - approx
            for copy in (
                pltpu.make_async_copy(ubuf.at[mat, at], update_ref.at[mat, at], sems.at[0, slot]),
                pltpu.make_async_copy(ebuf.at[mat, at], errors_ref.at[0, mat, at], sems.at[1, slot]),
            ):
                copy.start()
                copies.append(copy)
    for copy in copies:
        copy.wait()


def finish(left, right, merged, scale):
    mats, rows, cols = merged.shape
    return pl.pallas_call(
        functools.partial(finish_body, scale),
        out_shape=(
            jax.ShapeDtypeStruct((mats, rows, cols), BF16),
            jax.ShapeDtypeStruct((1, mats, rows, cols), F32),
        ),
        in_specs=[pl.BlockSpec(memory_space=pltpu.VMEM)] * 3,
        out_specs=[pl.BlockSpec(memory_space=pltpu.HBM)] * 2,
        scratch_shapes=[
            pltpu.VMEM((mats, rows, cols), BF16),
            pltpu.VMEM((mats, rows, cols), F32),
            pltpu.SemaphoreType.DMA((2, mats * CHUNKS)),
        ],
        compiler_params=pltpu.CompilerParams(vmem_limit_bytes=24 * 2**20),
        name="finish",
    )(left, right, pltpu.with_memory_space_constraint(merged, pltpu.VMEM))


def swap(value):
    return lax.ppermute(value, "tensor", [(0, 1), (1, 0)])


def cross_sum(value, turn):
    count = lax.axis_size("dp")
    step = 1
    while step < count:
        pairs = [(2 * at + core, 2 * (at ^ step) + 1 - core) for at in range(count) for core in range(2)]
        value = value + turn(lax.ppermute(value, ("dp", "tensor"), pairs))
        step *= 2
    return value


def body(grads, errors, seeds):
    replicas = lax.axis_size("dp")
    left_part, merged, high, low = project(seeds, grads, errors)
    both = jnp.stack([left_part, swap(left_part)], axis=0)
    both = cross_sum(both, lambda taken: lax.rev(taken, (0,)))
    left, right_part = reflect(both, high, low, 1.0 / replicas)
    right = cross_sum(right_part + swap(right_part), lambda taken: taken)
    return finish(left, right, merged, 1.0 / replicas)


def solution(mesh):
    in_specs = (
        P(("groups", "dp"), None, "tensor", None),
        P(("groups", "dp"), None, "tensor", None),
        P(),
    )
    out_specs = (P("groups", "tensor", None), P(("groups", "dp"), None, "tensor", None))
    return jax.shard_map(body, mesh=mesh, in_specs=in_specs, out_specs=out_specs, check_vma=False)
```

```python
import functools

import jax
import jax.numpy as jnp
from jax import lax
from jax.experimental import pallas as pl
from jax.experimental.pallas import tpu as pltpu
from jax.sharding import PartitionSpec as P

RANK = 4
EPSILON = 1e-08
CHUNKS = 4
BF16 = jnp.bfloat16
F32 = jnp.float32


def halves(value):
    high = value.astype(BF16).astype(F32)
    return high, value - high


def start_rows(seeds_ref, mats, cols):
    shape = (mats * RANK, cols)
    row = lax.broadcasted_iota(jnp.int32, shape, 0)
    col = lax.broadcasted_iota(jnp.int32, shape, 1)
    mat = row // RANK
    seed = jnp.full(shape, seeds_ref[0], jnp.int32)
    for index in range(1, mats):
        seed = jnp.where(mat == index, seeds_ref[index], seed)
    mixed = ((row - mat * RANK) * cols + col) * 747796405 + seed * 277803737 + 12345
    mixed = mixed ^ (mixed >> 15)
    mixed = mixed * 1274126177
    mixed = mixed ^ (mixed >> 13)
    lowbits = jnp.bitwise_and(mixed, 65535)
    return (lowbits.astype(F32) - 32767.5) / 32768.0


def fold(mat, value, product):
    part = product[: value.shape[0]] + product[value.shape[0] :]
    row = lax.broadcasted_iota(jnp.int32, value.shape, 0)
    return jnp.where(row // RANK == mat, part, value)


def project_body(seeds_ref, grads_ref, errors_ref, left_ref, gbuf, ebuf, seed, seed_sem, sems):
    _, mats, rows, cols = grads_ref.shape
    size = rows // CHUNKS
    seed_copy = pltpu.make_async_copy(seeds_ref, seed, seed_sem)
    seed_copy.start()
    copies = []
    for chunk in range(CHUNKS):
        at = pl.ds(chunk * size, size)
        for mat in range(mats):
            slot = chunk * mats + mat
            copies.append(pltpu.make_async_copy(grads_ref.at[0, mat, at], gbuf.at[mat, at], sems.at[0, slot]))
            copies.append(pltpu.make_async_copy(errors_ref.at[0, mat, at], ebuf.at[mat, at], sems.at[1, slot]))
    for copy in copies:
        copy.start()
    seed_copy.wait()
    start = start_rows(seed, mats, cols)
    weights = jnp.concatenate(halves(start), axis=0).astype(BF16)
    dims = (((1,), (1,)), ((), ()))
    for chunk in range(CHUNKS):
        at = pl.ds(chunk * size, size)
        left = jnp.zeros((mats * RANK, size), F32)
        for copy in copies[2 * mats * chunk : 2 * mats * (chunk + 1)]:
            copy.wait()
        for mat in range(mats):
            value = gbuf[mat, at].astype(F32) + ebuf[mat, at]
            high = value.astype(BF16)
            low = (value - high.astype(F32)).astype(BF16)
            product = lax.dot_general(weights, high, dims, preferred_element_type=F32)
            product = product + lax.dot_general(weights, low, dims, preferred_element_type=F32)
            left = fold(mat, left, product)
        left_ref[:, at] = left


def project(seeds, grads, errors):
    _, mats, rows, cols = grads.shape
    return pl.pallas_call(
        project_body,
        out_shape=(
            jax.ShapeDtypeStruct((mats * RANK, rows), F32),
            pltpu.VMEM((mats, rows, cols), BF16),
            pltpu.VMEM((mats, rows, cols), F32),
        ),
        in_specs=[pl.BlockSpec(memory_space=pltpu.HBM)] * 3,
        out_specs=[pl.BlockSpec(memory_space=pltpu.VMEM)] * 3,
        scratch_shapes=[
            pltpu.SMEM(seeds.shape, seeds.dtype),
            pltpu.SemaphoreType.DMA,
            pltpu.SemaphoreType.DMA((2, mats * CHUNKS)),
        ],
        compiler_params=pltpu.CompilerParams(vmem_limit_bytes=16 * 2**20),
        name="project",
    )(*[pltpu.with_memory_space_constraint(value, pltpu.HBM) for value in (seeds, grads, errors)])


def merge_body(grads_ref, errors_ref, merged_ref, high_ref, low_ref):
    mats, rows, cols = grads_ref.shape
    size = 64

    @pl.loop(0, rows // size)
    def _(step):
        at = pl.ds(pl.multiple_of(step * size, size), size)
        for mat in range(mats):
            value = grads_ref[mat, at].astype(F32) + errors_ref[mat, at]
            high = value.astype(BF16)
            merged_ref[mat, at] = value
            high_ref[mat, at] = high
            low_ref[mat, at] = (value - high.astype(F32)).astype(BF16)


def merge(grads, errors):
    shape = grads.shape
    return pl.pallas_call(
        merge_body,
        out_shape=(pltpu.VMEM(shape, F32), pltpu.VMEM(shape, BF16), pltpu.VMEM(shape, BF16)),
        in_specs=[pl.BlockSpec(memory_space=pltpu.VMEM)] * 2,
        out_specs=[pl.BlockSpec(memory_space=pltpu.VMEM)] * 3,
        compiler_params=pltpu.CompilerParams(vmem_limit_bytes=16 * 2**20),
        cost_estimate=pl.CostEstimate(flops=3 * grads.size, bytes_accessed=14 * grads.size, transcendentals=0),
        name="merge",
    )(*[pltpu.with_memory_space_constraint(value, pltpu.VMEM) for value in (grads, errors)])


def spread(column, count):
    picked = jnp.concatenate(
        [jnp.broadcast_to(column[row : row + 1], (RANK, column.shape[1])) for row in range(0, count, RANK)],
        axis=0,
    )
    return picked


def orthogonal(mine, other):
    count = mine.shape[0]
    lane = lax.broadcasted_iota(jnp.int32, (count, 1), 0) % RANK
    for index in range(RANK):
        current = spread(mine[index : count - RANK + index + 1], count - RANK + 1)
        partner = spread(other[index : count - RANK + index + 1], count - RANK + 1)
        products = jnp.sum(mine * current, axis=1, keepdims=True) + jnp.sum(
            other * partner, axis=1, keepdims=True
        )
        square = spread(products[index : count - RANK + index + 1], count - RANK + 1)
        length = jnp.sqrt(square) + EPSILON
        current = current / length
        partner = partner / length
        inner = products / length
        mine = jnp.where(lane == index, current, jnp.where(lane > index, mine - inner * current, mine))
        other = jnp.where(lane == index, partner, jnp.where(lane > index, other - inner * partner, other))
    return mine


def reflect_body(scale, mine_ref, other_ref, high_ref, low_ref, left_ref, right_ref):
    mats, rows, cols = high_ref.shape
    left = orthogonal(mine_ref[...] * scale, other_ref[...] * scale)
    left_ref[...] = left
    weights = jnp.concatenate(halves(left), axis=0).astype(BF16)
    right = jnp.zeros((mats * RANK, cols), F32)
    for mat in range(mats):
        product = jnp.dot(weights, high_ref[mat], preferred_element_type=F32)
        product = product + jnp.dot(weights, low_ref[mat], preferred_element_type=F32)
        right = fold(mat, right, product)
    right_ref[...] = right


def reflect(mine, other, high, low, scale):
    mats, rows, cols = high.shape
    return pl.pallas_call(
        functools.partial(reflect_body, scale),
        out_shape=(
            jax.ShapeDtypeStruct((mats * RANK, rows), F32),
            jax.ShapeDtypeStruct((mats * RANK, cols), F32),
        ),
        in_specs=[pl.BlockSpec(memory_space=pltpu.VMEM)] * 4,
        out_specs=[pl.BlockSpec(memory_space=pltpu.VMEM)] * 2,
        compiler_params=pltpu.CompilerParams(vmem_limit_bytes=24 * 2**20),
        name="reflect",
    )(mine, other, pltpu.with_memory_space_constraint(high, pltpu.VMEM), pltpu.with_memory_space_constraint(low, pltpu.VMEM))


def finish_body(scale, left_ref, right_ref, merged_ref, update_ref, errors_ref, ubuf, ebuf, sems):
    mats, rows, cols = merged_ref.shape
    size = rows // CHUNKS
    left_high, left_low = halves(left_ref[...])
    right_high, right_low = halves(right_ref[...] * scale)
    left = jnp.concatenate([left_high, left_low, left_high, left_low], axis=0).T.astype(BF16)
    right = jnp.concatenate([right_high, right_high, right_low, right_low], axis=0)
    row = lax.broadcasted_iota(jnp.int32, right.shape, 0) % (mats * RANK)
    copies = []
    for mat in range(mats):
        weights = jnp.where(row // RANK == mat, right, 0.0).astype(BF16)
        for chunk in range(CHUNKS):
            at = pl.ds(chunk * size, size)
            slot = mat * CHUNKS + chunk
            approx = jnp.dot(left[chunk * size : (chunk + 1) * size], weights, preferred_element_type=F32)
            ubuf[mat, at] = approx.astype(BF16)
            ebuf[mat, at] = merged_ref[mat, at] - approx
            for copy in (
                pltpu.make_async_copy(ubuf.at[mat, at], update_ref.at[mat, at], sems.at[0, slot]),
                pltpu.make_async_copy(ebuf.at[mat, at], errors_ref.at[0, mat, at], sems.at[1, slot]),
            ):
                copy.start()
                copies.append(copy)
    for copy in copies:
        copy.wait()


def finish(left, right, merged, scale):
    mats, rows, cols = merged.shape
    return pl.pallas_call(
        functools.partial(finish_body, scale),
        out_shape=(
            jax.ShapeDtypeStruct((mats, rows, cols), BF16),
            jax.ShapeDtypeStruct((1, mats, rows, cols), F32),
        ),
        in_specs=[pl.BlockSpec(memory_space=pltpu.VMEM)] * 3,
        out_specs=[pl.BlockSpec(memory_space=pltpu.HBM)] * 2,
        scratch_shapes=[
            pltpu.VMEM((mats, rows, cols), BF16),
            pltpu.VMEM((mats, rows, cols), F32),
            pltpu.SemaphoreType.DMA((2, mats * CHUNKS)),
        ],
        compiler_params=pltpu.CompilerParams(vmem_limit_bytes=24 * 2**20),
        name="finish",
    )(left, right, pltpu.with_memory_space_constraint(merged, pltpu.VMEM))


def swap(value, axis, step):
    pairs = [(index, index ^ step) for index in range(lax.axis_size(axis))]
    return lax.ppermute(value, axis, pairs)


def swap_sum(value, axis):
    count = lax.axis_size(axis)
    last = max(count // 4, 1)
    step = 1
    while step < last:
        value = value + swap(value, axis, step)
        step *= 2
    terms = [value] + [swap(value, axis, offset) for offset in range(last, count, last)]
    while len(terms) > 1:
        terms = [terms[at] + terms[at + 1] for at in range(0, len(terms), 2)]
    return terms[0]


def body(grads, errors, seeds):
    replicas = lax.axis_size("dp")
    left_part, grads, errors = project(seeds, grads, errors)
    merged, high, low = merge(grads, errors)
    mine = swap_sum(left_part, "dp")
    left, right_part = reflect(mine, swap(mine, "tensor", 1), high, low, 1.0 / replicas)
    right = swap_sum(right_part + swap(right_part, "tensor", 1), "dp")
    return finish(left, right, merged, 1.0 / replicas)


def solution(mesh):
    in_specs = (
        P(("groups", "dp"), None, "tensor", None),
        P(("groups", "dp"), None, "tensor", None),
        P(),
    )
    out_specs = (P("groups", "tensor", None), P(("groups", "dp"), None, "tensor", None))
    return jax.shard_map(body, mesh=mesh, in_specs=in_specs, out_specs=out_specs, check_vma=False)
```

```python
import functools

import jax
import jax.numpy as jnp
from jax import lax
from jax.experimental import pallas as pl
from jax.experimental.pallas import tpu as pltpu
from jax.sharding import PartitionSpec as P

RANK = 4
EPSILON = 1e-08
CHUNKS = 8
BF16 = jnp.bfloat16
F32 = jnp.float32


def halves(value):
    high = value.astype(BF16).astype(F32)
    return high, value - high


def start_rows(seeds_ref, mats, cols):
    shape = (mats * RANK, cols)
    row = lax.broadcasted_iota(jnp.int32, shape, 0)
    col = lax.broadcasted_iota(jnp.int32, shape, 1)
    mat = row // RANK
    seed = jnp.full(shape, seeds_ref[0], jnp.int32)
    for index in range(1, mats):
        seed = jnp.where(mat == index, seeds_ref[index], seed)
    mixed = ((row - mat * RANK) * cols + col) * 747796405 + seed * 277803737 + 12345
    mixed = mixed ^ (mixed >> 15)
    mixed = mixed * 1274126177
    mixed = mixed ^ (mixed >> 13)
    lowbits = jnp.bitwise_and(mixed, 65535)
    return (lowbits.astype(F32) - 32767.5) / 32768.0


def fold(mat, value, product):
    part = product[: value.shape[0]] + product[value.shape[0] :]
    row = lax.broadcasted_iota(jnp.int32, value.shape, 0)
    return jnp.where(row // RANK == mat, part, value)


def project_body(seeds_ref, grads_ref, errors_ref, left_ref, gbuf, ebuf, seed, seed_sem, sems):
    _, mats, rows, cols = grads_ref.shape
    size = rows // CHUNKS
    seed_copy = pltpu.make_async_copy(seeds_ref, seed, seed_sem)
    seed_copy.start()
    copies = []
    for chunk in range(CHUNKS):
        at = pl.ds(chunk * size, size)
        for mat in range(mats):
            slot = chunk * mats + mat
            copies.append(pltpu.make_async_copy(grads_ref.at[0, mat, at], gbuf.at[mat, at], sems.at[0, slot]))
            copies.append(pltpu.make_async_copy(errors_ref.at[0, mat, at], ebuf.at[mat, at], sems.at[1, slot]))
    for copy in copies:
        copy.start()
    seed_copy.wait()
    start = start_rows(seed, mats, cols)
    weights = jnp.concatenate(halves(start), axis=0).astype(BF16)
    dims = (((1,), (1,)), ((), ()))
    for chunk in range(CHUNKS):
        at = pl.ds(chunk * size, size)
        left = jnp.zeros((mats * RANK, size), F32)
        for copy in copies[2 * mats * chunk : 2 * mats * (chunk + 1)]:
            copy.wait()
        for mat in range(mats):
            value = gbuf[mat, at].astype(F32) + ebuf[mat, at]
            high = value.astype(BF16)
            low = (value - high.astype(F32)).astype(BF16)
            product = lax.dot_general(weights, high, dims, preferred_element_type=F32)
            product = product + lax.dot_general(weights, low, dims, preferred_element_type=F32)
            left = fold(mat, left, product)
        left_ref[:, at] = left


def project(seeds, grads, errors):
    _, mats, rows, cols = grads.shape
    return pl.pallas_call(
        project_body,
        out_shape=(
            jax.ShapeDtypeStruct((mats * RANK, rows), F32),
            pltpu.VMEM((mats, rows, cols), BF16),
            pltpu.VMEM((mats, rows, cols), F32),
        ),
        in_specs=[pl.BlockSpec(memory_space=pltpu.HBM)] * 3,
        out_specs=[pl.BlockSpec(memory_space=pltpu.VMEM)] * 3,
        scratch_shapes=[
            pltpu.SMEM(seeds.shape, seeds.dtype),
            pltpu.SemaphoreType.DMA,
            pltpu.SemaphoreType.DMA((2, mats * CHUNKS)),
        ],
        compiler_params=pltpu.CompilerParams(vmem_limit_bytes=16 * 2**20),
        name="project",
    )(*[pltpu.with_memory_space_constraint(value, pltpu.HBM) for value in (seeds, grads, errors)])


def merge_body(grads_ref, errors_ref, merged_ref, high_ref, low_ref):
    mats, rows, cols = grads_ref.shape
    size = 64

    @pl.loop(0, rows // size)
    def _(step):
        at = pl.ds(pl.multiple_of(step * size, size), size)
        for mat in range(mats):
            value = grads_ref[mat, at].astype(F32) + errors_ref[mat, at]
            high = value.astype(BF16)
            merged_ref[mat, at] = value
            high_ref[mat, at] = high
            low_ref[mat, at] = (value - high.astype(F32)).astype(BF16)


def merge(grads, errors):
    shape = grads.shape
    return pl.pallas_call(
        merge_body,
        out_shape=(pltpu.VMEM(shape, F32), pltpu.VMEM(shape, BF16), pltpu.VMEM(shape, BF16)),
        in_specs=[pl.BlockSpec(memory_space=pltpu.VMEM)] * 2,
        out_specs=[pl.BlockSpec(memory_space=pltpu.VMEM)] * 3,
        compiler_params=pltpu.CompilerParams(vmem_limit_bytes=16 * 2**20),
        cost_estimate=pl.CostEstimate(flops=3 * grads.size, bytes_accessed=14 * grads.size, transcendentals=0),
        name="merge",
    )(*[pltpu.with_memory_space_constraint(value, pltpu.VMEM) for value in (grads, errors)])


def pick(rows, index, count):
    return jnp.concatenate(
        [
            jnp.broadcast_to(rows[start + index : start + index + 1], (RANK, rows.shape[1]))
            for start in range(0, count, RANK)
        ],
        axis=0,
    )


def orthogonal(mine, other):
    count = mine.shape[0]
    rank = lax.broadcasted_iota(jnp.int32, (count, 1), 0) % RANK
    for index in range(RANK):
        current = pick(mine, index, count)
        partner = pick(other, index, count)
        products = jnp.sum(mine * current + other * partner, axis=1, keepdims=True)
        inverse = 1.0 / (jnp.sqrt(pick(products, index, count)) + EPSILON)
        inner = products * inverse
        weight = jnp.where(rank > index, inner * inverse, 0.0)
        here = rank == index
        mine = jnp.where(here, mine * inverse, mine - weight * current)
        if index < RANK - 1:
            other = jnp.where(here, other * inverse, other - weight * partner)
    return mine


def reflect_body(scale, mine_ref, other_ref, high_ref, low_ref, left_ref, right_ref):
    mats, rows, cols = high_ref.shape
    left = orthogonal(mine_ref[...] * scale, other_ref[...] * scale)
    left_ref[...] = left
    weights = jnp.concatenate(halves(left), axis=0).astype(BF16)
    right = jnp.zeros((mats * RANK, cols), F32)
    for mat in range(mats):
        product = jnp.dot(weights, high_ref[mat], preferred_element_type=F32)
        product = product + jnp.dot(weights, low_ref[mat], preferred_element_type=F32)
        right = fold(mat, right, product)
    right_ref[...] = right


def reflect(mine, other, high, low, scale):
    mats, rows, cols = high.shape
    return pl.pallas_call(
        functools.partial(reflect_body, scale),
        out_shape=(
            jax.ShapeDtypeStruct((mats * RANK, rows), F32),
            jax.ShapeDtypeStruct((mats * RANK, cols), F32),
        ),
        in_specs=[pl.BlockSpec(memory_space=pltpu.VMEM)] * 4,
        out_specs=[pl.BlockSpec(memory_space=pltpu.VMEM)] * 2,
        compiler_params=pltpu.CompilerParams(vmem_limit_bytes=24 * 2**20),
        name="reflect",
    )(mine, other, pltpu.with_memory_space_constraint(high, pltpu.VMEM), pltpu.with_memory_space_constraint(low, pltpu.VMEM))


def turn_body(left_ref, turned_ref):
    high, low = halves(left_ref[...])
    turned_ref[...] = jnp.concatenate([high, low, high, low], axis=0).T.astype(BF16)


def turn(left):
    count, rows = left.shape
    return pl.pallas_call(
        turn_body,
        out_shape=pltpu.VMEM((rows, 4 * count), BF16),
        in_specs=[pl.BlockSpec(memory_space=pltpu.VMEM)],
        out_specs=pl.BlockSpec(memory_space=pltpu.VMEM),
        compiler_params=pltpu.CompilerParams(vmem_limit_bytes=16 * 2**20),
        cost_estimate=pl.CostEstimate(flops=16 * left.size, bytes_accessed=64 * left.size, transcendentals=0),
        name="turn",
    )(left)


def finish_body(scale, left_ref, right_ref, merged_ref, update_ref, errors_ref, ubuf, ebuf, sems):
    mats, rows, cols = merged_ref.shape
    size = rows // CHUNKS
    high, low = halves(right_ref[...] * scale)
    right = jnp.concatenate([high, high, low, low], axis=0)
    row = lax.broadcasted_iota(jnp.int32, right.shape, 0) % (mats * RANK)
    copies = []
    for mat in range(mats):
        weights = jnp.where(row // RANK == mat, right, 0.0).astype(BF16)
        for chunk in range(CHUNKS):
            at = pl.ds(chunk * size, size)
            slot = mat * CHUNKS + chunk
            approx = jnp.dot(left_ref[at], weights, preferred_element_type=F32)
            ubuf[mat, at] = approx.astype(BF16)
            ebuf[mat, at] = merged_ref[mat, at] - approx
            for copy in (
                pltpu.make_async_copy(ubuf.at[mat, at], update_ref.at[mat, at], sems.at[0, slot]),
                pltpu.make_async_copy(ebuf.at[mat, at], errors_ref.at[0, mat, at], sems.at[1, slot]),
            ):
                copy.start()
                copies.append(copy)
    for copy in copies:
        copy.wait()


def finish(left, right, merged, scale):
    mats, rows, cols = merged.shape
    return pl.pallas_call(
        functools.partial(finish_body, scale),
        out_shape=(
            jax.ShapeDtypeStruct((mats, rows, cols), BF16),
            jax.ShapeDtypeStruct((1, mats, rows, cols), F32),
        ),
        in_specs=[pl.BlockSpec(memory_space=pltpu.VMEM)] * 3,
        out_specs=[pl.BlockSpec(memory_space=pltpu.HBM)] * 2,
        scratch_shapes=[
            pltpu.VMEM((mats, rows, cols), BF16),
            pltpu.VMEM((mats, rows, cols), F32),
            pltpu.SemaphoreType.DMA((2, mats * CHUNKS)),
        ],
        compiler_params=pltpu.CompilerParams(vmem_limit_bytes=16 * 2**20),
        name="finish",
    )(
        pltpu.with_memory_space_constraint(left, pltpu.VMEM),
        right,
        pltpu.with_memory_space_constraint(merged, pltpu.VMEM),
    )


def swap(value, axes, pairs):
    return lax.ppermute(value, axes, pairs + [(target, source) for source, target in pairs])


def swap_cores(value):
    return swap(value, "tensor", [(0, 1)])


def swap_chips(value, step, cross):
    lower = [at for at in range(lax.axis_size("dp")) if at < at ^ step]
    pairs = [(2 * at + core, 2 * (at ^ step) + (core ^ cross)) for at in lower for core in range(2)]
    return swap(value, ("dp", "tensor"), pairs)


def chips_sum(value, cross):
    count = lax.axis_size("dp")
    last = max(count // 4, 1)
    step = 1
    while step < last:
        value = value + swap_chips(value, step, cross)
        step *= 2
    terms = [value] + [swap_chips(value, offset, cross) for offset in range(last, count, last)]
    while len(terms) > 1:
        terms = [terms[at] + terms[at + 1] for at in range(0, len(terms), 2)]
    return terms[0]


def body(grads, errors, seeds):
    replicas = lax.axis_size("dp")
    left_part, grads, errors = project(seeds, grads, errors)
    merged, high, low = merge(grads, errors)
    mine = chips_sum(left_part, 0)
    left, right_part = reflect(mine, swap_cores(mine), high, low, 1.0 / replicas)
    right = chips_sum(right_part + swap_cores(right_part), 1)
    return finish(turn(left), right, merged, 1.0 / replicas)


def solution(mesh):
    in_specs = (
        P(("groups", "dp"), None, "tensor", None),
        P(("groups", "dp"), None, "tensor", None),
        P(),
    )
    out_specs = (P("groups", "tensor", None), P(("groups", "dp"), None, "tensor", None))
    return jax.shard_map(body, mesh=mesh, in_specs=in_specs, out_specs=out_specs, check_vma=False)
```

```python
import functools

import jax
import jax.numpy as jnp
from jax import lax
from jax.experimental import pallas as pl
from jax.experimental.pallas import tpu as pltpu
from jax.sharding import PartitionSpec as P

RANK = 4
EPSILON = 1e-08
CHUNKS = 4
SPLIT = ((3, 6), (5, 4), (1, 7))
SHARED = 2
BF16 = jnp.bfloat16
F32 = jnp.float32


def halves(value):
    high = value.astype(BF16).astype(F32)
    return high, value - high


def start_rows(seeds_ref, mats, cols):
    shape = (mats * RANK, cols)
    row = lax.broadcasted_iota(jnp.int32, shape, 0)
    col = lax.broadcasted_iota(jnp.int32, shape, 1)
    mat = row // RANK
    seed = jnp.full(shape, seeds_ref[0], jnp.int32)
    for index in range(1, mats):
        seed = jnp.where(mat == index, seeds_ref[index], seed)
    mixed = ((row - mat * RANK) * cols + col) * 747796405 + seed * 277803737 + 12345
    mixed = mixed ^ (mixed >> 15)
    mixed = mixed * 1274126177
    mixed = mixed ^ (mixed >> 13)
    lowbits = jnp.bitwise_and(mixed, 65535)
    return (lowbits.astype(F32) - 32767.5) / 32768.0


def fold(mat, value, product):
    part = product[: value.shape[0]] + product[value.shape[0] :]
    row = lax.broadcasted_iota(jnp.int32, value.shape, 0)
    return jnp.where(row // RANK == mat, part, value)


def project_body(seeds_ref, grads_ref, errors_ref, left_ref, gbuf, ebuf, seed, seed_sem, sems):
    _, mats, rows, cols = grads_ref.shape
    size = rows // CHUNKS
    seed_copy = pltpu.make_async_copy(seeds_ref, seed, seed_sem)
    seed_copy.start()
    copies = []
    for chunk in range(CHUNKS):
        at = pl.ds(chunk * size, size)
        for mat in range(mats):
            slot = chunk * mats + mat
            copies.append(pltpu.make_async_copy(grads_ref.at[0, mat, at], gbuf.at[mat, at], sems.at[0, slot]))
            copies.append(pltpu.make_async_copy(errors_ref.at[0, mat, at], ebuf.at[mat, at], sems.at[1, slot]))
    for copy in copies:
        copy.start()
    seed_copy.wait()
    start = start_rows(seed, mats, cols)
    weights = jnp.concatenate(halves(start), axis=0).T.astype(BF16)
    for chunk in range(CHUNKS):
        at = pl.ds(chunk * size, size)
        left = jnp.zeros((mats * RANK, size), F32)
        for copy in copies[2 * mats * chunk : 2 * mats * (chunk + 1)]:
            copy.wait()
        for mat in range(mats):
            value = gbuf[mat, at].astype(F32) + ebuf[mat, at]
            high = value.astype(BF16)
            low = (value - high.astype(F32)).astype(BF16)
            product = jnp.dot(high, weights, preferred_element_type=F32)
            product = product + jnp.dot(low, weights, preferred_element_type=F32)
            left = fold(mat, left, product.T)
        left_ref[:, at] = left


def project(seeds, grads, errors):
    _, mats, rows, cols = grads.shape
    return pl.pallas_call(
        project_body,
        out_shape=(
            jax.ShapeDtypeStruct((mats * RANK, rows), F32),
            pltpu.VMEM((mats, rows, cols), BF16),
            pltpu.VMEM((mats, rows, cols), F32),
        ),
        in_specs=[pl.BlockSpec(memory_space=pltpu.HBM)] * 3,
        out_specs=[pl.BlockSpec(memory_space=pltpu.VMEM)] * 3,
        scratch_shapes=[
            pltpu.SMEM(seeds.shape, seeds.dtype),
            pltpu.SemaphoreType.DMA,
            pltpu.SemaphoreType.DMA((2, mats * CHUNKS)),
        ],
        compiler_params=pltpu.CompilerParams(vmem_limit_bytes=16 * 2**20),
        name="project",
    )(*[pltpu.with_memory_space_constraint(value, pltpu.HBM) for value in (seeds, grads, errors)])


def merge_body(grads_ref, errors_ref, merged_ref, high_ref, low_ref):
    mats, rows, cols = grads_ref.shape
    size = 64

    @pl.loop(0, rows // size)
    def _(step):
        at = pl.ds(pl.multiple_of(step * size, size), size)
        for mat in range(mats):
            value = grads_ref[mat, at].astype(F32) + errors_ref[mat, at]
            high = value.astype(BF16)
            merged_ref[mat, at] = value
            high_ref[mat, at] = high
            low_ref[mat, at] = (value - high.astype(F32)).astype(BF16)


def merge(grads, errors):
    shape = grads.shape
    return pl.pallas_call(
        merge_body,
        out_shape=(pltpu.VMEM(shape, F32), pltpu.VMEM(shape, BF16), pltpu.VMEM(shape, BF16)),
        in_specs=[pl.BlockSpec(memory_space=pltpu.VMEM)] * 2,
        out_specs=[pl.BlockSpec(memory_space=pltpu.VMEM)] * 3,
        compiler_params=pltpu.CompilerParams(vmem_limit_bytes=16 * 2**20),
        cost_estimate=pl.CostEstimate(flops=3 * grads.size, bytes_accessed=14 * grads.size, transcendentals=0),
        name="merge",
    )(*[pltpu.with_memory_space_constraint(value, pltpu.VMEM) for value in (grads, errors)])


def pick(rows, index, count):
    return jnp.concatenate(
        [
            jnp.broadcast_to(rows[start + index : start + index + 1], (RANK, rows.shape[1]))
            for start in range(0, count, RANK)
        ],
        axis=0,
    )


def orthogonal(mine, other):
    count = mine.shape[0]
    rank = lax.broadcasted_iota(jnp.int32, (count, 1), 0) % RANK
    for index in range(RANK):
        current = pick(mine, index, count)
        partner = pick(other, index, count)
        products = jnp.sum(mine * current + other * partner, axis=1, keepdims=True)
        inverse = 1.0 / (jnp.sqrt(pick(products, index, count)) + EPSILON)
        inner = products * inverse
        weight = jnp.where(rank > index, inner * inverse, 0.0)
        here = rank == index
        mine = jnp.where(here, mine * inverse, mine - weight * current)
        if index < RANK - 1:
            other = jnp.where(here, other * inverse, other - weight * partner)
    return mine


def reflect_body(scale, mine_ref, other_ref, high_ref, low_ref, left_ref, right_ref):
    mats, rows, cols = high_ref.shape
    left = orthogonal(mine_ref[...] * scale, other_ref[...] * scale)
    left_ref[...] = left
    weights = jnp.concatenate(halves(left), axis=0).astype(BF16)
    right = jnp.zeros((mats * RANK, cols), F32)
    for mat in range(mats):
        product = jnp.dot(weights, high_ref[mat], preferred_element_type=F32)
        product = product + jnp.dot(weights, low_ref[mat], preferred_element_type=F32)
        right = fold(mat, right, product)
    right_ref[...] = right


def reflect(mine, other, high, low, scale):
    mats, rows, cols = high.shape
    return pl.pallas_call(
        functools.partial(reflect_body, scale),
        out_shape=(
            jax.ShapeDtypeStruct((mats * RANK, rows), F32),
            jax.ShapeDtypeStruct((mats * RANK, cols), F32),
        ),
        in_specs=[pl.BlockSpec(memory_space=pltpu.VMEM)] * 4,
        out_specs=[pl.BlockSpec(memory_space=pltpu.VMEM)] * 2,
        compiler_params=pltpu.CompilerParams(vmem_limit_bytes=24 * 2**20),
        name="reflect",
    )(mine, other, pltpu.with_memory_space_constraint(high, pltpu.VMEM), pltpu.with_memory_space_constraint(low, pltpu.VMEM))


def turn_body(left_ref, turned_ref):
    high, low = halves(left_ref[...])
    turned_ref[...] = jnp.concatenate([high, low, high, low], axis=0).T.astype(BF16)


def turn(left):
    count, rows = left.shape
    return pl.pallas_call(
        turn_body,
        out_shape=pltpu.VMEM((rows, 4 * count), BF16),
        in_specs=[pl.BlockSpec(memory_space=pltpu.VMEM)],
        out_specs=pl.BlockSpec(memory_space=pltpu.VMEM),
        compiler_params=pltpu.CompilerParams(vmem_limit_bytes=16 * 2**20),
        cost_estimate=pl.CostEstimate(flops=16 * left.size, bytes_accessed=64 * left.size, transcendentals=0),
        name="turn",
    )(left)


def total(own_ref, both_ref, taken_refs, given_refs):
    first = lax.axis_index("tensor") == 0
    terms = {0: own_ref[...], SHARED: both_ref[...]}
    for masks, taken_ref, given_ref in zip(SPLIT, taken_refs, given_refs):
        taken, given = taken_ref[...], given_ref[...]
        terms[masks[0]] = jnp.where(first, taken, given)
        terms[masks[1]] = jnp.where(first, given, taken)
    sums = [terms[index] for index in range(len(terms))]
    while len(sums) > 1:
        sums = [sums[at] + sums[at + 1] for at in range(0, len(sums), 2)]
    return sums[0]


def finish_body(scale, count, left_ref, merged_ref, own_ref, both_ref, *refs):
    taken_refs, given_refs = refs[:count], refs[count : 2 * count]
    update_ref, errors_ref, ubuf, ebuf, sems = refs[2 * count :]
    right = total(own_ref, both_ref, taken_refs, given_refs) * scale
    finish_rows(right, left_ref, merged_ref, update_ref, errors_ref, ubuf, ebuf, sems)


def finish_rows(right, left_ref, merged_ref, update_ref, errors_ref, ubuf, ebuf, sems):
    mats, rows, cols = merged_ref.shape
    size = rows // CHUNKS
    high, low = halves(right)
    right = jnp.concatenate([high, high, low, low], axis=0)
    row = lax.broadcasted_iota(jnp.int32, right.shape, 0) % (mats * RANK)
    copies = []
    for mat in range(mats):
        weights = jnp.where(row // RANK == mat, right, 0.0).astype(BF16)
        for chunk in range(CHUNKS):
            at = pl.ds(chunk * size, size)
            slot = mat * CHUNKS + chunk
            approx = jnp.dot(left_ref[at], weights, preferred_element_type=F32)
            ubuf[mat, at] = approx.astype(BF16)
            ebuf[mat, at] = merged_ref[mat, at] - approx
            for copy in (
                pltpu.make_async_copy(ubuf.at[mat, at], update_ref.at[mat, at], sems.at[0, slot]),
                pltpu.make_async_copy(ebuf.at[mat, at], errors_ref.at[0, mat, at], sems.at[1, slot]),
            ):
                copy.start()
                copies.append(copy)
    for copy in copies:
        copy.wait()


def finish(left, merged, own, both, taken, given, scale):
    mats, rows, cols = merged.shape
    return pl.pallas_call(
        functools.partial(finish_body, scale, len(taken)),
        out_shape=(
            jax.ShapeDtypeStruct((mats, rows, cols), BF16),
            jax.ShapeDtypeStruct((1, mats, rows, cols), F32),
        ),
        in_specs=[pl.BlockSpec(memory_space=pltpu.VMEM)] * (4 + 2 * len(taken)),
        out_specs=[pl.BlockSpec(memory_space=pltpu.HBM)] * 2,
        scratch_shapes=[
            pltpu.VMEM((mats, rows, cols), BF16),
            pltpu.VMEM((mats, rows, cols), F32),
            pltpu.SemaphoreType.DMA((2, mats * CHUNKS)),
        ],
        compiler_params=pltpu.CompilerParams(vmem_limit_bytes=16 * 2**20),
        name="finish",
    )(
        pltpu.with_memory_space_constraint(left, pltpu.VMEM),
        pltpu.with_memory_space_constraint(merged, pltpu.VMEM),
        own,
        both,
        *taken,
        *given,
    )


def swap(value, axes, pairs):
    return lax.ppermute(value, axes, pairs + [(target, source) for source, target in pairs])


def swap_cores(value):
    return swap(value, "tensor", [(0, 1)])


def swap_chips(value, masks, cross=0):
    pairs = []
    for core in range(2):
        for at in range(lax.axis_size("dp")):
            partner = at ^ masks[core]
            if at < partner:
                pairs.append((2 * at + core, 2 * partner + (core ^ cross)))
    return swap(value, ("dp", "tensor"), pairs)


def chips_sum(value):
    count = lax.axis_size("dp")
    last = max(count // 4, 1)
    step = 1
    while step < last:
        value = value + swap_chips(value, (step, step))
        step *= 2
    terms = [value] + [swap_chips(value, (offset, offset)) for offset in range(last, count, last)]
    while len(terms) > 1:
        terms = [terms[at] + terms[at + 1] for at in range(0, len(terms), 2)]
    return terms[0]


def chips_terms(value):
    count = lax.axis_size("dp")
    last = count // 8
    step = 1
    while step < last:
        value = value + swap_chips(value, (step, step), 1)
        step *= 2
    both = swap_chips(value, (SHARED * last, SHARED * last), 1)
    taken = [swap_chips(value, (lower * last, upper * last)) for lower, upper in SPLIT[::-1]][::-1]
    return value, both, taken, [swap_cores(term) for term in taken]


def body(grads, errors, seeds):
    replicas = lax.axis_size("dp")
    left_part, grads, errors = project(seeds, grads, errors)
    merged, high, low = merge(grads, errors)
    mine = chips_sum(left_part)
    left, right_part = reflect(mine, swap_cores(mine), high, low, 1.0 / replicas)
    terms = chips_terms(right_part + swap_cores(right_part))
    return finish(turn(left), merged, *terms, 1.0 / replicas)


def solution(mesh):
    in_specs = (
        P(("groups", "dp"), None, "tensor", None),
        P(("groups", "dp"), None, "tensor", None),
        P(),
    )
    out_specs = (P("groups", "tensor", None), P(("groups", "dp"), None, "tensor", None))
    return jax.shard_map(body, mesh=mesh, in_specs=in_specs, out_specs=out_specs, check_vma=False)
```

```python
import functools

import jax
import jax.numpy as jnp
from jax import lax
from jax.experimental import pallas as pl
from jax.experimental.pallas import tpu as pltpu
from jax.sharding import PartitionSpec as P

RANK = 4
EPSILON = 1e-08
CHUNKS = 4
BF16 = jnp.bfloat16
F32 = jnp.float32


def halves(value):
    high = value.astype(BF16).astype(F32)
    return high, value - high


def start_rows(seeds_ref, mats, cols):
    shape = (mats * RANK, cols)
    row = lax.broadcasted_iota(jnp.int32, shape, 0)
    col = lax.broadcasted_iota(jnp.int32, shape, 1)
    mat = row // RANK
    seed = jnp.full(shape, seeds_ref[0], jnp.int32)
    for index in range(1, mats):
        seed = jnp.where(mat == index, seeds_ref[index], seed)
    mixed = ((row - mat * RANK) * cols + col) * 747796405 + seed * 277803737 + 12345
    mixed = mixed ^ (mixed >> 15)
    mixed = mixed * 1274126177
    mixed = mixed ^ (mixed >> 13)
    lowbits = jnp.bitwise_and(mixed, 65535)
    return (lowbits.astype(F32) - 32767.5) / 32768.0


def fold(mat, value, product):
    part = product[: value.shape[0]] + product[value.shape[0] :]
    row = lax.broadcasted_iota(jnp.int32, value.shape, 0)
    return jnp.where(row // RANK == mat, part, value)


def project_body(seeds_ref, grads_ref, errors_ref, left_ref, gbuf, ebuf, seed, seed_sem, sems):
    _, mats, rows, cols = grads_ref.shape
    size = rows // CHUNKS
    seed_copy = pltpu.make_async_copy(seeds_ref, seed, seed_sem)
    seed_copy.start()
    copies = []
    for chunk in range(CHUNKS):
        at = pl.ds(chunk * size, size)
        for mat in range(mats):
            slot = chunk * mats + mat
            copies.append(pltpu.make_async_copy(grads_ref.at[0, mat, at], gbuf.at[mat, at], sems.at[0, slot]))
            copies.append(pltpu.make_async_copy(errors_ref.at[0, mat, at], ebuf.at[mat, at], sems.at[1, slot]))
    for copy in copies:
        copy.start()
    seed_copy.wait()
    start = start_rows(seed, mats, cols)
    weights = jnp.concatenate(halves(start), axis=0).astype(BF16)
    dims = (((1,), (1,)), ((), ()))
    for chunk in range(CHUNKS):
        at = pl.ds(chunk * size, size)
        left = jnp.zeros((mats * RANK, size), F32)
        for copy in copies[2 * mats * chunk : 2 * mats * (chunk + 1)]:
            copy.wait()
        for mat in range(mats):
            value = gbuf[mat, at].astype(F32) + ebuf[mat, at]
            high = value.astype(BF16)
            low = (value - high.astype(F32)).astype(BF16)
            product = lax.dot_general(weights, high, dims, preferred_element_type=F32)
            product = product + lax.dot_general(weights, low, dims, preferred_element_type=F32)
            left = fold(mat, left, product)
        left_ref[:, at] = left


def project(seeds, grads, errors):
    _, mats, rows, cols = grads.shape
    return pl.pallas_call(
        project_body,
        out_shape=(
            jax.ShapeDtypeStruct((mats * RANK, rows), F32),
            pltpu.VMEM((mats, rows, cols), BF16),
            pltpu.VMEM((mats, rows, cols), F32),
        ),
        in_specs=[pl.BlockSpec(memory_space=pltpu.HBM)] * 3,
        out_specs=[pl.BlockSpec(memory_space=pltpu.VMEM)] * 3,
        scratch_shapes=[
            pltpu.SMEM(seeds.shape, seeds.dtype),
            pltpu.SemaphoreType.DMA,
            pltpu.SemaphoreType.DMA((2, mats * CHUNKS)),
        ],
        compiler_params=pltpu.CompilerParams(vmem_limit_bytes=16 * 2**20),
        name="project",
    )(*[pltpu.with_memory_space_constraint(value, pltpu.HBM) for value in (seeds, grads, errors)])


def merge_body(grads_ref, errors_ref, merged_ref, high_ref, low_ref, zero_ref):
    mats, rows, cols = grads_ref.shape
    size = 64
    zero_ref[...] = jnp.zeros_like(zero_ref)

    @pl.loop(0, rows // size)
    def _(step):
        at = pl.ds(pl.multiple_of(step * size, size), size)
        for mat in range(mats):
            value = grads_ref[mat, at].astype(F32) + errors_ref[mat, at]
            high = value.astype(BF16)
            merged_ref[mat, at] = value
            high_ref[mat, at] = high
            low_ref[mat, at] = (value - high.astype(F32)).astype(BF16)


def merge(grads, errors):
    shape = grads.shape
    return pl.pallas_call(
        merge_body,
        out_shape=(
            pltpu.VMEM(shape, F32),
            pltpu.VMEM(shape, BF16),
            pltpu.VMEM(shape, BF16),
            jax.ShapeDtypeStruct((shape[0] * RANK, shape[1]), F32),
        ),
        in_specs=[pl.BlockSpec(memory_space=pltpu.VMEM)] * 2,
        out_specs=[pl.BlockSpec(memory_space=pltpu.VMEM)] * 4,
        compiler_params=pltpu.CompilerParams(vmem_limit_bytes=16 * 2**20),
        cost_estimate=pl.CostEstimate(flops=3 * grads.size, bytes_accessed=14 * grads.size, transcendentals=0),
        name="merge",
    )(*[pltpu.with_memory_space_constraint(value, pltpu.VMEM) for value in (grads, errors)])


def pick(rows, index, count):
    return jnp.concatenate(
        [
            jnp.broadcast_to(rows[start + index : start + index + 1], (RANK, rows.shape[1]))
            for start in range(0, count, RANK)
        ],
        axis=0,
    )


def orthogonal(mine, other):
    count = mine.shape[0]
    rank = lax.broadcasted_iota(jnp.int32, (count, 1), 0) % RANK
    for index in range(RANK):
        current = pick(mine, index, count)
        partner = pick(other, index, count)
        products = jnp.sum(mine * current + other * partner, axis=1, keepdims=True)
        inverse = 1.0 / (jnp.sqrt(pick(products, index, count)) + EPSILON)
        inner = products * inverse
        weight = jnp.where(rank > index, inner * inverse, 0.0)
        here = rank == index
        mine = jnp.where(here, mine * inverse, mine - weight * current)
        if index < RANK - 1:
            other = jnp.where(here, other * inverse, other - weight * partner)
    return mine


def reflect_body(scale, mine_ref, other_ref, high_ref, low_ref, left_ref, right_ref):
    mats, rows, cols = high_ref.shape
    left = orthogonal(mine_ref[...] * scale, other_ref[...] * scale)
    left_ref[...] = left
    weights = jnp.concatenate(halves(left), axis=0).astype(BF16)
    right = jnp.zeros((mats * RANK, cols), F32)
    for mat in range(mats):
        product = jnp.dot(weights, high_ref[mat], preferred_element_type=F32)
        product = product + jnp.dot(weights, low_ref[mat], preferred_element_type=F32)
        right = fold(mat, right, product)
    right_ref[...] = right


def reflect(mine, other, high, low, scale):
    mats, rows, cols = high.shape
    return pl.pallas_call(
        functools.partial(reflect_body, scale),
        out_shape=(
            jax.ShapeDtypeStruct((mats * RANK, rows), F32),
            jax.ShapeDtypeStruct((mats * RANK, cols), F32),
        ),
        in_specs=[pl.BlockSpec(memory_space=pltpu.VMEM)] * 4,
        out_specs=[pl.BlockSpec(memory_space=pltpu.VMEM)] * 2,
        compiler_params=pltpu.CompilerParams(vmem_limit_bytes=24 * 2**20),
        name="reflect",
    )(mine, other, pltpu.with_memory_space_constraint(high, pltpu.VMEM), pltpu.with_memory_space_constraint(low, pltpu.VMEM))


def turn_body(left_ref, turned_ref):
    high, low = halves(left_ref[...])
    turned_ref[...] = jnp.concatenate([high, low, high, low], axis=0).T.astype(BF16)


def turn(left):
    count, rows = left.shape
    return pl.pallas_call(
        turn_body,
        out_shape=pltpu.VMEM((rows, 4 * count), BF16),
        in_specs=[pl.BlockSpec(memory_space=pltpu.VMEM)],
        out_specs=pl.BlockSpec(memory_space=pltpu.VMEM),
        compiler_params=pltpu.CompilerParams(vmem_limit_bytes=16 * 2**20),
        cost_estimate=pl.CostEstimate(flops=16 * left.size, bytes_accessed=64 * left.size, transcendentals=0),
        name="turn",
    )(left)


def finish_body(scale, left_ref, right_ref, merged_ref, update_ref, errors_ref, ubuf, ebuf, sems):
    mats, rows, cols = merged_ref.shape
    size = rows // CHUNKS
    high, low = halves(right_ref[...] * scale)
    right = jnp.concatenate([high, high, low, low], axis=0)
    row = lax.broadcasted_iota(jnp.int32, right.shape, 0) % (mats * RANK)
    copies = []
    for mat in range(mats):
        weights = jnp.where(row // RANK == mat, right, 0.0).astype(BF16)
        for chunk in range(CHUNKS):
            at = pl.ds(chunk * size, size)
            slot = mat * CHUNKS + chunk
            approx = jnp.dot(left_ref[at], weights, preferred_element_type=F32)
            ubuf[mat, at] = approx.astype(BF16)
            ebuf[mat, at] = merged_ref[mat, at] - approx
            for copy in (
                pltpu.make_async_copy(ubuf.at[mat, at], update_ref.at[mat, at], sems.at[0, slot]),
                pltpu.make_async_copy(ebuf.at[mat, at], errors_ref.at[0, mat, at], sems.at[1, slot]),
            ):
                copy.start()
                copies.append(copy)
    for copy in copies:
        copy.wait()


def finish(left, right, merged, scale):
    mats, rows, cols = merged.shape
    return pl.pallas_call(
        functools.partial(finish_body, scale),
        out_shape=(
            jax.ShapeDtypeStruct((mats, rows, cols), BF16),
            jax.ShapeDtypeStruct((1, mats, rows, cols), F32),
        ),
        in_specs=[pl.BlockSpec(memory_space=pltpu.VMEM)] * 3,
        out_specs=[pl.BlockSpec(memory_space=pltpu.HBM)] * 2,
        scratch_shapes=[
            pltpu.VMEM((mats, rows, cols), BF16),
            pltpu.VMEM((mats, rows, cols), F32),
            pltpu.SemaphoreType.DMA((2, mats * CHUNKS)),
        ],
        compiler_params=pltpu.CompilerParams(vmem_limit_bytes=16 * 2**20),
        name="finish",
    )(
        pltpu.with_memory_space_constraint(left, pltpu.VMEM),
        right,
        pltpu.with_memory_space_constraint(merged, pltpu.VMEM),
    )


def swap(value, axes, pairs):
    return lax.ppermute(value, axes, pairs + [(target, source) for source, target in pairs])


def swap_cores(value):
    return swap(value, "tensor", [(0, 1)])


def swap_chips(value, step, cross):
    lower = [at for at in range(lax.axis_size("dp")) if at < at ^ step]
    pairs = [(2 * at + core, 2 * (at ^ step) + (core ^ cross)) for at in lower for core in range(2)]
    return swap(value, ("dp", "tensor"), pairs)


def chips_sum(value, cross, zero=0.0):
    count = lax.axis_size("dp")
    last = max(count // 4, 1)
    step = 1
    while step < last:
        value = value + (swap_chips(value, step, cross) + zero)
        zero = 0.0
        step *= 2
    terms = [value] + [swap_chips(value, offset, cross) for offset in range(last, count, last)]
    while len(terms) > 1:
        terms = [terms[at] + terms[at + 1] for at in range(0, len(terms), 2)]
    return terms[0]


def body(grads, errors, seeds):
    replicas = lax.axis_size("dp")
    left_part, grads, errors = project(seeds, grads, errors)
    merged, high, low, zero = merge(grads, errors)
    mine = chips_sum(left_part, 0, zero)
    left, right_part = reflect(mine, swap_cores(mine), high, low, 1.0 / replicas)
    right = chips_sum(right_part + swap_cores(right_part), 1)
    return finish(turn(left), right, merged, 1.0 / replicas)


def solution(mesh):
    in_specs = (
        P(("groups", "dp"), None, "tensor", None),
        P(("groups", "dp"), None, "tensor", None),
        P(),
    )
    out_specs = (P("groups", "tensor", None), P(("groups", "dp"), None, "tensor", None))
    return jax.shard_map(body, mesh=mesh, in_specs=in_specs, out_specs=out_specs, check_vma=False)
```

```python
import functools

import jax
import jax.numpy as jnp
from jax import lax
from jax.experimental import pallas as pl
from jax.experimental.pallas import tpu as pltpu
from jax.sharding import PartitionSpec as P

RANK = 4
EPSILON = 1e-08
CHUNKS = 4
BF16 = jnp.bfloat16
F32 = jnp.float32


def halves(value):
    high = value.astype(BF16).astype(F32)
    return high, value - high


def start_rows(seeds_ref, mats, cols):
    shape = (mats * RANK, cols)
    row = lax.broadcasted_iota(jnp.int32, shape, 0)
    col = lax.broadcasted_iota(jnp.int32, shape, 1)
    mat = row // RANK
    seed = jnp.full(shape, seeds_ref[0], jnp.int32)
    for index in range(1, mats):
        seed = jnp.where(mat == index, seeds_ref[index], seed)
    mixed = ((row - mat * RANK) * cols + col) * 747796405 + seed * 277803737 + 12345
    mixed = mixed ^ (mixed >> 15)
    mixed = mixed * 1274126177
    mixed = mixed ^ (mixed >> 13)
    lowbits = jnp.bitwise_and(mixed, 65535)
    return (lowbits.astype(F32) - 32767.5) / 32768.0


def fold(mat, value, product):
    part = product[: value.shape[0]] + product[value.shape[0] :]
    row = lax.broadcasted_iota(jnp.int32, value.shape, 0)
    return jnp.where(row // RANK == mat, part, value)


def project_body(seeds_ref, grads_ref, errors_ref, left_ref, gbuf, ebuf, seed, seed_sem, sems):
    _, mats, rows, cols = grads_ref.shape
    size = rows // CHUNKS
    seed_copy = pltpu.make_async_copy(seeds_ref, seed, seed_sem)
    seed_copy.start()
    copies = []
    for chunk in range(CHUNKS):
        at = pl.ds(chunk * size, size)
        for mat in range(mats):
            slot = chunk * mats + mat
            copies.append(pltpu.make_async_copy(grads_ref.at[0, mat, at], gbuf.at[mat, at], sems.at[0, slot]))
            copies.append(pltpu.make_async_copy(errors_ref.at[0, mat, at], ebuf.at[mat, at], sems.at[1, slot]))
    for copy in copies:
        copy.start()
    seed_copy.wait()
    start = start_rows(seed, mats, cols)
    weights = jnp.concatenate(halves(start), axis=0).astype(BF16)
    dims = (((1,), (1,)), ((), ()))
    for chunk in range(CHUNKS):
        at = pl.ds(chunk * size, size)
        left = jnp.zeros((mats * RANK, size), F32)
        for copy in copies[2 * mats * chunk : 2 * mats * (chunk + 1)]:
            copy.wait()
        for mat in range(mats):
            value = gbuf[mat, at].astype(F32) + ebuf[mat, at]
            high = value.astype(BF16)
            low = (value - high.astype(F32)).astype(BF16)
            product = lax.dot_general(weights, high, dims, preferred_element_type=F32)
            product = product + lax.dot_general(weights, low, dims, preferred_element_type=F32)
            left = fold(mat, left, product)
        left_ref[:, at] = left


def project(seeds, grads, errors):
    _, mats, rows, cols = grads.shape
    return pl.pallas_call(
        project_body,
        out_shape=(
            jax.ShapeDtypeStruct((mats * RANK, rows), F32),
            pltpu.VMEM((mats, rows, cols), BF16),
            pltpu.VMEM((mats, rows, cols), F32),
        ),
        in_specs=[pl.BlockSpec(memory_space=pltpu.HBM)] * 3,
        out_specs=[pl.BlockSpec(memory_space=pltpu.VMEM)] * 3,
        scratch_shapes=[
            pltpu.SMEM(seeds.shape, seeds.dtype),
            pltpu.SemaphoreType.DMA,
            pltpu.SemaphoreType.DMA((2, mats * CHUNKS)),
        ],
        compiler_params=pltpu.CompilerParams(vmem_limit_bytes=16 * 2**20),
        name="project",
    )(*[pltpu.with_memory_space_constraint(value, pltpu.HBM) for value in (seeds, grads, errors)])


def merge_body(grads_ref, errors_ref, merged_ref, high_ref, low_ref, zero_ref):
    mats, rows, cols = grads_ref.shape
    size = 64
    zero_ref[...] = jnp.zeros_like(zero_ref)

    @pl.loop(0, rows // size)
    def _(step):
        at = pl.ds(pl.multiple_of(step * size, size), size)
        for mat in range(mats):
            value = grads_ref[mat, at].astype(F32) + errors_ref[mat, at]
            high = value.astype(BF16)
            merged_ref[mat, at] = value
            high_ref[mat, at] = high
            low_ref[mat, at] = (value - high.astype(F32)).astype(BF16)


def merge(grads, errors):
    shape = grads.shape
    return pl.pallas_call(
        merge_body,
        out_shape=(
            pltpu.VMEM(shape, F32),
            pltpu.VMEM(shape, BF16),
            pltpu.VMEM(shape, BF16),
            jax.ShapeDtypeStruct((shape[0] * RANK, shape[1]), F32),
        ),
        in_specs=[pl.BlockSpec(memory_space=pltpu.VMEM)] * 2,
        out_specs=[pl.BlockSpec(memory_space=pltpu.VMEM)] * 4,
        compiler_params=pltpu.CompilerParams(vmem_limit_bytes=16 * 2**20),
        cost_estimate=pl.CostEstimate(flops=3 * grads.size, bytes_accessed=14 * grads.size, transcendentals=0),
        name="merge",
    )(*[pltpu.with_memory_space_constraint(value, pltpu.VMEM) for value in (grads, errors)])


def pick(rows, index, count):
    return jnp.concatenate(
        [
            jnp.broadcast_to(rows[start + index : start + index + 1], (RANK, rows.shape[1]))
            for start in range(0, count, RANK)
        ],
        axis=0,
    )


def orthogonal(mine, other):
    count = mine.shape[0]
    rank = lax.broadcasted_iota(jnp.int32, (count, 1), 0) % RANK
    for index in range(RANK):
        current = pick(mine, index, count)
        partner = pick(other, index, count)
        products = jnp.sum(mine * current + other * partner, axis=1, keepdims=True)
        inverse = 1.0 / (jnp.sqrt(pick(products, index, count)) + EPSILON)
        inner = products * inverse
        weight = jnp.where(rank > index, inner * inverse, 0.0)
        here = rank == index
        mine = jnp.where(here, mine * inverse, mine - weight * current)
        if index < RANK - 1:
            other = jnp.where(here, other * inverse, other - weight * partner)
    return mine


def reflect_body(scale, mine_ref, other_ref, high_ref, low_ref, left_ref, right_ref):
    mats, rows, cols = high_ref.shape
    left = orthogonal(mine_ref[...] * scale, other_ref[...] * scale)
    left_ref[...] = left
    weights = jnp.concatenate(halves(left), axis=0).astype(BF16)
    right = jnp.zeros((mats * RANK, cols), F32)
    for mat in range(mats):
        product = jnp.dot(weights, high_ref[mat], preferred_element_type=F32)
        product = product + jnp.dot(weights, low_ref[mat], preferred_element_type=F32)
        right = fold(mat, right, product)
    right_ref[...] = right


def reflect(mine, other, high, low, scale):
    mats, rows, cols = high.shape
    return pl.pallas_call(
        functools.partial(reflect_body, scale),
        out_shape=(
            jax.ShapeDtypeStruct((mats * RANK, rows), F32),
            jax.ShapeDtypeStruct((mats * RANK, cols), F32),
        ),
        in_specs=[pl.BlockSpec(memory_space=pltpu.VMEM)] * 4,
        out_specs=[pl.BlockSpec(memory_space=pltpu.VMEM)] * 2,
        compiler_params=pltpu.CompilerParams(vmem_limit_bytes=24 * 2**20),
        name="reflect",
    )(mine, other, pltpu.with_memory_space_constraint(high, pltpu.VMEM), pltpu.with_memory_space_constraint(low, pltpu.VMEM))


def turn_body(left_ref, turned_ref):
    high, low = halves(left_ref[...])
    turned_ref[...] = jnp.concatenate([high, low, high, low], axis=0).T.astype(BF16)


def turn(left):
    count, rows = left.shape
    return pl.pallas_call(
        turn_body,
        out_shape=pltpu.VMEM((rows, 4 * count), BF16),
        in_specs=[pl.BlockSpec(memory_space=pltpu.VMEM)],
        out_specs=pl.BlockSpec(memory_space=pltpu.VMEM),
        compiler_params=pltpu.CompilerParams(vmem_limit_bytes=16 * 2**20),
        cost_estimate=pl.CostEstimate(flops=16 * left.size, bytes_accessed=64 * left.size, transcendentals=0),
        name="turn",
    )(left)


def finish_body(scale, left_ref, right_ref, merged_ref, update_ref, errors_ref, ubuf, ebuf, sems):
    mats, rows, cols = merged_ref.shape
    size = rows // CHUNKS
    high, low = halves(right_ref[...] * scale)
    right = jnp.concatenate([high, high, low, low], axis=0)
    row = lax.broadcasted_iota(jnp.int32, right.shape, 0) % (mats * RANK)
    copies = []
    for mat in range(mats):
        weights = jnp.where(row // RANK == mat, right, 0.0).astype(BF16)
        for chunk in range(CHUNKS):
            at = pl.ds(chunk * size, size)
            slot = mat * CHUNKS + chunk
            approx = jnp.dot(left_ref[at], weights, preferred_element_type=F32)
            ubuf[mat, at] = approx.astype(BF16)
            ebuf[mat, at] = merged_ref[mat, at] - approx
            for copy in (
                pltpu.make_async_copy(ubuf.at[mat, at], update_ref.at[mat, at], sems.at[0, slot]),
                pltpu.make_async_copy(ebuf.at[mat, at], errors_ref.at[0, mat, at], sems.at[1, slot]),
            ):
                copy.start()
                copies.append(copy)
    for copy in copies:
        copy.wait()


def finish(left, right, merged, scale):
    mats, rows, cols = merged.shape
    return pl.pallas_call(
        functools.partial(finish_body, scale),
        out_shape=(
            jax.ShapeDtypeStruct((mats, rows, cols), BF16),
            jax.ShapeDtypeStruct((1, mats, rows, cols), F32),
        ),
        in_specs=[pl.BlockSpec(memory_space=pltpu.VMEM)] * 3,
        out_specs=[pl.BlockSpec(memory_space=pltpu.HBM)] * 2,
        scratch_shapes=[
            pltpu.VMEM((mats, rows, cols), BF16),
            pltpu.VMEM((mats, rows, cols), F32),
            pltpu.SemaphoreType.DMA((2, mats * CHUNKS)),
        ],
        compiler_params=pltpu.CompilerParams(vmem_limit_bytes=16 * 2**20),
        name="finish",
    )(
        pltpu.with_memory_space_constraint(left, pltpu.VMEM),
        right,
        pltpu.with_memory_space_constraint(merged, pltpu.VMEM),
    )


def swap(value, axes, pairs):
    return lax.ppermute(value, axes, pairs + [(target, source) for source, target in pairs])


def swap_cores(value):
    return swap(value, "tensor", [(0, 1)])


def swap_chips(value, step, cross):
    lower = [at for at in range(lax.axis_size("dp")) if at < at ^ step]
    pairs = [(2 * at + core, 2 * (at ^ step) + (core ^ cross)) for at in lower for core in range(2)]
    return swap(value, ("dp", "tensor"), pairs)


def chips_sum(value, cross, zero=0.0):
    count = lax.axis_size("dp")
    last = max(count // 4, 1)
    step = 1
    while step < last:
        value = value + (swap_chips(value, step, cross) + zero)
        zero = 0.0
        step *= 2
    terms = [swap_chips(value, offset, cross) for offset in range(count - last, 0, -last)]
    terms = [value] + terms[::-1]
    while len(terms) > 1:
        terms = [terms[at + 1] + terms[at] for at in range(0, len(terms), 2)]
    return terms[0]


def body(grads, errors, seeds):
    replicas = lax.axis_size("dp")
    left_part, grads, errors = project(seeds, grads, errors)
    merged, high, low, zero = merge(grads, errors)
    mine = chips_sum(left_part, 0, zero)
    left, right_part = reflect(mine, swap_cores(mine), high, low, 1.0 / replicas)
    right = chips_sum(right_part + swap_cores(right_part), 1)
    return finish(turn(left), right, merged, 1.0 / replicas)


def solution(mesh):
    in_specs = (
        P(("groups", "dp"), None, "tensor", None),
        P(("groups", "dp"), None, "tensor", None),
        P(),
    )
    out_specs = (P("groups", "tensor", None), P(("groups", "dp"), None, "tensor", None))
    return jax.shard_map(body, mesh=mesh, in_specs=in_specs, out_specs=out_specs, check_vma=False)
```

```python
import functools

import jax
import jax.numpy as jnp
from jax import lax
from jax.experimental import pallas as pl
from jax.experimental.pallas import tpu as pltpu
from jax.sharding import PartitionSpec as P

RANK = 4
EPSILON = 1e-08
CHUNKS = 4
BF16 = jnp.bfloat16
F32 = jnp.float32


def halves(value):
    high = value.astype(BF16).astype(F32)
    return high, value - high


def start_rows(seeds_ref, mats, cols):
    shape = (mats * RANK, cols)
    row = lax.broadcasted_iota(jnp.int32, shape, 0)
    col = lax.broadcasted_iota(jnp.int32, shape, 1)
    mat = row // RANK
    seed = jnp.full(shape, seeds_ref[0], jnp.int32)
    for index in range(1, mats):
        seed = jnp.where(mat == index, seeds_ref[index], seed)
    mixed = ((row - mat * RANK) * cols + col) * 747796405 + seed * 277803737 + 12345
    mixed = mixed ^ (mixed >> 15)
    mixed = mixed * 1274126177
    mixed = mixed ^ (mixed >> 13)
    lowbits = jnp.bitwise_and(mixed, 65535)
    return (lowbits.astype(F32) - 32767.5) / 32768.0


def fold(mat, value, product):
    part = product[: value.shape[0]] + product[value.shape[0] :]
    row = lax.broadcasted_iota(jnp.int32, value.shape, 0)
    return jnp.where(row // RANK == mat, part, value)


def project_body(seeds_ref, grads_ref, errors_ref, left_ref, gbuf, ebuf, seed, seed_sem, sems):
    _, mats, rows, cols = grads_ref.shape
    size = rows // CHUNKS
    seed_copy = pltpu.make_async_copy(seeds_ref, seed, seed_sem)
    seed_copy.start()
    copies = []
    for chunk in range(CHUNKS):
        at = pl.ds(chunk * size, size)
        for mat in range(mats):
            slot = chunk * mats + mat
            copies.append(pltpu.make_async_copy(grads_ref.at[0, mat, at], gbuf.at[mat, at], sems.at[0, slot]))
            copies.append(pltpu.make_async_copy(errors_ref.at[0, mat, at], ebuf.at[mat, at], sems.at[1, slot]))
    for copy in copies:
        copy.start()
    seed_copy.wait()
    start = start_rows(seed, mats, cols)
    weights = jnp.concatenate(halves(start), axis=0).astype(BF16)
    dims = (((1,), (1,)), ((), ()))
    for chunk in range(CHUNKS):
        at = pl.ds(chunk * size, size)
        left = jnp.zeros((mats * RANK, size), F32)
        for copy in copies[2 * mats * chunk : 2 * mats * (chunk + 1)]:
            copy.wait()
        for mat in range(mats):
            error = ebuf[mat, at]
            high = error.astype(BF16)
            low = (error - high.astype(F32)).astype(BF16)
            product = lax.dot_general(weights, gbuf[mat, at], dims, preferred_element_type=F32)
            product = product + lax.dot_general(weights, high, dims, preferred_element_type=F32)
            product = product + lax.dot_general(weights, low, dims, preferred_element_type=F32)
            left = fold(mat, left, product)
        left_ref[:, at] = left


def project(seeds, grads, errors):
    _, mats, rows, cols = grads.shape
    return pl.pallas_call(
        project_body,
        out_shape=(
            jax.ShapeDtypeStruct((mats * RANK, rows), F32),
            pltpu.VMEM((mats, rows, cols), BF16),
            pltpu.VMEM((mats, rows, cols), F32),
        ),
        in_specs=[pl.BlockSpec(memory_space=pltpu.HBM)] * 3,
        out_specs=[pl.BlockSpec(memory_space=pltpu.VMEM)] * 3,
        scratch_shapes=[
            pltpu.SMEM(seeds.shape, seeds.dtype),
            pltpu.SemaphoreType.DMA,
            pltpu.SemaphoreType.DMA((2, mats * CHUNKS)),
        ],
        compiler_params=pltpu.CompilerParams(vmem_limit_bytes=16 * 2**20),
        name="project",
    )(*[pltpu.with_memory_space_constraint(value, pltpu.HBM) for value in (seeds, grads, errors)])


def merge_body(grads_ref, errors_ref, merged_ref, high_ref, low_ref, zero_ref):
    mats, rows, cols = grads_ref.shape
    size = 64
    zero_ref[...] = jnp.zeros_like(zero_ref)

    @pl.loop(0, rows // size)
    def _(step):
        at = pl.ds(pl.multiple_of(step * size, size), size)
        for mat in range(mats):
            value = grads_ref[mat, at].astype(F32) + errors_ref[mat, at]
            high = value.astype(BF16)
            merged_ref[mat, at] = value
            high_ref[mat, at] = high
            low_ref[mat, at] = (value - high.astype(F32)).astype(BF16)


def merge(grads, errors):
    shape = grads.shape
    return pl.pallas_call(
        merge_body,
        out_shape=(
            pltpu.VMEM(shape, F32),
            pltpu.VMEM(shape, BF16),
            pltpu.VMEM(shape, BF16),
            jax.ShapeDtypeStruct((shape[0] * RANK, shape[1]), F32),
        ),
        in_specs=[pl.BlockSpec(memory_space=pltpu.VMEM)] * 2,
        out_specs=[pl.BlockSpec(memory_space=pltpu.VMEM)] * 4,
        compiler_params=pltpu.CompilerParams(vmem_limit_bytes=16 * 2**20),
        cost_estimate=pl.CostEstimate(flops=3 * grads.size, bytes_accessed=14 * grads.size, transcendentals=0),
        name="merge",
    )(*[pltpu.with_memory_space_constraint(value, pltpu.VMEM) for value in (grads, errors)])


def pick(rows, index, count):
    return jnp.concatenate(
        [
            jnp.broadcast_to(rows[start + index : start + index + 1], (RANK, rows.shape[1]))
            for start in range(0, count, RANK)
        ],
        axis=0,
    )


def orthogonal(mine, other):
    count = mine.shape[0]
    rank = lax.broadcasted_iota(jnp.int32, (count, 1), 0) % RANK
    for index in range(RANK):
        current = pick(mine, index, count)
        partner = pick(other, index, count)
        products = jnp.sum(mine * current + other * partner, axis=1, keepdims=True)
        inverse = 1.0 / (jnp.sqrt(pick(products, index, count)) + EPSILON)
        inner = products * inverse
        weight = jnp.where(rank > index, inner * inverse, 0.0)
        here = rank == index
        mine = jnp.where(here, mine * inverse, mine - weight * current)
        if index < RANK - 1:
            other = jnp.where(here, other * inverse, other - weight * partner)
    return mine


def reflect_body(scale, mine_ref, other_ref, high_ref, low_ref, left_ref, right_ref):
    mats, rows, cols = high_ref.shape
    left = orthogonal(mine_ref[...] * scale, other_ref[...] * scale)
    left_ref[...] = left
    weights = jnp.concatenate(halves(left), axis=0).astype(BF16)
    right = jnp.zeros((mats * RANK, cols), F32)
    for mat in range(mats):
        product = jnp.dot(weights, high_ref[mat], preferred_element_type=F32)
        product = product + jnp.dot(weights, low_ref[mat], preferred_element_type=F32)
        right = fold(mat, right, product)
    right_ref[...] = right


def reflect(mine, other, high, low, scale):
    mats, rows, cols = high.shape
    return pl.pallas_call(
        functools.partial(reflect_body, scale),
        out_shape=(
            jax.ShapeDtypeStruct((mats * RANK, rows), F32),
            jax.ShapeDtypeStruct((mats * RANK, cols), F32),
        ),
        in_specs=[pl.BlockSpec(memory_space=pltpu.VMEM)] * 4,
        out_specs=[pl.BlockSpec(memory_space=pltpu.VMEM)] * 2,
        compiler_params=pltpu.CompilerParams(vmem_limit_bytes=24 * 2**20),
        name="reflect",
    )(mine, other, pltpu.with_memory_space_constraint(high, pltpu.VMEM), pltpu.with_memory_space_constraint(low, pltpu.VMEM))


def turn_body(left_ref, turned_ref):
    high, low = halves(left_ref[...])
    turned_ref[...] = jnp.concatenate([high, low, high, low], axis=0).T.astype(BF16)


def turn(left):
    count, rows = left.shape
    return pl.pallas_call(
        turn_body,
        out_shape=pltpu.VMEM((rows, 4 * count), BF16),
        in_specs=[pl.BlockSpec(memory_space=pltpu.VMEM)],
        out_specs=pl.BlockSpec(memory_space=pltpu.VMEM),
        compiler_params=pltpu.CompilerParams(vmem_limit_bytes=16 * 2**20),
        cost_estimate=pl.CostEstimate(flops=16 * left.size, bytes_accessed=64 * left.size, transcendentals=0),
        name="turn",
    )(left)


def finish_body(scale, left_ref, right_ref, merged_ref, update_ref, errors_ref, ubuf, ebuf, sems):
    mats, rows, cols = merged_ref.shape
    size = rows // CHUNKS
    high, low = halves(right_ref[...] * scale)
    right = jnp.concatenate([high, high, low, low], axis=0)
    row = lax.broadcasted_iota(jnp.int32, right.shape, 0) % (mats * RANK)
    copies = []
    for mat in range(mats):
        weights = jnp.where(row // RANK == mat, right, 0.0).astype(BF16)
        for chunk in range(CHUNKS):
            at = pl.ds(chunk * size, size)
            slot = mat * CHUNKS + chunk
            approx = jnp.dot(left_ref[at], weights, preferred_element_type=F32)
            ubuf[mat, at] = approx.astype(BF16)
            ebuf[mat, at] = merged_ref[mat, at] - approx
            for copy in (
                pltpu.make_async_copy(ubuf.at[mat, at], update_ref.at[mat, at], sems.at[0, slot]),
                pltpu.make_async_copy(ebuf.at[mat, at], errors_ref.at[0, mat, at], sems.at[1, slot]),
            ):
                copy.start()
                copies.append(copy)
    for copy in copies:
        copy.wait()


def finish(left, right, merged, scale):
    mats, rows, cols = merged.shape
    return pl.pallas_call(
        functools.partial(finish_body, scale),
        out_shape=(
            jax.ShapeDtypeStruct((mats, rows, cols), BF16),
            jax.ShapeDtypeStruct((1, mats, rows, cols), F32),
        ),
        in_specs=[pl.BlockSpec(memory_space=pltpu.VMEM)] * 3,
        out_specs=[pl.BlockSpec(memory_space=pltpu.HBM)] * 2,
        scratch_shapes=[
            pltpu.VMEM((mats, rows, cols), BF16),
            pltpu.VMEM((mats, rows, cols), F32),
            pltpu.SemaphoreType.DMA((2, mats * CHUNKS)),
        ],
        compiler_params=pltpu.CompilerParams(vmem_limit_bytes=16 * 2**20),
        name="finish",
    )(
        pltpu.with_memory_space_constraint(left, pltpu.VMEM),
        right,
        pltpu.with_memory_space_constraint(merged, pltpu.VMEM),
    )


def swap(value, axes, pairs):
    return lax.ppermute(value, axes, pairs + [(target, source) for source, target in pairs])


def swap_cores(value):
    return swap(value, "tensor", [(0, 1)])


def swap_chips(value, step, cross):
    lower = [at for at in range(lax.axis_size("dp")) if at < at ^ step]
    pairs = [(2 * at + core, 2 * (at ^ step) + (core ^ cross)) for at in lower for core in range(2)]
    return swap(value, ("dp", "tensor"), pairs)


def chips_sum(value, cross, zero=0.0):
    count = lax.axis_size("dp")
    last = max(count // 4, 1)
    step = 1
    while step < last:
        value = value + (swap_chips(value, step, cross) + zero)
        zero = 0.0
        step *= 2
    terms = [swap_chips(value, offset, cross) for offset in range(count - last, 0, -last)]
    terms = [value] + terms[::-1]
    while len(terms) > 1:
        terms = [terms[at + 1] + terms[at] for at in range(0, len(terms), 2)]
    return terms[0]


def body(grads, errors, seeds):
    replicas = lax.axis_size("dp")
    left_part, grads, errors = project(seeds, grads, errors)
    merged, high, low, zero = merge(grads, errors)
    mine = chips_sum(left_part, 0, zero)
    left, right_part = reflect(mine, swap_cores(mine), high, low, 1.0 / replicas)
    right = chips_sum(right_part + swap_cores(right_part), 1)
    return finish(turn(left), right, merged, 1.0 / replicas)


def solution(mesh):
    in_specs = (
        P(("groups", "dp"), None, "tensor", None),
        P(("groups", "dp"), None, "tensor", None),
        P(),
    )
    out_specs = (P("groups", "tensor", None), P(("groups", "dp"), None, "tensor", None))
    return jax.shard_map(body, mesh=mesh, in_specs=in_specs, out_specs=out_specs, check_vma=False)
```

```python
import functools

import jax
import jax.numpy as jnp
from jax import lax
from jax.experimental import pallas as pl
from jax.experimental.pallas import tpu as pltpu
from jax.sharding import PartitionSpec as P

RANK = 4
EPSILON = 1e-08
CHUNKS = 4
BF16 = jnp.bfloat16
F32 = jnp.float32


def halves(value):
    high = value.astype(BF16).astype(F32)
    return high, value - high


def start_rows(seeds_ref, mats, cols):
    shape = (mats * RANK, cols)
    row = lax.broadcasted_iota(jnp.int32, shape, 0)
    col = lax.broadcasted_iota(jnp.int32, shape, 1)
    mat = row // RANK
    seed = jnp.full(shape, seeds_ref[0], jnp.int32)
    for index in range(1, mats):
        seed = jnp.where(mat == index, seeds_ref[index], seed)
    mixed = ((row - mat * RANK) * cols + col) * 747796405 + seed * 277803737 + 12345
    mixed = mixed ^ (mixed >> 15)
    mixed = mixed * 1274126177
    mixed = mixed ^ (mixed >> 13)
    lowbits = jnp.bitwise_and(mixed, 65535)
    return (lowbits.astype(F32) - 32767.5) / 32768.0


def fold(mat, value, product):
    part = product[: value.shape[0]] + product[value.shape[0] :]
    row = lax.broadcasted_iota(jnp.int32, value.shape, 0)
    return jnp.where(row // RANK == mat, part, value)


def project_body(seeds_ref, grads_ref, errors_ref, left_ref, gbuf, ebuf, seed, seed_sem, sems):
    _, mats, rows, cols = grads_ref.shape
    size = rows // CHUNKS
    seed_copy = pltpu.make_async_copy(seeds_ref, seed, seed_sem)
    seed_copy.start()
    copies = []
    for chunk in range(CHUNKS):
        at = pl.ds(chunk * size, size)
        for mat in range(mats):
            slot = chunk * mats + mat
            copies.append(pltpu.make_async_copy(grads_ref.at[0, mat, at], gbuf.at[mat, at], sems.at[0, slot]))
            copies.append(pltpu.make_async_copy(errors_ref.at[0, mat, at], ebuf.at[mat, at], sems.at[1, slot]))
    for copy in copies:
        copy.start()
    seed_copy.wait()
    start = start_rows(seed, mats, cols)
    weights = jnp.concatenate(halves(start), axis=0).astype(BF16)
    dims = (((1,), (1,)), ((), ()))
    for chunk in range(CHUNKS):
        at = pl.ds(chunk * size, size)
        left = jnp.zeros((mats * RANK, size), F32)
        for copy in copies[2 * mats * chunk : 2 * mats * (chunk + 1)]:
            copy.wait()
        for mat in range(mats):
            value = gbuf[mat, at].astype(F32) + ebuf[mat, at]
            high = value.astype(BF16)
            low = (value - high.astype(F32)).astype(BF16)
            product = lax.dot_general(weights, high, dims, preferred_element_type=F32)
            product = product + lax.dot_general(weights, low, dims, preferred_element_type=F32)
            left = fold(mat, left, product)
        left_ref[:, at] = left


def project(seeds, grads, errors):
    _, mats, rows, cols = grads.shape
    return pl.pallas_call(
        project_body,
        out_shape=(
            jax.ShapeDtypeStruct((mats * RANK, rows), F32),
            pltpu.VMEM((mats, rows, cols), BF16),
            pltpu.VMEM((mats, rows, cols), F32),
        ),
        in_specs=[pl.BlockSpec(memory_space=pltpu.HBM)] * 3,
        out_specs=[pl.BlockSpec(memory_space=pltpu.VMEM)] * 3,
        scratch_shapes=[
            pltpu.SMEM(seeds.shape, seeds.dtype),
            pltpu.SemaphoreType.DMA,
            pltpu.SemaphoreType.DMA((2, mats * CHUNKS)),
        ],
        compiler_params=pltpu.CompilerParams(vmem_limit_bytes=16 * 2**20),
        name="project",
    )(*[pltpu.with_memory_space_constraint(value, pltpu.HBM) for value in (seeds, grads, errors)])


def merge_body(grads_ref, errors_ref, merged_ref, high_ref, low_ref, zero_ref):
    mats, rows, cols = grads_ref.shape
    size = 64
    zero_ref[...] = jnp.zeros_like(zero_ref)

    @pl.loop(0, rows // size)
    def _(step):
        at = pl.ds(pl.multiple_of(step * size, size), size)
        for mat in range(mats):
            value = grads_ref[mat, at].astype(F32) + errors_ref[mat, at]
            high = value.astype(BF16)
            merged_ref[mat, at] = value
            high_ref[mat, at] = high
            low_ref[mat, at] = (value - high.astype(F32)).astype(BF16)


def merge(grads, errors):
    shape = grads.shape
    return pl.pallas_call(
        merge_body,
        out_shape=(
            pltpu.VMEM(shape, F32),
            pltpu.VMEM(shape, BF16),
            pltpu.VMEM(shape, BF16),
            jax.ShapeDtypeStruct((shape[0] * RANK, shape[1]), F32),
        ),
        in_specs=[pl.BlockSpec(memory_space=pltpu.VMEM)] * 2,
        out_specs=[pl.BlockSpec(memory_space=pltpu.VMEM)] * 4,
        compiler_params=pltpu.CompilerParams(vmem_limit_bytes=16 * 2**20),
        cost_estimate=pl.CostEstimate(flops=3 * grads.size, bytes_accessed=14 * grads.size, transcendentals=0),
        name="merge",
    )(*[pltpu.with_memory_space_constraint(value, pltpu.VMEM) for value in (grads, errors)])


def pick(rows, index, count):
    return jnp.concatenate(
        [
            jnp.broadcast_to(rows[start + index : start + index + 1], (RANK, rows.shape[1]))
            for start in range(0, count, RANK)
        ],
        axis=0,
    )


def orthogonal(mine, other):
    count = mine.shape[0]
    rank = lax.broadcasted_iota(jnp.int32, (count, 1), 0) % RANK
    for index in range(RANK):
        current = pick(mine, index, count)
        partner = pick(other, index, count)
        products = jnp.sum(mine * current + other * partner, axis=1, keepdims=True)
        inverse = 1.0 / (jnp.sqrt(pick(products, index, count)) + EPSILON)
        inner = products * inverse
        weight = jnp.where(rank > index, inner * inverse, 0.0)
        here = rank == index
        mine = jnp.where(here, mine * inverse, mine - weight * current)
        if index < RANK - 1:
            other = jnp.where(here, other * inverse, other - weight * partner)
    return mine


def reflect_body(scale, mine_ref, other_ref, high_ref, low_ref, left_ref, right_ref):
    mats, rows, cols = high_ref.shape
    left = orthogonal(mine_ref[...] * scale, other_ref[...] * scale)
    left_ref[...] = left
    weights = jnp.concatenate(halves(left), axis=0).astype(BF16)
    right = jnp.zeros((mats * RANK, cols), F32)
    for mat in range(mats):
        product = jnp.dot(weights, high_ref[mat], preferred_element_type=F32)
        product = product + jnp.dot(weights, low_ref[mat], preferred_element_type=F32)
        right = fold(mat, right, product)
    right_ref[...] = right


def reflect(mine, other, high, low, scale):
    mats, rows, cols = high.shape
    return pl.pallas_call(
        functools.partial(reflect_body, scale),
        out_shape=(
            jax.ShapeDtypeStruct((mats * RANK, rows), F32),
            jax.ShapeDtypeStruct((mats * RANK, cols), F32),
        ),
        in_specs=[pl.BlockSpec(memory_space=pltpu.VMEM)] * 4,
        out_specs=[pl.BlockSpec(memory_space=pltpu.VMEM)] * 2,
        compiler_params=pltpu.CompilerParams(vmem_limit_bytes=24 * 2**20),
        name="reflect",
    )(mine, other, pltpu.with_memory_space_constraint(high, pltpu.VMEM), pltpu.with_memory_space_constraint(low, pltpu.VMEM))


def turn_body(left_ref, turned_ref):
    high, low = halves(left_ref[...])
    turned_ref[...] = jnp.concatenate([high, low, high, low], axis=0).T.astype(BF16)


def turn(left):
    count, rows = left.shape
    return pl.pallas_call(
        turn_body,
        out_shape=pltpu.VMEM((rows, 4 * count), BF16),
        in_specs=[pl.BlockSpec(memory_space=pltpu.VMEM)],
        out_specs=pl.BlockSpec(memory_space=pltpu.VMEM),
        compiler_params=pltpu.CompilerParams(vmem_limit_bytes=16 * 2**20),
        cost_estimate=pl.CostEstimate(flops=16 * left.size, bytes_accessed=64 * left.size, transcendentals=0),
        name="turn",
    )(left)


def finish_body(scale, left_ref, right_ref, merged_ref, update_ref, errors_ref, ubuf, ebuf, sems):
    mats, rows, cols = merged_ref.shape
    size = rows // CHUNKS
    high, low = halves(right_ref[...] * scale)
    right = jnp.concatenate([high, high, low, low], axis=0)
    row = lax.broadcasted_iota(jnp.int32, right.shape, 0) % (mats * RANK)
    copies = []
    for mat in range(mats):
        weights = jnp.where(row // RANK == mat, right, 0.0).astype(BF16)
        for chunk in range(CHUNKS):
            at = pl.ds(chunk * size, size)
            slot = mat * CHUNKS + chunk
            approx = jnp.dot(left_ref[at], weights, preferred_element_type=F32)
            ubuf[mat, at] = approx.astype(BF16)
            ebuf[mat, at] = merged_ref[mat, at] - approx
            for copy in (
                pltpu.make_async_copy(ubuf.at[mat, at], update_ref.at[mat, at], sems.at[0, slot]),
                pltpu.make_async_copy(ebuf.at[mat, at], errors_ref.at[0, mat, at], sems.at[1, slot]),
            ):
                copy.start()
                copies.append(copy)
    for copy in copies:
        copy.wait()


def finish(left, right, merged, scale):
    mats, rows, cols = merged.shape
    return pl.pallas_call(
        functools.partial(finish_body, scale),
        out_shape=(
            jax.ShapeDtypeStruct((mats, rows, cols), BF16),
            jax.ShapeDtypeStruct((1, mats, rows, cols), F32),
        ),
        in_specs=[pl.BlockSpec(memory_space=pltpu.VMEM)] * 3,
        out_specs=[pl.BlockSpec(memory_space=pltpu.HBM)] * 2,
        scratch_shapes=[
            pltpu.VMEM((mats, rows, cols), BF16),
            pltpu.VMEM((mats, rows, cols), F32),
            pltpu.SemaphoreType.DMA((2, mats * CHUNKS)),
        ],
        compiler_params=pltpu.CompilerParams(vmem_limit_bytes=16 * 2**20),
        name="finish",
    )(
        pltpu.with_memory_space_constraint(left, pltpu.VMEM),
        right,
        pltpu.with_memory_space_constraint(merged, pltpu.VMEM),
    )


def swap(value, axes, pairs):
    return lax.ppermute(value, axes, pairs + [(target, source) for source, target in pairs])


def swap_cores(value):
    return swap(value, "tensor", [(0, 1)])


def swap_chips(value, step, cross):
    lower = [at for at in range(lax.axis_size("dp")) if at < at ^ step]
    pairs = [(2 * at + core, 2 * (at ^ step) + (core ^ cross)) for at in lower for core in range(2)]
    return swap(value, ("dp", "tensor"), pairs)


def chips_sum(value, cross, zero=0.0):
    count = lax.axis_size("dp")
    last = max(count // 4, 1)
    step = 1
    while step < last:
        value = value + (zero + swap_chips(value, step, cross))
        zero = 0.0
        step *= 2
    terms = [swap_chips(value, offset, cross) for offset in range(count - last, 0, -last)]
    terms = [value] + terms[::-1]
    while len(terms) > 1:
        terms = [terms[at] + terms[at + 1] for at in range(0, len(terms), 2)]
    return terms[0]


def body(grads, errors, seeds):
    replicas = lax.axis_size("dp")
    left_part, grads, errors = project(seeds, grads, errors)
    merged, high, low, zero = merge(grads, errors)
    mine = chips_sum(left_part, 0, zero)
    left, right_part = reflect(mine, swap_cores(mine), high, low, 1.0 / replicas)
    right = chips_sum(right_part + swap_cores(right_part), 1)
    return finish(turn(left), right, merged, 1.0 / replicas)


def solution(mesh):
    in_specs = (
        P(("groups", "dp"), None, "tensor", None),
        P(("groups", "dp"), None, "tensor", None),
        P(),
    )
    out_specs = (P("groups", "tensor", None), P(("groups", "dp"), None, "tensor", None))
    return jax.shard_map(body, mesh=mesh, in_specs=in_specs, out_specs=out_specs, check_vma=False)
```

```python
import functools

import jax
import jax.numpy as jnp
from jax import lax
from jax.experimental import pallas as pl
from jax.experimental.pallas import tpu as pltpu
from jax.sharding import PartitionSpec as P

RANK = 4
EPSILON = 1e-08
CHUNKS = 4
SPLIT = ((1, 7), (5, 4), (2, 6))
SHARED = 3
BF16 = jnp.bfloat16
F32 = jnp.float32


def halves(value):
    high = value.astype(BF16).astype(F32)
    return high, value - high


def start_rows(seeds_ref, mats, cols):
    shape = (mats * RANK, cols)
    row = lax.broadcasted_iota(jnp.int32, shape, 0)
    col = lax.broadcasted_iota(jnp.int32, shape, 1)
    mat = row // RANK
    seed = jnp.full(shape, seeds_ref[0], jnp.int32)
    for index in range(1, mats):
        seed = jnp.where(mat == index, seeds_ref[index], seed)
    mixed = ((row - mat * RANK) * cols + col) * 747796405 + seed * 277803737 + 12345
    mixed = mixed ^ (mixed >> 15)
    mixed = mixed * 1274126177
    mixed = mixed ^ (mixed >> 13)
    lowbits = jnp.bitwise_and(mixed, 65535)
    return (lowbits.astype(F32) - 32767.5) / 32768.0


def fold(mat, value, product):
    part = product[: value.shape[0]] + product[value.shape[0] :]
    row = lax.broadcasted_iota(jnp.int32, value.shape, 0)
    return jnp.where(row // RANK == mat, part, value)


def project_body(seeds_ref, grads_ref, errors_ref, left_ref, gbuf, ebuf, seed, seed_sem, sems):
    _, mats, rows, cols = grads_ref.shape
    size = rows // CHUNKS
    seed_copy = pltpu.make_async_copy(seeds_ref, seed, seed_sem)
    seed_copy.start()
    copies = []
    for chunk in range(CHUNKS):
        at = pl.ds(chunk * size, size)
        for mat in range(mats):
            slot = chunk * mats + mat
            copies.append(pltpu.make_async_copy(grads_ref.at[0, mat, at], gbuf.at[mat, at], sems.at[0, slot]))
            copies.append(pltpu.make_async_copy(errors_ref.at[0, mat, at], ebuf.at[mat, at], sems.at[1, slot]))
    for copy in copies:
        copy.start()
    seed_copy.wait()
    start = start_rows(seed, mats, cols)
    weights = jnp.concatenate(halves(start), axis=0).astype(BF16)
    dims = (((1,), (1,)), ((), ()))
    for chunk in range(CHUNKS):
        at = pl.ds(chunk * size, size)
        left = jnp.zeros((mats * RANK, size), F32)
        for copy in copies[2 * mats * chunk : 2 * mats * (chunk + 1)]:
            copy.wait()
        for mat in range(mats):
            value = gbuf[mat, at].astype(F32) + ebuf[mat, at]
            high = value.astype(BF16)
            low = (value - high.astype(F32)).astype(BF16)
            product = lax.dot_general(weights, high, dims, preferred_element_type=F32)
            product = product + lax.dot_general(weights, low, dims, preferred_element_type=F32)
            left = fold(mat, left, product)
        left_ref[:, at] = left


def project(seeds, grads, errors):
    _, mats, rows, cols = grads.shape
    return pl.pallas_call(
        project_body,
        out_shape=(
            jax.ShapeDtypeStruct((mats * RANK, rows), F32),
            pltpu.VMEM((mats, rows, cols), BF16),
            pltpu.VMEM((mats, rows, cols), F32),
        ),
        in_specs=[pl.BlockSpec(memory_space=pltpu.HBM)] * 3,
        out_specs=[pl.BlockSpec(memory_space=pltpu.VMEM)] * 3,
        scratch_shapes=[
            pltpu.SMEM(seeds.shape, seeds.dtype),
            pltpu.SemaphoreType.DMA,
            pltpu.SemaphoreType.DMA((2, mats * CHUNKS)),
        ],
        compiler_params=pltpu.CompilerParams(vmem_limit_bytes=16 * 2**20),
        name="project",
    )(*[pltpu.with_memory_space_constraint(value, pltpu.HBM) for value in (seeds, grads, errors)])


def merge_body(grads_ref, errors_ref, merged_ref, high_ref, low_ref, zero_ref):
    mats, rows, cols = grads_ref.shape
    size = 64
    zero_ref[...] = jnp.zeros_like(zero_ref)

    @pl.loop(0, rows // size)
    def _(step):
        at = pl.ds(pl.multiple_of(step * size, size), size)
        for mat in range(mats):
            value = grads_ref[mat, at].astype(F32) + errors_ref[mat, at]
            high = value.astype(BF16)
            merged_ref[mat, at] = value
            high_ref[mat, at] = high
            low_ref[mat, at] = (value - high.astype(F32)).astype(BF16)


def merge(grads, errors):
    shape = grads.shape
    return pl.pallas_call(
        merge_body,
        out_shape=(
            pltpu.VMEM(shape, F32),
            pltpu.VMEM(shape, BF16),
            pltpu.VMEM(shape, BF16),
            jax.ShapeDtypeStruct((shape[0] * RANK, shape[1]), F32),
        ),
        in_specs=[pl.BlockSpec(memory_space=pltpu.VMEM)] * 2,
        out_specs=[pl.BlockSpec(memory_space=pltpu.VMEM)] * 4,
        compiler_params=pltpu.CompilerParams(vmem_limit_bytes=16 * 2**20),
        cost_estimate=pl.CostEstimate(flops=3 * grads.size, bytes_accessed=14 * grads.size, transcendentals=0),
        name="merge",
    )(*[pltpu.with_memory_space_constraint(value, pltpu.VMEM) for value in (grads, errors)])


def pick(rows, index, count):
    return jnp.concatenate(
        [
            jnp.broadcast_to(rows[start + index : start + index + 1], (RANK, rows.shape[1]))
            for start in range(0, count, RANK)
        ],
        axis=0,
    )


def orthogonal(mine, other):
    count = mine.shape[0]
    rank = lax.broadcasted_iota(jnp.int32, (count, 1), 0) % RANK
    for index in range(RANK):
        current = pick(mine, index, count)
        partner = pick(other, index, count)
        products = jnp.sum(mine * current + other * partner, axis=1, keepdims=True)
        inverse = 1.0 / (jnp.sqrt(pick(products, index, count)) + EPSILON)
        inner = products * inverse
        weight = jnp.where(rank > index, inner * inverse, 0.0)
        here = rank == index
        mine = jnp.where(here, mine * inverse, mine - weight * current)
        if index < RANK - 1:
            other = jnp.where(here, other * inverse, other - weight * partner)
    return mine


def reflect_body(scale, mine_ref, other_ref, high_ref, low_ref, left_ref, right_ref):
    mats, rows, cols = high_ref.shape
    left = orthogonal(mine_ref[...] * scale, other_ref[...] * scale)
    left_ref[...] = left
    weights = jnp.concatenate(halves(left), axis=0).astype(BF16)
    right = jnp.zeros((mats * RANK, cols), F32)
    for mat in range(mats):
        product = jnp.dot(weights, high_ref[mat], preferred_element_type=F32)
        product = product + jnp.dot(weights, low_ref[mat], preferred_element_type=F32)
        right = fold(mat, right, product)
    right_ref[...] = right


def reflect(mine, other, high, low, scale):
    mats, rows, cols = high.shape
    return pl.pallas_call(
        functools.partial(reflect_body, scale),
        out_shape=(
            jax.ShapeDtypeStruct((mats * RANK, rows), F32),
            jax.ShapeDtypeStruct((mats * RANK, cols), F32),
        ),
        in_specs=[pl.BlockSpec(memory_space=pltpu.VMEM)] * 4,
        out_specs=[pl.BlockSpec(memory_space=pltpu.VMEM)] * 2,
        compiler_params=pltpu.CompilerParams(vmem_limit_bytes=24 * 2**20),
        name="reflect",
    )(mine, other, pltpu.with_memory_space_constraint(high, pltpu.VMEM), pltpu.with_memory_space_constraint(low, pltpu.VMEM))


def turn_body(left_ref, turned_ref):
    high, low = halves(left_ref[...])
    turned_ref[...] = jnp.concatenate([high, low, high, low], axis=0).T.astype(BF16)


def turn(left):
    count, rows = left.shape
    return pl.pallas_call(
        turn_body,
        out_shape=pltpu.VMEM((rows, 4 * count), BF16),
        in_specs=[pl.BlockSpec(memory_space=pltpu.VMEM)],
        out_specs=pl.BlockSpec(memory_space=pltpu.VMEM),
        compiler_params=pltpu.CompilerParams(vmem_limit_bytes=16 * 2**20),
        cost_estimate=pl.CostEstimate(flops=16 * left.size, bytes_accessed=64 * left.size, transcendentals=0),
        name="turn",
    )(left)


def total(own_ref, both_ref, taken_refs, given_refs):
    first = lax.axis_index("tensor") == 0
    terms = {0: own_ref[...], SHARED: both_ref[...]}
    for masks, taken_ref, given_ref in zip(SPLIT, taken_refs, given_refs):
        taken, given = taken_ref[...], given_ref[...]
        terms[masks[0]] = jnp.where(first, taken, given)
        terms[masks[1]] = jnp.where(first, given, taken)
    sums = [terms[index] for index in range(len(terms))]
    while len(sums) > 1:
        sums = [sums[at] + sums[at + 1] for at in range(0, len(sums), 2)]
    return sums[0]


def finish_body(scale, count, left_ref, merged_ref, own_ref, both_ref, *refs):
    taken_refs, given_refs = refs[:count], refs[count : 2 * count]
    update_ref, errors_ref, ubuf, ebuf, sems = refs[2 * count :]
    right = total(own_ref, both_ref, taken_refs, given_refs) * scale
    finish_rows(right, left_ref, merged_ref, update_ref, errors_ref, ubuf, ebuf, sems)


def finish_rows(right, left_ref, merged_ref, update_ref, errors_ref, ubuf, ebuf, sems):
    mats, rows, cols = merged_ref.shape
    size = rows // CHUNKS
    high, low = halves(right)
    right = jnp.concatenate([high, high, low, low], axis=0)
    row = lax.broadcasted_iota(jnp.int32, right.shape, 0) % (mats * RANK)
    copies = []
    for mat in range(mats):
        weights = jnp.where(row // RANK == mat, right, 0.0).astype(BF16)
        for chunk in range(CHUNKS):
            at = pl.ds(chunk * size, size)
            slot = mat * CHUNKS + chunk
            approx = jnp.dot(left_ref[at], weights, preferred_element_type=F32)
            ubuf[mat, at] = approx.astype(BF16)
            ebuf[mat, at] = merged_ref[mat, at] - approx
            for copy in (
                pltpu.make_async_copy(ubuf.at[mat, at], update_ref.at[mat, at], sems.at[0, slot]),
                pltpu.make_async_copy(ebuf.at[mat, at], errors_ref.at[0, mat, at], sems.at[1, slot]),
            ):
                copy.start()
                copies.append(copy)
    for copy in copies:
        copy.wait()


def finish(left, merged, own, both, taken, given, scale):
    mats, rows, cols = merged.shape
    return pl.pallas_call(
        functools.partial(finish_body, scale, len(taken)),
        out_shape=(
            jax.ShapeDtypeStruct((mats, rows, cols), BF16),
            jax.ShapeDtypeStruct((1, mats, rows, cols), F32),
        ),
        in_specs=[pl.BlockSpec(memory_space=pltpu.VMEM)] * (4 + 2 * len(taken)),
        out_specs=[pl.BlockSpec(memory_space=pltpu.HBM)] * 2,
        scratch_shapes=[
            pltpu.VMEM((mats, rows, cols), BF16),
            pltpu.VMEM((mats, rows, cols), F32),
            pltpu.SemaphoreType.DMA((2, mats * CHUNKS)),
        ],
        compiler_params=pltpu.CompilerParams(vmem_limit_bytes=16 * 2**20),
        name="finish",
    )(
        pltpu.with_memory_space_constraint(left, pltpu.VMEM),
        pltpu.with_memory_space_constraint(merged, pltpu.VMEM),
        own,
        both,
        *taken,
        *given,
    )


def swap(value, axes, pairs):
    return lax.ppermute(value, axes, pairs + [(target, source) for source, target in pairs])


def swap_cores(value):
    return swap(value, "tensor", [(0, 1)])


def swap_chips(value, masks, cross=0):
    pairs = []
    for core in range(2):
        for at in range(lax.axis_size("dp")):
            partner = at ^ masks[core]
            if at < partner:
                pairs.append((2 * at + core, 2 * partner + (core ^ cross)))
    return swap(value, ("dp", "tensor"), pairs)


def chips_sum(value, zero):
    count = lax.axis_size("dp")
    last = max(count // 4, 1)
    step = 1
    while step < last:
        value = value + (zero + swap_chips(value, (step, step)))
        zero = 0.0
        step *= 2
    terms = [value] + [swap_chips(value, (offset, offset)) for offset in range(last, count, last)]
    while len(terms) > 1:
        terms = [terms[at] + terms[at + 1] for at in range(0, len(terms), 2)]
    return terms[0]


def chips_terms(value):
    count = lax.axis_size("dp")
    last = count // 8
    step = 1
    while step < last:
        value = value + swap_chips(value, (step, step), 1)
        step *= 2
    both = swap_chips(value, (SHARED * last, SHARED * last), 1)
    taken = [swap_chips(value, (lower * last, upper * last)) for lower, upper in SPLIT[::-1]][::-1]
    return value, both, taken, [swap_cores(term) for term in taken]


def body(grads, errors, seeds):
    replicas = lax.axis_size("dp")
    left_part, grads, errors = project(seeds, grads, errors)
    merged, high, low, zero = merge(grads, errors)
    mine = chips_sum(left_part, zero)
    left, right_part = reflect(mine, swap_cores(mine), high, low, 1.0 / replicas)
    terms = chips_terms(right_part + swap_cores(right_part))
    return finish(turn(left), merged, *terms, 1.0 / replicas)


def solution(mesh):
    in_specs = (
        P(("groups", "dp"), None, "tensor", None),
        P(("groups", "dp"), None, "tensor", None),
        P(),
    )
    out_specs = (P("groups", "tensor", None), P(("groups", "dp"), None, "tensor", None))
    return jax.shard_map(body, mesh=mesh, in_specs=in_specs, out_specs=out_specs, check_vma=False)
```

```python
import functools

import jax
import jax.numpy as jnp
from jax import lax
from jax.experimental import pallas as pl
from jax.experimental.pallas import tpu as pltpu
from jax.sharding import PartitionSpec as P

RANK = 4
EPSILON = 1e-08
CHUNKS = 4
SPLIT = ((1, 7), (5, 4), (2, 6))
SHARED = 3
BF16 = jnp.bfloat16
F32 = jnp.float32


def halves(value):
    high = value.astype(BF16).astype(F32)
    return high, value - high


def start_rows(seeds_ref, mats, cols):
    shape = (mats * RANK, cols)
    row = lax.broadcasted_iota(jnp.int32, shape, 0)
    col = lax.broadcasted_iota(jnp.int32, shape, 1)
    mat = row // RANK
    seed = jnp.full(shape, seeds_ref[0], jnp.int32)
    for index in range(1, mats):
        seed = jnp.where(mat == index, seeds_ref[index], seed)
    mixed = ((row - mat * RANK) * cols + col) * 747796405 + seed * 277803737 + 12345
    mixed = mixed ^ (mixed >> 15)
    mixed = mixed * 1274126177
    mixed = mixed ^ (mixed >> 13)
    lowbits = jnp.bitwise_and(mixed, 65535)
    return (lowbits.astype(F32) - 32767.5) / 32768.0


def fold(mat, value, product):
    part = product[: value.shape[0]] + product[value.shape[0] :]
    row = lax.broadcasted_iota(jnp.int32, value.shape, 0)
    return jnp.where(row // RANK == mat, part, value)


def project_body(seeds_ref, grads_ref, errors_ref, left_ref, gbuf, ebuf, seed, seed_sem, sems):
    _, mats, rows, cols = grads_ref.shape
    size = rows // CHUNKS
    seed_copy = pltpu.make_async_copy(seeds_ref, seed, seed_sem)
    seed_copy.start()
    copies = []
    for chunk in range(CHUNKS):
        at = pl.ds(chunk * size, size)
        for mat in range(mats):
            slot = chunk * mats + mat
            copies.append(pltpu.make_async_copy(grads_ref.at[0, mat, at], gbuf.at[mat, at], sems.at[0, slot]))
            copies.append(pltpu.make_async_copy(errors_ref.at[0, mat, at], ebuf.at[mat, at], sems.at[1, slot]))
    for copy in copies:
        copy.start()
    seed_copy.wait()
    start = start_rows(seed, mats, cols)
    weights = jnp.concatenate(halves(start), axis=0).astype(BF16)
    dims = (((1,), (1,)), ((), ()))
    for chunk in range(CHUNKS):
        at = pl.ds(chunk * size, size)
        left = jnp.zeros((mats * RANK, size), F32)
        for copy in copies[2 * mats * chunk : 2 * mats * (chunk + 1)]:
            copy.wait()
        for mat in range(mats):
            value = gbuf[mat, at].astype(F32) + ebuf[mat, at]
            high = value.astype(BF16)
            low = (value - high.astype(F32)).astype(BF16)
            product = lax.dot_general(weights, high, dims, preferred_element_type=F32)
            product = product + lax.dot_general(weights, low, dims, preferred_element_type=F32)
            left = fold(mat, left, product)
        left_ref[:, at] = left


def project(seeds, grads, errors):
    _, mats, rows, cols = grads.shape
    return pl.pallas_call(
        project_body,
        out_shape=(
            jax.ShapeDtypeStruct((mats * RANK, rows), F32),
            pltpu.VMEM((mats, rows, cols), BF16),
            pltpu.VMEM((mats, rows, cols), F32),
        ),
        in_specs=[pl.BlockSpec(memory_space=pltpu.HBM)] * 3,
        out_specs=[pl.BlockSpec(memory_space=pltpu.VMEM)] * 3,
        scratch_shapes=[
            pltpu.SMEM(seeds.shape, seeds.dtype),
            pltpu.SemaphoreType.DMA,
            pltpu.SemaphoreType.DMA((2, mats * CHUNKS)),
        ],
        compiler_params=pltpu.CompilerParams(vmem_limit_bytes=16 * 2**20),
        name="project",
    )(*[pltpu.with_memory_space_constraint(value, pltpu.HBM) for value in (seeds, grads, errors)])


def merge_body(grads_ref, errors_ref, merged_ref, high_ref, low_ref, zero_ref):
    mats, rows, cols = grads_ref.shape
    size = 64
    zero_ref[...] = jnp.zeros_like(zero_ref)

    @pl.loop(0, rows // size)
    def _(step):
        at = pl.ds(pl.multiple_of(step * size, size), size)
        for mat in range(mats):
            value = grads_ref[mat, at].astype(F32) + errors_ref[mat, at]
            high = value.astype(BF16)
            merged_ref[mat, at] = value
            high_ref[mat, at] = high
            low_ref[mat, at] = (value - high.astype(F32)).astype(BF16)


def merge(grads, errors):
    shape = grads.shape
    return pl.pallas_call(
        merge_body,
        out_shape=(
            pltpu.VMEM(shape, F32),
            pltpu.VMEM(shape, BF16),
            pltpu.VMEM(shape, BF16),
            jax.ShapeDtypeStruct((shape[0] * RANK, shape[1]), F32),
        ),
        in_specs=[pl.BlockSpec(memory_space=pltpu.VMEM)] * 2,
        out_specs=[pl.BlockSpec(memory_space=pltpu.VMEM)] * 4,
        compiler_params=pltpu.CompilerParams(vmem_limit_bytes=16 * 2**20),
        cost_estimate=pl.CostEstimate(flops=3 * grads.size, bytes_accessed=14 * grads.size, transcendentals=0),
        name="merge",
    )(*[pltpu.with_memory_space_constraint(value, pltpu.VMEM) for value in (grads, errors)])


def pick(rows, index, count):
    return jnp.concatenate(
        [
            jnp.broadcast_to(rows[start + index : start + index + 1], (RANK, rows.shape[1]))
            for start in range(0, count, RANK)
        ],
        axis=0,
    )


def orthogonal(mine, other):
    count = mine.shape[0]
    rank = lax.broadcasted_iota(jnp.int32, (count, 1), 0) % RANK
    for index in range(RANK):
        current = pick(mine, index, count)
        partner = pick(other, index, count)
        products = jnp.sum(mine * current + other * partner, axis=1, keepdims=True)
        inverse = 1.0 / (jnp.sqrt(pick(products, index, count)) + EPSILON)
        inner = products * inverse
        weight = jnp.where(rank > index, inner * inverse, 0.0)
        here = rank == index
        mine = jnp.where(here, mine * inverse, mine - weight * current)
        if index < RANK - 1:
            other = jnp.where(here, other * inverse, other - weight * partner)
    return mine


def reflect_body(scale, count, high_ref, low_ref, own_ref, both_ref, *refs):
    mats, rows, cols = high_ref.shape
    left_ref, right_ref = refs[2 * count :]
    mine, other = [
        total(
            own_ref[at],
            both_ref[1 - at],
            [ref[at] for ref in refs[:count]],
            [ref[1 - at] for ref in refs[count : 2 * count]],
        )
        * scale
        for at in range(2)
    ]
    left = orthogonal(mine, other)
    left_ref[...] = left
    weights = jnp.concatenate(halves(left), axis=0).astype(BF16)
    right = jnp.zeros((mats * RANK, cols), F32)
    for mat in range(mats):
        product = jnp.dot(weights, high_ref[mat], preferred_element_type=F32)
        product = product + jnp.dot(weights, low_ref[mat], preferred_element_type=F32)
        right = fold(mat, right, product)
    right_ref[...] = right


def reflect(high, low, own, both, taken, given, scale):
    mats, rows, cols = high.shape
    return pl.pallas_call(
        functools.partial(reflect_body, scale, len(taken)),
        out_shape=(
            jax.ShapeDtypeStruct((mats * RANK, rows), F32),
            jax.ShapeDtypeStruct((mats * RANK, cols), F32),
        ),
        in_specs=[pl.BlockSpec(memory_space=pltpu.VMEM)] * (4 + 2 * len(taken)),
        out_specs=[pl.BlockSpec(memory_space=pltpu.VMEM)] * 2,
        compiler_params=pltpu.CompilerParams(vmem_limit_bytes=16 * 2**20),
        name="reflect",
    )(
        pltpu.with_memory_space_constraint(high, pltpu.VMEM),
        pltpu.with_memory_space_constraint(low, pltpu.VMEM),
        own,
        both,
        *taken,
        *given,
    )


def turn_body(left_ref, turned_ref):
    high, low = halves(left_ref[...])
    turned_ref[...] = jnp.concatenate([high, low, high, low], axis=0).T.astype(BF16)


def turn(left):
    count, rows = left.shape
    return pl.pallas_call(
        turn_body,
        out_shape=pltpu.VMEM((rows, 4 * count), BF16),
        in_specs=[pl.BlockSpec(memory_space=pltpu.VMEM)],
        out_specs=pl.BlockSpec(memory_space=pltpu.VMEM),
        compiler_params=pltpu.CompilerParams(vmem_limit_bytes=16 * 2**20),
        cost_estimate=pl.CostEstimate(flops=16 * left.size, bytes_accessed=64 * left.size, transcendentals=0),
        name="turn",
    )(left)


def total(own, both, taken, given):
    first = lax.axis_index("tensor") == 0
    terms = {0: own, SHARED: both}
    for masks, near, far in zip(SPLIT, taken, given):
        terms[masks[0]] = jnp.where(first, near, far)
        terms[masks[1]] = jnp.where(first, far, near)
    sums = [terms[index] for index in range(len(terms))]
    while len(sums) > 1:
        sums = [sums[at] + sums[at + 1] for at in range(0, len(sums), 2)]
    return sums[0]


def finish_body(scale, count, left_ref, merged_ref, own_ref, both_ref, *refs):
    taken, given = [ref[...] for ref in refs[:count]], [ref[...] for ref in refs[count : 2 * count]]
    update_ref, errors_ref, ubuf, ebuf, sems = refs[2 * count :]
    right = total(own_ref[...], both_ref[...], taken, given) * scale
    finish_rows(right, left_ref, merged_ref, update_ref, errors_ref, ubuf, ebuf, sems)


def finish_rows(right, left_ref, merged_ref, update_ref, errors_ref, ubuf, ebuf, sems):
    mats, rows, cols = merged_ref.shape
    size = rows // CHUNKS
    high, low = halves(right)
    right = jnp.concatenate([high, high, low, low], axis=0)
    row = lax.broadcasted_iota(jnp.int32, right.shape, 0) % (mats * RANK)
    copies = []
    for mat in range(mats):
        weights = jnp.where(row // RANK == mat, right, 0.0).astype(BF16)
        for chunk in range(CHUNKS):
            at = pl.ds(chunk * size, size)
            slot = mat * CHUNKS + chunk
            approx = jnp.dot(left_ref[at], weights, preferred_element_type=F32)
            ubuf[mat, at] = approx.astype(BF16)
            ebuf[mat, at] = merged_ref[mat, at] - approx
            for copy in (
                pltpu.make_async_copy(ubuf.at[mat, at], update_ref.at[mat, at], sems.at[0, slot]),
                pltpu.make_async_copy(ebuf.at[mat, at], errors_ref.at[0, mat, at], sems.at[1, slot]),
            ):
                copy.start()
                copies.append(copy)
    for copy in copies:
        copy.wait()


def finish(left, merged, own, both, taken, given, scale):
    mats, rows, cols = merged.shape
    return pl.pallas_call(
        functools.partial(finish_body, scale, len(taken)),
        out_shape=(
            jax.ShapeDtypeStruct((mats, rows, cols), BF16),
            jax.ShapeDtypeStruct((1, mats, rows, cols), F32),
        ),
        in_specs=[pl.BlockSpec(memory_space=pltpu.VMEM)] * (4 + 2 * len(taken)),
        out_specs=[pl.BlockSpec(memory_space=pltpu.HBM)] * 2,
        scratch_shapes=[
            pltpu.VMEM((mats, rows, cols), BF16),
            pltpu.VMEM((mats, rows, cols), F32),
            pltpu.SemaphoreType.DMA((2, mats * CHUNKS)),
        ],
        compiler_params=pltpu.CompilerParams(vmem_limit_bytes=16 * 2**20),
        name="finish",
    )(
        pltpu.with_memory_space_constraint(left, pltpu.VMEM),
        pltpu.with_memory_space_constraint(merged, pltpu.VMEM),
        own,
        both,
        *taken,
        *given,
    )


def swap(value, axes, pairs):
    return lax.ppermute(value, axes, pairs + [(target, source) for source, target in pairs])


def swap_cores(value):
    return swap(value, "tensor", [(0, 1)])


def swap_chips(value, masks, cross=0):
    pairs = []
    for core in range(2):
        for at in range(lax.axis_size("dp")):
            partner = at ^ masks[core]
            if at < partner:
                pairs.append((2 * at + core, 2 * partner + (core ^ cross)))
    return swap(value, ("dp", "tensor"), pairs)


def chips_terms(value, turned):
    count = lax.axis_size("dp")
    last = count // 8
    step = 1
    while step < last:
        value = value + turned(swap_chips(value, (step, step), 1))
        step *= 2
    both = swap_chips(value, (SHARED * last, SHARED * last), 1)
    taken = [swap_chips(value, (lower * last, upper * last)) for lower, upper in SPLIT[::-1]][::-1]
    return value, both, taken, [swap_cores(term) for term in taken]


def body(grads, errors, seeds):
    replicas = lax.axis_size("dp")
    left_part, grads, errors = project(seeds, grads, errors)
    merged, high, low, zero = merge(grads, errors)
    both = jnp.stack([left_part, swap_cores(left_part) + zero], axis=0)
    terms = chips_terms(both, lambda taken: lax.rev(taken, (0,)))
    left, right_part = reflect(high, low, *terms, 1.0 / replicas)
    terms = chips_terms(right_part + swap_cores(right_part), lambda taken: taken)
    return finish(turn(left), merged, *terms, 1.0 / replicas)


def solution(mesh):
    in_specs = (
        P(("groups", "dp"), None, "tensor", None),
        P(("groups", "dp"), None, "tensor", None),
        P(),
    )
    out_specs = (P("groups", "tensor", None), P(("groups", "dp"), None, "tensor", None))
    return jax.shard_map(body, mesh=mesh, in_specs=in_specs, out_specs=out_specs, check_vma=False)
```

```python
import functools

import jax
import jax.numpy as jnp
from jax import lax
from jax.experimental import pallas as pl
from jax.experimental.pallas import tpu as pltpu
from jax.sharding import PartitionSpec as P

RANK = 4
EPSILON = 1e-08
CHUNKS = 4
LEFT_SPLIT = ((6, 4), (1, 7), (2, 5))
RIGHT_SPLIT = ((1, 7), (5, 4), (2, 6))
SHARED = 3
BF16 = jnp.bfloat16
F32 = jnp.float32


def halves(value):
    high = value.astype(BF16).astype(F32)
    return high, value - high


def start_rows(seeds_ref, mats, cols):
    shape = (mats * RANK, cols)
    row = lax.broadcasted_iota(jnp.int32, shape, 0)
    col = lax.broadcasted_iota(jnp.int32, shape, 1)
    mat = row // RANK
    seed = jnp.full(shape, seeds_ref[0], jnp.int32)
    for index in range(1, mats):
        seed = jnp.where(mat == index, seeds_ref[index], seed)
    mixed = ((row - mat * RANK) * cols + col) * 747796405 + seed * 277803737 + 12345
    mixed = mixed ^ (mixed >> 15)
    mixed = mixed * 1274126177
    mixed = mixed ^ (mixed >> 13)
    lowbits = jnp.bitwise_and(mixed, 65535)
    return (lowbits.astype(F32) - 32767.5) / 32768.0


def fold(mat, value, product):
    part = product[: value.shape[0]] + product[value.shape[0] :]
    row = lax.broadcasted_iota(jnp.int32, value.shape, 0)
    return jnp.where(row // RANK == mat, part, value)


def project_body(seeds_ref, grads_ref, errors_ref, left_ref, gbuf, ebuf, seed, seed_sem, sems):
    _, mats, rows, cols = grads_ref.shape
    size = rows // CHUNKS
    seed_copy = pltpu.make_async_copy(seeds_ref, seed, seed_sem)
    seed_copy.start()
    copies = []
    for chunk in range(CHUNKS):
        at = pl.ds(chunk * size, size)
        for mat in range(mats):
            slot = chunk * mats + mat
            copies.append(pltpu.make_async_copy(grads_ref.at[0, mat, at], gbuf.at[mat, at], sems.at[0, slot]))
            copies.append(pltpu.make_async_copy(errors_ref.at[0, mat, at], ebuf.at[mat, at], sems.at[1, slot]))
    for copy in copies:
        copy.start()
    seed_copy.wait()
    start = start_rows(seed, mats, cols)
    weights = jnp.concatenate(halves(start), axis=0).astype(BF16)
    dims = (((1,), (1,)), ((), ()))
    for chunk in range(CHUNKS):
        at = pl.ds(chunk * size, size)
        left = jnp.zeros((mats * RANK, size), F32)
        for copy in copies[2 * mats * chunk : 2 * mats * (chunk + 1)]:
            copy.wait()
        for mat in range(mats):
            value = gbuf[mat, at].astype(F32) + ebuf[mat, at]
            high = value.astype(BF16)
            low = (value - high.astype(F32)).astype(BF16)
            product = lax.dot_general(weights, high, dims, preferred_element_type=F32)
            product = product + lax.dot_general(weights, low, dims, preferred_element_type=F32)
            left = fold(mat, left, product)
        left_ref[:, at] = left


def project(seeds, grads, errors):
    _, mats, rows, cols = grads.shape
    return pl.pallas_call(
        project_body,
        out_shape=(
            jax.ShapeDtypeStruct((mats * RANK, rows), F32),
            pltpu.VMEM((mats, rows, cols), BF16),
            pltpu.VMEM((mats, rows, cols), F32),
        ),
        in_specs=[pl.BlockSpec(memory_space=pltpu.HBM)] * 3,
        out_specs=[pl.BlockSpec(memory_space=pltpu.VMEM)] * 3,
        scratch_shapes=[
            pltpu.SMEM(seeds.shape, seeds.dtype),
            pltpu.SemaphoreType.DMA,
            pltpu.SemaphoreType.DMA((2, mats * CHUNKS)),
        ],
        compiler_params=pltpu.CompilerParams(vmem_limit_bytes=16 * 2**20),
        name="project",
    )(*[pltpu.with_memory_space_constraint(value, pltpu.HBM) for value in (seeds, grads, errors)])


def merge_body(grads_ref, errors_ref, merged_ref, high_ref, low_ref, zero_ref):
    mats, rows, cols = grads_ref.shape
    size = 64
    zero_ref[...] = jnp.zeros_like(zero_ref)

    @pl.loop(0, rows // size)
    def _(step):
        at = pl.ds(pl.multiple_of(step * size, size), size)
        for mat in range(mats):
            value = grads_ref[mat, at].astype(F32) + errors_ref[mat, at]
            high = value.astype(BF16)
            merged_ref[mat, at] = value
            high_ref[mat, at] = high
            low_ref[mat, at] = (value - high.astype(F32)).astype(BF16)


def merge(grads, errors):
    shape = grads.shape
    return pl.pallas_call(
        merge_body,
        out_shape=(
            pltpu.VMEM(shape, F32),
            pltpu.VMEM(shape, BF16),
            pltpu.VMEM(shape, BF16),
            jax.ShapeDtypeStruct((shape[0] * RANK, shape[1]), F32),
        ),
        in_specs=[pl.BlockSpec(memory_space=pltpu.VMEM)] * 2,
        out_specs=[pl.BlockSpec(memory_space=pltpu.VMEM)] * 4,
        compiler_params=pltpu.CompilerParams(vmem_limit_bytes=16 * 2**20),
        cost_estimate=pl.CostEstimate(flops=3 * grads.size, bytes_accessed=14 * grads.size, transcendentals=0),
        name="merge",
    )(*[pltpu.with_memory_space_constraint(value, pltpu.VMEM) for value in (grads, errors)])


def pick(rows, index, count):
    return jnp.concatenate(
        [
            jnp.broadcast_to(rows[start + index : start + index + 1], (RANK, rows.shape[1]))
            for start in range(0, count, RANK)
        ],
        axis=0,
    )


def orthogonal(mine, other):
    count = mine.shape[0]
    rank = lax.broadcasted_iota(jnp.int32, (count, 1), 0) % RANK
    for index in range(RANK):
        current = pick(mine, index, count)
        partner = pick(other, index, count)
        products = jnp.sum(mine * current + other * partner, axis=1, keepdims=True)
        inverse = 1.0 / (jnp.sqrt(pick(products, index, count)) + EPSILON)
        inner = products * inverse
        weight = jnp.where(rank > index, inner * inverse, 0.0)
        here = rank == index
        mine = jnp.where(here, mine * inverse, mine - weight * current)
        if index < RANK - 1:
            other = jnp.where(here, other * inverse, other - weight * partner)
    return mine


def reflect_body(scale, count, high_ref, low_ref, own_ref, both_ref, *refs):
    mats, rows, cols = high_ref.shape
    left_ref, right_ref = refs[2 * count :]
    mine, other = [
        total(
            LEFT_SPLIT,
            own_ref[at],
            both_ref[1 - at],
            [ref[at] for ref in refs[:count]],
            [ref[1 - at] for ref in refs[count : 2 * count]],
        )
        * scale
        for at in range(2)
    ]
    left = orthogonal(mine, other)
    left_ref[...] = left
    weights = jnp.concatenate(halves(left), axis=0).astype(BF16)
    right = jnp.zeros((mats * RANK, cols), F32)
    for mat in range(mats):
        product = jnp.dot(weights, high_ref[mat], preferred_element_type=F32)
        product = product + jnp.dot(weights, low_ref[mat], preferred_element_type=F32)
        right = fold(mat, right, product)
    right_ref[...] = right


def reflect(high, low, own, both, taken, given, scale):
    mats, rows, cols = high.shape
    return pl.pallas_call(
        functools.partial(reflect_body, scale, len(taken)),
        out_shape=(
            jax.ShapeDtypeStruct((mats * RANK, rows), F32),
            jax.ShapeDtypeStruct((mats * RANK, cols), F32),
        ),
        in_specs=[pl.BlockSpec(memory_space=pltpu.VMEM)] * (4 + 2 * len(taken)),
        out_specs=[pl.BlockSpec(memory_space=pltpu.VMEM)] * 2,
        compiler_params=pltpu.CompilerParams(vmem_limit_bytes=16 * 2**20),
        name="reflect",
    )(
        pltpu.with_memory_space_constraint(high, pltpu.VMEM),
        pltpu.with_memory_space_constraint(low, pltpu.VMEM),
        own,
        both,
        *taken,
        *given,
    )


def turn_body(left_ref, turned_ref):
    high, low = halves(left_ref[...])
    turned_ref[...] = jnp.concatenate([high, low, high, low], axis=0).T.astype(BF16)


def turn(left):
    count, rows = left.shape
    return pl.pallas_call(
        turn_body,
        out_shape=pltpu.VMEM((rows, 4 * count), BF16),
        in_specs=[pl.BlockSpec(memory_space=pltpu.VMEM)],
        out_specs=pl.BlockSpec(memory_space=pltpu.VMEM),
        compiler_params=pltpu.CompilerParams(vmem_limit_bytes=16 * 2**20),
        cost_estimate=pl.CostEstimate(flops=16 * left.size, bytes_accessed=64 * left.size, transcendentals=0),
        name="turn",
    )(left)


def total(split, own, both, taken, given):
    first = lax.axis_index("tensor") == 0
    terms = {0: own, SHARED: both}
    for masks, near, far in zip(split, taken, given):
        terms[masks[0]] = jnp.where(first, near, far)
        terms[masks[1]] = jnp.where(first, far, near)
    sums = [terms[index] for index in range(len(terms))]
    while len(sums) > 1:
        sums = [sums[at] + sums[at + 1] for at in range(0, len(sums), 2)]
    return sums[0]


def finish_body(scale, count, left_ref, merged_ref, own_ref, both_ref, *refs):
    taken, given = [ref[...] for ref in refs[:count]], [ref[...] for ref in refs[count : 2 * count]]
    update_ref, errors_ref, ubuf, ebuf, sems = refs[2 * count :]
    right = total(RIGHT_SPLIT, own_ref[...], both_ref[...], taken, given) * scale
    finish_rows(right, left_ref, merged_ref, update_ref, errors_ref, ubuf, ebuf, sems)


def finish_rows(right, left_ref, merged_ref, update_ref, errors_ref, ubuf, ebuf, sems):
    mats, rows, cols = merged_ref.shape
    size = rows // CHUNKS
    high, low = halves(right)
    right = jnp.concatenate([high, high, low, low], axis=0)
    row = lax.broadcasted_iota(jnp.int32, right.shape, 0) % (mats * RANK)
    copies = []
    for mat in range(mats):
        weights = jnp.where(row // RANK == mat, right, 0.0).astype(BF16)
        for chunk in range(CHUNKS):
            at = pl.ds(chunk * size, size)
            slot = mat * CHUNKS + chunk
            approx = jnp.dot(left_ref[at], weights, preferred_element_type=F32)
            ubuf[mat, at] = approx.astype(BF16)
            ebuf[mat, at] = merged_ref[mat, at] - approx
            for copy in (
                pltpu.make_async_copy(ubuf.at[mat, at], update_ref.at[mat, at], sems.at[0, slot]),
                pltpu.make_async_copy(ebuf.at[mat, at], errors_ref.at[0, mat, at], sems.at[1, slot]),
            ):
                copy.start()
                copies.append(copy)
    for copy in copies:
        copy.wait()


def finish(left, merged, own, both, taken, given, scale):
    mats, rows, cols = merged.shape
    return pl.pallas_call(
        functools.partial(finish_body, scale, len(taken)),
        out_shape=(
            jax.ShapeDtypeStruct((mats, rows, cols), BF16),
            jax.ShapeDtypeStruct((1, mats, rows, cols), F32),
        ),
        in_specs=[pl.BlockSpec(memory_space=pltpu.VMEM)] * (4 + 2 * len(taken)),
        out_specs=[pl.BlockSpec(memory_space=pltpu.HBM)] * 2,
        scratch_shapes=[
            pltpu.VMEM((mats, rows, cols), BF16),
            pltpu.VMEM((mats, rows, cols), F32),
            pltpu.SemaphoreType.DMA((2, mats * CHUNKS)),
        ],
        compiler_params=pltpu.CompilerParams(vmem_limit_bytes=16 * 2**20),
        name="finish",
    )(
        pltpu.with_memory_space_constraint(left, pltpu.VMEM),
        pltpu.with_memory_space_constraint(merged, pltpu.VMEM),
        own,
        both,
        *taken,
        *given,
    )


def swap(value, axes, pairs):
    return lax.ppermute(value, axes, pairs + [(target, source) for source, target in pairs])


def swap_cores(value):
    return swap(value, "tensor", [(0, 1)])


def swap_chips(value, masks, cross=0):
    pairs = []
    for core in range(2):
        for at in range(lax.axis_size("dp")):
            partner = at ^ masks[core]
            if at < partner:
                pairs.append((2 * at + core, 2 * partner + (core ^ cross)))
    return swap(value, ("dp", "tensor"), pairs)


def chips_terms(value, split, turned):
    count = lax.axis_size("dp")
    last = count // 8
    step = 1
    while step < last:
        value = value + turned(swap_chips(value, (step, step), 1))
        step *= 2
    both = swap_chips(value, (SHARED * last, SHARED * last), 1)
    taken = [swap_chips(value, (lower * last, upper * last)) for lower, upper in split[::-1]][::-1]
    return value, both, taken, [swap_cores(term) for term in taken]


def body(grads, errors, seeds):
    replicas = lax.axis_size("dp")
    left_part, grads, errors = project(seeds, grads, errors)
    merged, high, low, zero = merge(grads, errors)
    both = jnp.stack([left_part, swap_cores(left_part) + zero], axis=0)
    terms = chips_terms(both, LEFT_SPLIT, lambda taken: lax.rev(taken, (0,)))
    left, right_part = reflect(high, low, *terms, 1.0 / replicas)
    terms = chips_terms(right_part + swap_cores(right_part), RIGHT_SPLIT, lambda taken: taken)
    return finish(turn(left), merged, *terms, 1.0 / replicas)


def solution(mesh):
    in_specs = (
        P(("groups", "dp"), None, "tensor", None),
        P(("groups", "dp"), None, "tensor", None),
        P(),
    )
    out_specs = (P("groups", "tensor", None), P(("groups", "dp"), None, "tensor", None))
    return jax.shard_map(body, mesh=mesh, in_specs=in_specs, out_specs=out_specs, check_vma=False)
```

```python
import functools

import jax
import jax.numpy as jnp
from jax import lax
from jax.experimental import pallas as pl
from jax.experimental.pallas import tpu as pltpu
from jax.sharding import PartitionSpec as P

RANK = 4
EPSILON = 1e-08
CHUNKS = 4
SPLIT = ((1, 7), (5, 4), (2, 6))
SHARED = 3
BF16 = jnp.bfloat16
F32 = jnp.float32


def halves(value):
    high = value.astype(BF16).astype(F32)
    return high, value - high


def start_rows(seeds_ref, mats, cols):
    shape = (mats * RANK, cols)
    row = lax.broadcasted_iota(jnp.int32, shape, 0)
    col = lax.broadcasted_iota(jnp.int32, shape, 1)
    mat = row // RANK
    seed = jnp.full(shape, seeds_ref[0], jnp.int32)
    for index in range(1, mats):
        seed = jnp.where(mat == index, seeds_ref[index], seed)
    mixed = ((row - mat * RANK) * cols + col) * 747796405 + seed * 277803737 + 12345
    mixed = mixed ^ (mixed >> 15)
    mixed = mixed * 1274126177
    mixed = mixed ^ (mixed >> 13)
    lowbits = jnp.bitwise_and(mixed, 65535)
    return (lowbits.astype(F32) - 32767.5) / 32768.0


def fold(mat, value, product):
    part = product[: value.shape[0]] + product[value.shape[0] :]
    row = lax.broadcasted_iota(jnp.int32, value.shape, 0)
    return jnp.where(row // RANK == mat, part, value)


def project_body(seeds_ref, grads_ref, errors_ref, left_ref, gbuf, ebuf, seed, seed_sem, sems):
    _, mats, rows, cols = grads_ref.shape
    size = rows // CHUNKS
    seed_copy = pltpu.make_async_copy(seeds_ref, seed, seed_sem)
    seed_copy.start()
    copies = []
    for chunk in range(CHUNKS):
        at = pl.ds(chunk * size, size)
        for mat in range(mats):
            slot = chunk * mats + mat
            copies.append(pltpu.make_async_copy(grads_ref.at[0, mat, at], gbuf.at[mat, at], sems.at[0, slot]))
            copies.append(pltpu.make_async_copy(errors_ref.at[0, mat, at], ebuf.at[mat, at], sems.at[1, slot]))
    for copy in copies:
        copy.start()
    seed_copy.wait()
    start = start_rows(seed, mats, cols)
    weights = jnp.concatenate(halves(start), axis=0).astype(BF16)
    dims = (((1,), (1,)), ((), ()))
    for chunk in range(CHUNKS):
        at = pl.ds(chunk * size, size)
        left = jnp.zeros((mats * RANK, size), F32)
        for copy in copies[2 * mats * chunk : 2 * mats * (chunk + 1)]:
            copy.wait()
        for mat in range(mats):
            value = gbuf[mat, at].astype(F32) + ebuf[mat, at]
            high = value.astype(BF16)
            low = (value - high.astype(F32)).astype(BF16)
            product = lax.dot_general(weights, high, dims, preferred_element_type=F32)
            product = product + lax.dot_general(weights, low, dims, preferred_element_type=F32)
            left = fold(mat, left, product)
        left_ref[:, at] = left


def project(seeds, grads, errors):
    _, mats, rows, cols = grads.shape
    return pl.pallas_call(
        project_body,
        out_shape=(
            jax.ShapeDtypeStruct((mats * RANK, rows), F32),
            pltpu.VMEM((mats, rows, cols), BF16),
            pltpu.VMEM((mats, rows, cols), F32),
        ),
        in_specs=[pl.BlockSpec(memory_space=pltpu.HBM)] * 3,
        out_specs=[pl.BlockSpec(memory_space=pltpu.VMEM)] * 3,
        scratch_shapes=[
            pltpu.SMEM(seeds.shape, seeds.dtype),
            pltpu.SemaphoreType.DMA,
            pltpu.SemaphoreType.DMA((2, mats * CHUNKS)),
        ],
        compiler_params=pltpu.CompilerParams(vmem_limit_bytes=16 * 2**20),
        name="project",
    )(*[pltpu.with_memory_space_constraint(value, pltpu.HBM) for value in (seeds, grads, errors)])


def merge_body(grads_ref, errors_ref, merged_ref, high_ref, low_ref, zero_ref):
    mats, rows, cols = grads_ref.shape
    size = 64
    zero_ref[...] = jnp.zeros_like(zero_ref)

    @pl.loop(0, rows // size)
    def _(step):
        at = pl.ds(pl.multiple_of(step * size, size), size)
        for mat in range(mats):
            value = grads_ref[mat, at].astype(F32) + errors_ref[mat, at]
            high = value.astype(BF16)
            merged_ref[mat, at] = value
            high_ref[mat, at] = high
            low_ref[mat, at] = (value - high.astype(F32)).astype(BF16)


def merge(grads, errors):
    shape = grads.shape
    return pl.pallas_call(
        merge_body,
        out_shape=(
            pltpu.VMEM(shape, F32),
            pltpu.VMEM(shape, BF16),
            pltpu.VMEM(shape, BF16),
            jax.ShapeDtypeStruct((shape[0] * RANK, shape[1]), F32),
        ),
        in_specs=[pl.BlockSpec(memory_space=pltpu.VMEM)] * 2,
        out_specs=[pl.BlockSpec(memory_space=pltpu.VMEM)] * 4,
        compiler_params=pltpu.CompilerParams(vmem_limit_bytes=16 * 2**20),
        cost_estimate=pl.CostEstimate(flops=3 * grads.size, bytes_accessed=14 * grads.size, transcendentals=0),
        name="merge",
    )(*[pltpu.with_memory_space_constraint(value, pltpu.VMEM) for value in (grads, errors)])


def pick(rows, index, count):
    return jnp.concatenate(
        [
            jnp.broadcast_to(rows[start + index : start + index + 1], (RANK, rows.shape[1]))
            for start in range(0, count, RANK)
        ],
        axis=0,
    )


def orthogonal(mine, other):
    count = mine.shape[0]
    rank = lax.broadcasted_iota(jnp.int32, (count, 1), 0) % RANK
    for index in range(RANK):
        current = pick(mine, index, count)
        partner = pick(other, index, count)
        products = jnp.sum(mine * current + other * partner, axis=1, keepdims=True)
        inverse = 1.0 / (jnp.sqrt(pick(products, index, count)) + EPSILON)
        inner = products * inverse
        weight = jnp.where(rank > index, inner * inverse, 0.0)
        here = rank == index
        mine = jnp.where(here, mine * inverse, mine - weight * current)
        if index < RANK - 1:
            other = jnp.where(here, other * inverse, other - weight * partner)
    return mine


def reflect_body(scale, kept_ref, given_ref, high_ref, low_ref, left_ref, right_ref):
    mats, rows, cols = high_ref.shape
    idle = lax.axis_index("tensor") == 0
    mine = jnp.where(idle, given_ref[1], kept_ref[0]) * scale
    other = jnp.where(idle, given_ref[0], kept_ref[1]) * scale
    left = orthogonal(mine, other)
    left_ref[...] = left
    weights = jnp.concatenate(halves(left), axis=0).astype(BF16)
    right = jnp.zeros((mats * RANK, cols), F32)
    for mat in range(mats):
        product = jnp.dot(weights, high_ref[mat], preferred_element_type=F32)
        product = product + jnp.dot(weights, low_ref[mat], preferred_element_type=F32)
        right = fold(mat, right, product)
    right_ref[...] = right


def reflect(kept, given, high, low, scale):
    mats, rows, cols = high.shape
    return pl.pallas_call(
        functools.partial(reflect_body, scale),
        out_shape=(
            jax.ShapeDtypeStruct((mats * RANK, rows), F32),
            jax.ShapeDtypeStruct((mats * RANK, cols), F32),
        ),
        in_specs=[pl.BlockSpec(memory_space=pltpu.VMEM)] * 4,
        out_specs=[pl.BlockSpec(memory_space=pltpu.VMEM)] * 2,
        compiler_params=pltpu.CompilerParams(vmem_limit_bytes=24 * 2**20),
        name="reflect",
    )(kept, given, pltpu.with_memory_space_constraint(high, pltpu.VMEM), pltpu.with_memory_space_constraint(low, pltpu.VMEM))


def turn_body(left_ref, turned_ref):
    high, low = halves(left_ref[...])
    turned_ref[...] = jnp.concatenate([high, low, high, low], axis=0).T.astype(BF16)


def turn(left):
    count, rows = left.shape
    return pl.pallas_call(
        turn_body,
        out_shape=pltpu.VMEM((rows, 4 * count), BF16),
        in_specs=[pl.BlockSpec(memory_space=pltpu.VMEM)],
        out_specs=pl.BlockSpec(memory_space=pltpu.VMEM),
        compiler_params=pltpu.CompilerParams(vmem_limit_bytes=16 * 2**20),
        cost_estimate=pl.CostEstimate(flops=16 * left.size, bytes_accessed=64 * left.size, transcendentals=0),
        name="turn",
    )(left)


def total(own_ref, both_ref, taken_refs, given_refs):
    first = lax.axis_index("tensor") == 0
    terms = {0: own_ref[...], SHARED: both_ref[...]}
    for masks, taken_ref, given_ref in zip(SPLIT, taken_refs, given_refs):
        taken, given = taken_ref[...], given_ref[...]
        terms[masks[0]] = jnp.where(first, taken, given)
        terms[masks[1]] = jnp.where(first, given, taken)
    sums = [terms[index] for index in range(len(terms))]
    while len(sums) > 1:
        sums = [sums[at] + sums[at + 1] for at in range(0, len(sums), 2)]
    return sums[0]


def finish_body(scale, count, left_ref, merged_ref, own_ref, both_ref, *refs):
    taken_refs, given_refs = refs[:count], refs[count : 2 * count]
    update_ref, errors_ref, ubuf, ebuf, sems = refs[2 * count :]
    right = total(own_ref, both_ref, taken_refs, given_refs) * scale
    finish_rows(right, left_ref, merged_ref, update_ref, errors_ref, ubuf, ebuf, sems)


def finish_rows(right, left_ref, merged_ref, update_ref, errors_ref, ubuf, ebuf, sems):
    mats, rows, cols = merged_ref.shape
    size = rows // CHUNKS
    high, low = halves(right)
    right = jnp.concatenate([high, high, low, low], axis=0)
    row = lax.broadcasted_iota(jnp.int32, right.shape, 0) % (mats * RANK)
    copies = []
    for mat in range(mats):
        weights = jnp.where(row // RANK == mat, right, 0.0).astype(BF16)
        for chunk in range(CHUNKS):
            at = pl.ds(chunk * size, size)
            slot = mat * CHUNKS + chunk
            approx = jnp.dot(left_ref[at], weights, preferred_element_type=F32)
            ubuf[mat, at] = approx.astype(BF16)
            ebuf[mat, at] = merged_ref[mat, at] - approx
            for copy in (
                pltpu.make_async_copy(ubuf.at[mat, at], update_ref.at[mat, at], sems.at[0, slot]),
                pltpu.make_async_copy(ebuf.at[mat, at], errors_ref.at[0, mat, at], sems.at[1, slot]),
            ):
                copy.start()
                copies.append(copy)
    for copy in copies:
        copy.wait()


def finish(left, merged, own, both, taken, given, scale):
    mats, rows, cols = merged.shape
    return pl.pallas_call(
        functools.partial(finish_body, scale, len(taken)),
        out_shape=(
            jax.ShapeDtypeStruct((mats, rows, cols), BF16),
            jax.ShapeDtypeStruct((1, mats, rows, cols), F32),
        ),
        in_specs=[pl.BlockSpec(memory_space=pltpu.VMEM)] * (4 + 2 * len(taken)),
        out_specs=[pl.BlockSpec(memory_space=pltpu.HBM)] * 2,
        scratch_shapes=[
            pltpu.VMEM((mats, rows, cols), BF16),
            pltpu.VMEM((mats, rows, cols), F32),
            pltpu.SemaphoreType.DMA((2, mats * CHUNKS)),
        ],
        compiler_params=pltpu.CompilerParams(vmem_limit_bytes=16 * 2**20),
        name="finish",
    )(
        pltpu.with_memory_space_constraint(left, pltpu.VMEM),
        pltpu.with_memory_space_constraint(merged, pltpu.VMEM),
        own,
        both,
        *taken,
        *given,
    )


def swap(value, axes, pairs):
    return lax.ppermute(value, axes, pairs + [(target, source) for source, target in pairs])


def swap_cores(value):
    return swap(value, "tensor", [(0, 1)])


def swap_chips(value, masks, cross=0):
    pairs = []
    for core in range(2):
        for at in range(lax.axis_size("dp")):
            partner = at ^ masks[core]
            if at < partner:
                pairs.append((2 * at + core, 2 * partner + (core ^ cross)))
    return swap(value, ("dp", "tensor"), pairs)


def swap_fast(value, mask):
    groups, count = lax.axis_size("groups"), lax.axis_size("dp")
    pairs = []
    for group in range(groups):
        for at in range(count):
            place = 2 * (group * count + at)
            partner = 2 * (group * count + (at ^ mask))
            idle = 2 * ((group ^ 1) * count + at) if groups % 2 == 0 else partner
            if place < partner:
                pairs.append((place + 1, partner + 1))
            if place < idle:
                pairs.append((place, idle))
    return swap(value, ("groups", "dp", "tensor"), pairs)


def fast_sum(value):
    count = lax.axis_size("dp")
    last = max(count // 4, 1)
    step = 1
    while step < last:
        value = value + swap_fast(value, step)
        step *= 2
    terms = [value] + [swap_fast(value, offset) for offset in range(last, count, last)]
    while len(terms) > 1:
        terms = [terms[at + 1] + terms[at] for at in range(0, len(terms), 2)]
    return terms[0]


def chips_terms(value):
    count = lax.axis_size("dp")
    last = count // 8
    step = 1
    while step < last:
        value = value + swap_chips(value, (step, step), 1)
        step *= 2
    both = swap_chips(value, (SHARED * last, SHARED * last), 1)
    taken = [swap_chips(value, (lower * last, upper * last)) for lower, upper in SPLIT[::-1]][::-1]
    return value, both, taken, [swap_cores(term) for term in taken]


def body(grads, errors, seeds):
    replicas = lax.axis_size("dp")
    left_part, grads, errors = project(seeds, grads, errors)
    merged, high, low, zero = merge(grads, errors)
    kept = fast_sum(jnp.stack([left_part, swap_cores(left_part) + zero], axis=0))
    left, right_part = reflect(kept, swap_cores(kept), high, low, 1.0 / replicas)
    terms = chips_terms(right_part + swap_cores(right_part))
    return finish(turn(left), merged, *terms, 1.0 / replicas)


def solution(mesh):
    in_specs = (
        P(("groups", "dp"), None, "tensor", None),
        P(("groups", "dp"), None, "tensor", None),
        P(),
    )
    out_specs = (P("groups", "tensor", None), P(("groups", "dp"), None, "tensor", None))
    return jax.shard_map(body, mesh=mesh, in_specs=in_specs, out_specs=out_specs, check_vma=False)
```

```python
import functools

import jax
import jax.numpy as jnp
from jax import lax
from jax.experimental import pallas as pl
from jax.experimental.pallas import tpu as pltpu
from jax.sharding import PartitionSpec as P

RANK = 4
EPSILON = 1e-08
CHUNKS = 4
SPLIT = ((1, 7), (5, 4), (2, 6))
SHARED = 3
BF16 = jnp.bfloat16
F32 = jnp.float32


def halves(value):
    high = value.astype(BF16).astype(F32)
    return high, value - high


def thirds(value):
    high, rest = halves(value)
    middle, low = halves(rest)
    return high, middle, low


def start_rows(seeds_ref, mats, cols):
    shape = (mats * RANK, cols)
    row = lax.broadcasted_iota(jnp.int32, shape, 0)
    col = lax.broadcasted_iota(jnp.int32, shape, 1)
    mat = row // RANK
    seed = jnp.full(shape, seeds_ref[0], jnp.int32)
    for index in range(1, mats):
        seed = jnp.where(mat == index, seeds_ref[index], seed)
    mixed = ((row - mat * RANK) * cols + col) * 747796405 + seed * 277803737 + 12345
    mixed = mixed ^ (mixed >> 15)
    mixed = mixed * 1274126177
    mixed = mixed ^ (mixed >> 13)
    lowbits = jnp.bitwise_and(mixed, 65535)
    return (lowbits.astype(F32) - 32767.5) / 32768.0


def fold(mat, value, product):
    part = product[: value.shape[0]] + product[value.shape[0] :]
    row = lax.broadcasted_iota(jnp.int32, value.shape, 0)
    return jnp.where(row // RANK == mat, part, value)


def project_body(seeds_ref, grads_ref, errors_ref, left_ref, gbuf, ebuf, seed, seed_sem, sems):
    _, mats, rows, cols = grads_ref.shape
    size = rows // CHUNKS
    seed_copy = pltpu.make_async_copy(seeds_ref, seed, seed_sem)
    seed_copy.start()
    copies = []
    for chunk in range(CHUNKS):
        at = pl.ds(chunk * size, size)
        for mat in range(mats):
            slot = chunk * mats + mat
            copies.append(pltpu.make_async_copy(grads_ref.at[0, mat, at], gbuf.at[mat, at], sems.at[0, slot]))
            copies.append(pltpu.make_async_copy(errors_ref.at[0, mat, at], ebuf.at[mat, at], sems.at[1, slot]))
    for copy in copies:
        copy.start()
    seed_copy.wait()
    start = start_rows(seed, mats, cols)
    weights = jnp.concatenate(halves(start), axis=0).astype(BF16)
    dims = (((1,), (1,)), ((), ()))
    for chunk in range(CHUNKS):
        at = pl.ds(chunk * size, size)
        left = jnp.zeros((mats * RANK, size), F32)
        for copy in copies[2 * mats * chunk : 2 * mats * (chunk + 1)]:
            copy.wait()
        for mat in range(mats):
            value = gbuf[mat, at].astype(F32) + ebuf[mat, at]
            high = value.astype(BF16)
            low = (value - high.astype(F32)).astype(BF16)
            product = lax.dot_general(weights, high, dims, preferred_element_type=F32)
            product = product + lax.dot_general(weights, low, dims, preferred_element_type=F32)
            left = fold(mat, left, product)
        left_ref[:, at] = left


def project(seeds, grads, errors):
    _, mats, rows, cols = grads.shape
    return pl.pallas_call(
        project_body,
        out_shape=(
            jax.ShapeDtypeStruct((mats * RANK, rows), F32),
            pltpu.VMEM((mats, rows, cols), BF16),
            pltpu.VMEM((mats, rows, cols), F32),
        ),
        in_specs=[pl.BlockSpec(memory_space=pltpu.HBM)] * 3,
        out_specs=[pl.BlockSpec(memory_space=pltpu.VMEM)] * 3,
        scratch_shapes=[
            pltpu.SMEM(seeds.shape, seeds.dtype),
            pltpu.SemaphoreType.DMA,
            pltpu.SemaphoreType.DMA((2, mats * CHUNKS)),
        ],
        compiler_params=pltpu.CompilerParams(vmem_limit_bytes=16 * 2**20),
        name="project",
    )(*[pltpu.with_memory_space_constraint(value, pltpu.HBM) for value in (seeds, grads, errors)])


def merge_body(grads_ref, errors_ref, merged_ref, high_ref, low_ref, zero_ref):
    mats, rows, cols = grads_ref.shape
    size = 64
    zero_ref[...] = jnp.zeros_like(zero_ref)

    @pl.loop(0, rows // size)
    def _(step):
        at = pl.ds(pl.multiple_of(step * size, size), size)
        for mat in range(mats):
            value = grads_ref[mat, at].astype(F32) + errors_ref[mat, at]
            high = value.astype(BF16)
            merged_ref[mat, at] = value
            high_ref[mat, at] = high
            low_ref[mat, at] = (value - high.astype(F32)).astype(BF16)


def merge(grads, errors):
    shape = grads.shape
    return pl.pallas_call(
        merge_body,
        out_shape=(
            pltpu.VMEM(shape, F32),
            pltpu.VMEM(shape, BF16),
            pltpu.VMEM(shape, BF16),
            jax.ShapeDtypeStruct((shape[0] * RANK, shape[1]), F32),
        ),
        in_specs=[pl.BlockSpec(memory_space=pltpu.VMEM)] * 2,
        out_specs=[pl.BlockSpec(memory_space=pltpu.VMEM)] * 4,
        compiler_params=pltpu.CompilerParams(vmem_limit_bytes=16 * 2**20),
        cost_estimate=pl.CostEstimate(flops=3 * grads.size, bytes_accessed=14 * grads.size, transcendentals=0),
        name="merge",
    )(*[pltpu.with_memory_space_constraint(value, pltpu.VMEM) for value in (grads, errors)])


def pick(rows, index, count):
    return jnp.concatenate(
        [
            jnp.broadcast_to(rows[start + index : start + index + 1], (RANK, rows.shape[1]))
            for start in range(0, count, RANK)
        ],
        axis=0,
    )


def orthogonal(mine, other):
    count = mine.shape[0]
    rank = lax.broadcasted_iota(jnp.int32, (count, 1), 0) % RANK
    for index in range(RANK):
        current = pick(mine, index, count)
        partner = pick(other, index, count)
        products = jnp.sum(mine * current + other * partner, axis=1, keepdims=True)
        inverse = 1.0 / (jnp.sqrt(pick(products, index, count)) + EPSILON)
        inner = products * inverse
        weight = jnp.where(rank > index, inner * inverse, 0.0)
        here = rank == index
        mine = jnp.where(here, mine * inverse, mine - weight * current)
        if index < RANK - 1:
            other = jnp.where(here, other * inverse, other - weight * partner)
    return mine


def reflect_body(scale, mine_ref, other_ref, high_ref, low_ref, left_ref, right_ref):
    mats, rows, cols = high_ref.shape
    left = orthogonal(mine_ref[...] * scale, other_ref[...] * scale)
    left_ref[...] = left
    weights = jnp.concatenate(halves(left), axis=0).astype(BF16)
    right = jnp.zeros((mats * RANK, cols), F32)
    for mat in range(mats):
        product = jnp.dot(weights, high_ref[mat], preferred_element_type=F32)
        product = product + jnp.dot(weights, low_ref[mat], preferred_element_type=F32)
        right = fold(mat, right, product)
    right_ref[...] = right


def reflect(mine, other, high, low, scale):
    mats, rows, cols = high.shape
    return pl.pallas_call(
        functools.partial(reflect_body, scale),
        out_shape=(
            jax.ShapeDtypeStruct((mats * RANK, rows), F32),
            jax.ShapeDtypeStruct((mats * RANK, cols), F32),
        ),
        in_specs=[pl.BlockSpec(memory_space=pltpu.VMEM)] * 4,
        out_specs=[pl.BlockSpec(memory_space=pltpu.VMEM)] * 2,
        compiler_params=pltpu.CompilerParams(vmem_limit_bytes=24 * 2**20),
        name="reflect",
    )(mine, other, pltpu.with_memory_space_constraint(high, pltpu.VMEM), pltpu.with_memory_space_constraint(low, pltpu.VMEM))


def turn_body(left_ref, turned_ref):
    high, middle, low = thirds(left_ref[...])
    turned_ref[...] = jnp.concatenate([high, high, high, middle, middle, low], axis=0).T.astype(BF16)


def turn(left):
    count, rows = left.shape
    return pl.pallas_call(
        turn_body,
        out_shape=pltpu.VMEM((rows, 6 * count), BF16),
        in_specs=[pl.BlockSpec(memory_space=pltpu.VMEM)],
        out_specs=pl.BlockSpec(memory_space=pltpu.VMEM),
        compiler_params=pltpu.CompilerParams(vmem_limit_bytes=16 * 2**20),
        cost_estimate=pl.CostEstimate(flops=16 * left.size, bytes_accessed=64 * left.size, transcendentals=0),
        name="turn",
    )(left)


def total(own_ref, both_ref, taken_refs, given_refs):
    first = lax.axis_index("tensor") == 0
    terms = {0: own_ref[...], SHARED: both_ref[...]}
    for masks, taken_ref, given_ref in zip(SPLIT, taken_refs, given_refs):
        taken, given = taken_ref[...], given_ref[...]
        terms[masks[0]] = jnp.where(first, taken, given)
        terms[masks[1]] = jnp.where(first, given, taken)
    sums = [terms[index] for index in range(len(terms))]
    while len(sums) > 1:
        sums = [sums[at] + sums[at + 1] for at in range(0, len(sums), 2)]
    return sums[0]


def finish_body(scale, count, left_ref, merged_ref, own_ref, both_ref, *refs):
    taken_refs, given_refs = refs[:count], refs[count : 2 * count]
    update_ref, errors_ref, ubuf, ebuf, sems = refs[2 * count :]
    right = total(own_ref, both_ref, taken_refs, given_refs) * scale
    finish_rows(right, left_ref, merged_ref, update_ref, errors_ref, ubuf, ebuf, sems)


def finish_rows(right, left_ref, merged_ref, update_ref, errors_ref, ubuf, ebuf, sems):
    mats, rows, cols = merged_ref.shape
    size = rows // CHUNKS
    high, middle, low = thirds(right)
    right = jnp.concatenate([high, middle, low, high, middle, high], axis=0)
    row = lax.broadcasted_iota(jnp.int32, right.shape, 0) % (mats * RANK)
    copies = []
    for mat in range(mats):
        weights = jnp.where(row // RANK == mat, right, 0.0).astype(BF16)
        for chunk in range(CHUNKS):
            at = pl.ds(chunk * size, size)
            slot = mat * CHUNKS + chunk
            approx = jnp.dot(left_ref[at], weights, preferred_element_type=F32)
            ubuf[mat, at] = approx.astype(BF16)
            ebuf[mat, at] = merged_ref[mat, at] - approx
            for copy in (
                pltpu.make_async_copy(ubuf.at[mat, at], update_ref.at[mat, at], sems.at[0, slot]),
                pltpu.make_async_copy(ebuf.at[mat, at], errors_ref.at[0, mat, at], sems.at[1, slot]),
            ):
                copy.start()
                copies.append(copy)
    for copy in copies:
        copy.wait()


def finish(left, merged, own, both, taken, given, scale):
    mats, rows, cols = merged.shape
    return pl.pallas_call(
        functools.partial(finish_body, scale, len(taken)),
        out_shape=(
            jax.ShapeDtypeStruct((mats, rows, cols), BF16),
            jax.ShapeDtypeStruct((1, mats, rows, cols), F32),
        ),
        in_specs=[pl.BlockSpec(memory_space=pltpu.VMEM)] * (4 + 2 * len(taken)),
        out_specs=[pl.BlockSpec(memory_space=pltpu.HBM)] * 2,
        scratch_shapes=[
            pltpu.VMEM((mats, rows, cols), BF16),
            pltpu.VMEM((mats, rows, cols), F32),
            pltpu.SemaphoreType.DMA((2, mats * CHUNKS)),
        ],
        compiler_params=pltpu.CompilerParams(vmem_limit_bytes=16 * 2**20),
        name="finish",
    )(
        pltpu.with_memory_space_constraint(left, pltpu.VMEM),
        pltpu.with_memory_space_constraint(merged, pltpu.VMEM),
        own,
        both,
        *taken,
        *given,
    )


def swap(value, axes, pairs):
    return lax.ppermute(value, axes, pairs + [(target, source) for source, target in pairs])


def swap_cores(value):
    return swap(value, "tensor", [(0, 1)])


def swap_chips(value, masks, cross=0):
    pairs = []
    for core in range(2):
        for at in range(lax.axis_size("dp")):
            partner = at ^ masks[core]
            if at < partner:
                pairs.append((2 * at + core, 2 * partner + (core ^ cross)))
    return swap(value, ("dp", "tensor"), pairs)


def chips_sum(value, zero):
    count = lax.axis_size("dp")
    last = max(count // 4, 1)
    step = 1
    while step < last:
        value = value + (zero + swap_chips(value, (step, step)))
        zero = 0.0
        step *= 2
    terms = [value] + [swap_chips(value, (offset, offset)) for offset in range(last, count, last)]
    while len(terms) > 1:
        terms = [terms[at] + terms[at + 1] for at in range(0, len(terms), 2)]
    return terms[0]


def chips_terms(value):
    count = lax.axis_size("dp")
    last = count // 8
    step = 1
    while step < last:
        value = value + swap_chips(value, (step, step), 1)
        step *= 2
    both = swap_chips(value, (SHARED * last, SHARED * last), 1)
    taken = [swap_chips(value, (lower * last, upper * last)) for lower, upper in SPLIT[::-1]][::-1]
    return value, both, taken, [swap_cores(term) for term in taken]


def body(grads, errors, seeds):
    replicas = lax.axis_size("dp")
    left_part, grads, errors = project(seeds, grads, errors)
    merged, high, low, zero = merge(grads, errors)
    mine = chips_sum(left_part, zero)
    left, right_part = reflect(mine, swap_cores(mine), high, low, 1.0 / replicas)
    terms = chips_terms(right_part + swap_cores(right_part))
    return finish(turn(left), merged, *terms, 1.0 / replicas)


def solution(mesh):
    in_specs = (
        P(("groups", "dp"), None, "tensor", None),
        P(("groups", "dp"), None, "tensor", None),
        P(),
    )
    out_specs = (P("groups", "tensor", None), P(("groups", "dp"), None, "tensor", None))
    return jax.shard_map(body, mesh=mesh, in_specs=in_specs, out_specs=out_specs, check_vma=False)
```

```python
import functools

import jax
import jax.numpy as jnp
from jax import lax
from jax.experimental import pallas as pl
from jax.experimental.pallas import tpu as pltpu
from jax.sharding import PartitionSpec as P

RANK = 4
EPSILON = 1e-08
CHUNKS = 4
SPLIT = ((1, 7), (5, 4), (2, 6))
SHARED = 3
BF16 = jnp.bfloat16
F32 = jnp.float32


def halves(value):
    high = value.astype(BF16).astype(F32)
    return high, value - high


def thirds(value):
    high, rest = halves(value)
    middle, low = halves(rest)
    return high, middle, low


def start_rows(seeds_ref, mats, cols):
    shape = (mats * RANK, cols)
    row = lax.broadcasted_iota(jnp.int32, shape, 0)
    col = lax.broadcasted_iota(jnp.int32, shape, 1)
    mat = row // RANK
    seed = jnp.full(shape, seeds_ref[0], jnp.int32)
    for index in range(1, mats):
        seed = jnp.where(mat == index, seeds_ref[index], seed)
    mixed = ((row - mat * RANK) * cols + col) * 747796405 + seed * 277803737 + 12345
    mixed = mixed ^ (mixed >> 15)
    mixed = mixed * 1274126177
    mixed = mixed ^ (mixed >> 13)
    lowbits = jnp.bitwise_and(mixed, 65535)
    return (lowbits.astype(F32) - 32767.5) / 32768.0


def fold(mat, value, product):
    part = product[: value.shape[0]] + product[value.shape[0] :]
    row = lax.broadcasted_iota(jnp.int32, value.shape, 0)
    return jnp.where(row // RANK == mat, part, value)


def project_body(seeds_ref, grads_ref, errors_ref, left_ref, gbuf, ebuf, seed, seed_sem, sems):
    _, mats, rows, cols = grads_ref.shape
    size = rows // CHUNKS
    seed_copy = pltpu.make_async_copy(seeds_ref, seed, seed_sem)
    seed_copy.start()
    copies = []
    for chunk in range(CHUNKS):
        at = pl.ds(chunk * size, size)
        for mat in range(mats):
            slot = chunk * mats + mat
            copies.append(pltpu.make_async_copy(grads_ref.at[0, mat, at], gbuf.at[mat, at], sems.at[0, slot]))
            copies.append(pltpu.make_async_copy(errors_ref.at[0, mat, at], ebuf.at[mat, at], sems.at[1, slot]))
    for copy in copies:
        copy.start()
    seed_copy.wait()
    start = start_rows(seed, mats, cols)
    weights = jnp.concatenate(halves(start), axis=0).astype(BF16)
    dims = (((1,), (1,)), ((), ()))
    for chunk in range(CHUNKS):
        at = pl.ds(chunk * size, size)
        left = jnp.zeros((mats * RANK, size), F32)
        for copy in copies[2 * mats * chunk : 2 * mats * (chunk + 1)]:
            copy.wait()
        for mat in range(mats):
            value = gbuf[mat, at].astype(F32) + ebuf[mat, at]
            high = value.astype(BF16)
            low = (value - high.astype(F32)).astype(BF16)
            product = lax.dot_general(weights, high, dims, preferred_element_type=F32)
            product = product + lax.dot_general(weights, low, dims, preferred_element_type=F32)
            left = fold(mat, left, product)
        left_ref[:, at] = left


def project(seeds, grads, errors):
    _, mats, rows, cols = grads.shape
    return pl.pallas_call(
        project_body,
        out_shape=(
            jax.ShapeDtypeStruct((mats * RANK, rows), F32),
            pltpu.VMEM((mats, rows, cols), BF16),
            pltpu.VMEM((mats, rows, cols), F32),
        ),
        in_specs=[pl.BlockSpec(memory_space=pltpu.HBM)] * 3,
        out_specs=[pl.BlockSpec(memory_space=pltpu.VMEM)] * 3,
        scratch_shapes=[
            pltpu.SMEM(seeds.shape, seeds.dtype),
            pltpu.SemaphoreType.DMA,
            pltpu.SemaphoreType.DMA((2, mats * CHUNKS)),
        ],
        compiler_params=pltpu.CompilerParams(vmem_limit_bytes=16 * 2**20),
        name="project",
    )(*[pltpu.with_memory_space_constraint(value, pltpu.HBM) for value in (seeds, grads, errors)])


def merge_body(grads_ref, errors_ref, merged_ref, high_ref, low_ref, zero_ref):
    mats, rows, cols = grads_ref.shape
    size = 64
    zero_ref[...] = jnp.zeros_like(zero_ref)

    @pl.loop(0, rows // size)
    def _(step):
        at = pl.ds(pl.multiple_of(step * size, size), size)
        for mat in range(mats):
            value = grads_ref[mat, at].astype(F32) + errors_ref[mat, at]
            high = value.astype(BF16)
            merged_ref[mat, at] = value
            high_ref[mat, at] = high
            low_ref[mat, at] = (value - high.astype(F32)).astype(BF16)


def merge(grads, errors):
    shape = grads.shape
    return pl.pallas_call(
        merge_body,
        out_shape=(
            pltpu.VMEM(shape, F32),
            pltpu.VMEM(shape, BF16),
            pltpu.VMEM(shape, BF16),
            jax.ShapeDtypeStruct((shape[0] * RANK, shape[1]), F32),
        ),
        in_specs=[pl.BlockSpec(memory_space=pltpu.VMEM)] * 2,
        out_specs=[pl.BlockSpec(memory_space=pltpu.VMEM)] * 4,
        compiler_params=pltpu.CompilerParams(vmem_limit_bytes=16 * 2**20),
        cost_estimate=pl.CostEstimate(flops=3 * grads.size, bytes_accessed=14 * grads.size, transcendentals=0),
        name="merge",
    )(*[pltpu.with_memory_space_constraint(value, pltpu.VMEM) for value in (grads, errors)])


def pick(rows, index, count):
    return jnp.concatenate(
        [
            jnp.broadcast_to(rows[start + index : start + index + 1], (RANK, rows.shape[1]))
            for start in range(0, count, RANK)
        ],
        axis=0,
    )


def orthogonal(mine, other):
    count = mine.shape[0]
    rank = lax.broadcasted_iota(jnp.int32, (count, 1), 0) % RANK
    steps = []
    for index in range(RANK):
        current = pick(mine, index, count)
        partner = pick(other, index, count)
        products = jnp.sum(mine * current + other * partner, axis=1, keepdims=True)
        inverse = 1.0 / (jnp.sqrt(pick(products, index, count)) + EPSILON)
        weight = jnp.where(rank > index, products * inverse * inverse, 0.0)
        steps.append(jnp.where(rank == index, inverse, weight))
        mine = row_step(mine, current, steps[-1], index)
        if index < RANK - 1:
            other = row_step(other, partner, steps[-1], index)
    return mine, steps


def row_step(rows, current, step, index):
    rank = lax.broadcasted_iota(jnp.int32, (rows.shape[0], 1), 0) % RANK
    return jnp.where(rank == index, rows * step, rows - step * current)


def reflect_body(scale, mine_ref, high_ref, low_ref, right_ref):
    mats, rows, cols = high_ref.shape
    weights = jnp.concatenate(halves(mine_ref[...] * scale), axis=0).astype(BF16)
    right = jnp.zeros((mats * RANK, cols), F32)
    for mat in range(mats):
        product = jnp.dot(weights, high_ref[mat], preferred_element_type=F32)
        product = product + jnp.dot(weights, low_ref[mat], preferred_element_type=F32)
        right = fold(mat, right, product)
    right_ref[...] = right


def reflect(mine, high, low, scale):
    mats, rows, cols = high.shape
    return pl.pallas_call(
        functools.partial(reflect_body, scale),
        out_shape=jax.ShapeDtypeStruct((mats * RANK, cols), F32),
        in_specs=[pl.BlockSpec(memory_space=pltpu.VMEM)] * 3,
        out_specs=pl.BlockSpec(memory_space=pltpu.VMEM),
        compiler_params=pltpu.CompilerParams(vmem_limit_bytes=16 * 2**20),
        cost_estimate=pl.CostEstimate(flops=64 * high.size, bytes_accessed=4 * high.size, transcendentals=0),
        name="reflect",
    )(mine, pltpu.with_memory_space_constraint(high, pltpu.VMEM), pltpu.with_memory_space_constraint(low, pltpu.VMEM))


def turn_body(scale, mine_ref, other_ref, turned_ref, steps_ref, zero_ref):
    zero_ref[...] = jnp.zeros_like(zero_ref)
    left, steps = orthogonal(mine_ref[...] * scale, other_ref[...] * scale)
    for index in range(RANK):
        steps_ref[index] = jnp.broadcast_to(steps[index], steps_ref.shape[1:])
    high, middle, low = thirds(left)
    turned_ref[...] = jnp.concatenate([high, high, high, middle, middle, low], axis=0).T.astype(BF16)


def turn(mine, other, cols, scale):
    count, rows = mine.shape
    return pl.pallas_call(
        functools.partial(turn_body, scale),
        out_shape=(
            pltpu.VMEM((rows, 6 * count), BF16),
            jax.ShapeDtypeStruct((RANK, count, cols), F32),
            jax.ShapeDtypeStruct((count, cols), F32),
        ),
        in_specs=[pl.BlockSpec(memory_space=pltpu.VMEM)] * 2,
        out_specs=[pl.BlockSpec(memory_space=pltpu.VMEM)] * 3,
        compiler_params=pltpu.CompilerParams(vmem_limit_bytes=16 * 2**20),
        cost_estimate=pl.CostEstimate(flops=64 * mine.size, bytes_accessed=128 * mine.size, transcendentals=0),
        name="turn",
    )(mine, other)


def total(own_ref, both_ref, taken_refs, given_refs):
    first = lax.axis_index("tensor") == 0
    terms = {0: own_ref[...], SHARED: both_ref[...]}
    for masks, taken_ref, given_ref in zip(SPLIT, taken_refs, given_refs):
        taken, given = taken_ref[...], given_ref[...]
        terms[masks[0]] = jnp.where(first, taken, given)
        terms[masks[1]] = jnp.where(first, given, taken)
    sums = [terms[index] for index in range(len(terms))]
    while len(sums) > 1:
        sums = [sums[at] + sums[at + 1] for at in range(0, len(sums), 2)]
    return sums[0]


def finish_body(scale, count, left_ref, steps_ref, merged_ref, own_ref, both_ref, *refs):
    taken_refs, given_refs = refs[:count], refs[count : 2 * count]
    update_ref, errors_ref, ubuf, ebuf, sems = refs[2 * count :]
    right = total(own_ref, both_ref, taken_refs, given_refs) * scale
    for index in range(RANK):
        right = row_step(right, pick(right, index, right.shape[0]), steps_ref[index], index)
    finish_rows(right, left_ref, merged_ref, update_ref, errors_ref, ubuf, ebuf, sems)


def finish_rows(right, left_ref, merged_ref, update_ref, errors_ref, ubuf, ebuf, sems):
    mats, rows, cols = merged_ref.shape
    size = rows // CHUNKS
    high, middle, low = thirds(right)
    right = jnp.concatenate([high, middle, low, high, middle, high], axis=0)
    row = lax.broadcasted_iota(jnp.int32, right.shape, 0) % (mats * RANK)
    copies = []
    for mat in range(mats):
        weights = jnp.where(row // RANK == mat, right, 0.0).astype(BF16)
        for chunk in range(CHUNKS):
            at = pl.ds(chunk * size, size)
            slot = mat * CHUNKS + chunk
            approx = jnp.dot(left_ref[at], weights, preferred_element_type=F32)
            ubuf[mat, at] = approx.astype(BF16)
            ebuf[mat, at] = merged_ref[mat, at] - approx
            for copy in (
                pltpu.make_async_copy(ubuf.at[mat, at], update_ref.at[mat, at], sems.at[0, slot]),
                pltpu.make_async_copy(ebuf.at[mat, at], errors_ref.at[0, mat, at], sems.at[1, slot]),
            ):
                copy.start()
                copies.append(copy)
    for copy in copies:
        copy.wait()


def finish(left, steps, merged, own, both, taken, given, scale):
    mats, rows, cols = merged.shape
    return pl.pallas_call(
        functools.partial(finish_body, scale, len(taken)),
        out_shape=(
            jax.ShapeDtypeStruct((mats, rows, cols), BF16),
            jax.ShapeDtypeStruct((1, mats, rows, cols), F32),
        ),
        in_specs=[pl.BlockSpec(memory_space=pltpu.VMEM)] * (5 + 2 * len(taken)),
        out_specs=[pl.BlockSpec(memory_space=pltpu.HBM)] * 2,
        scratch_shapes=[
            pltpu.VMEM((mats, rows, cols), BF16),
            pltpu.VMEM((mats, rows, cols), F32),
            pltpu.SemaphoreType.DMA((2, mats * CHUNKS)),
        ],
        compiler_params=pltpu.CompilerParams(vmem_limit_bytes=16 * 2**20),
        name="finish",
    )(
        pltpu.with_memory_space_constraint(left, pltpu.VMEM),
        steps,
        pltpu.with_memory_space_constraint(merged, pltpu.VMEM),
        own,
        both,
        *taken,
        *given,
    )


def swap(value, axes, pairs):
    return lax.ppermute(value, axes, pairs + [(target, source) for source, target in pairs])


def swap_cores(value):
    return swap(value, "tensor", [(0, 1)])


def swap_chips(value, masks, cross=0):
    pairs = []
    for core in range(2):
        for at in range(lax.axis_size("dp")):
            partner = at ^ masks[core]
            if at < partner:
                pairs.append((2 * at + core, 2 * partner + (core ^ cross)))
    return swap(value, ("dp", "tensor"), pairs)


def chips_sum(value, zero):
    count = lax.axis_size("dp")
    last = max(count // 4, 1)
    step = 1
    while step < last:
        value = value + (zero + swap_chips(value, (step, step)))
        zero = 0.0
        step *= 2
    terms = [value] + [swap_chips(value, (offset, offset)) for offset in range(last, count, last)]
    while len(terms) > 1:
        terms = [terms[at] + terms[at + 1] for at in range(0, len(terms), 2)]
    return terms[0]


def chips_terms(value):
    count = lax.axis_size("dp")
    last = count // 8
    step = 1
    while step < last:
        value = value + swap_chips(value, (step, step), 1)
        step *= 2
    both = swap_chips(value, (SHARED * last, SHARED * last), 1)
    taken = [swap_chips(value, (lower * last, upper * last)) for lower, upper in SPLIT[::-1]][::-1]
    return value, both, taken, [swap_cores(term) for term in taken]


def body(grads, errors, seeds):
    replicas = lax.axis_size("dp")
    left_part, grads, errors = project(seeds, grads, errors)
    merged, high, low, zero = merge(grads, errors)
    mine = chips_sum(left_part, zero)
    other = swap_cores(mine)
    right_part = reflect(mine, high, low, 1.0 / replicas)
    left, steps, zero = turn(mine, other, right_part.shape[1], 1.0 / replicas)
    terms = chips_terms(right_part + (zero + swap_cores(right_part)))
    return finish(left, steps, merged, *terms, 1.0 / replicas)


def solution(mesh):
    in_specs = (
        P(("groups", "dp"), None, "tensor", None),
        P(("groups", "dp"), None, "tensor", None),
        P(),
    )
    out_specs = (P("groups", "tensor", None), P(("groups", "dp"), None, "tensor", None))
    return jax.shard_map(body, mesh=mesh, in_specs=in_specs, out_specs=out_specs, check_vma=False)
```

```python
import functools

import jax
import jax.numpy as jnp
from jax import lax
from jax.experimental import pallas as pl
from jax.experimental.pallas import tpu as pltpu
from jax.sharding import PartitionSpec as P

RANK = 4
EPSILON = 1e-08
CHUNKS = 4
SPLIT = ((1, 7), (5, 4), (2, 6))
SHARED = 3
BF16 = jnp.bfloat16
F32 = jnp.float32


def halves(value):
    high = value.astype(BF16).astype(F32)
    return high, value - high


def thirds(value):
    high, rest = halves(value)
    middle, low = halves(rest)
    return high, middle, low


def start_rows(seeds_ref, mats, cols):
    shape = (mats * RANK, cols)
    row = lax.broadcasted_iota(jnp.int32, shape, 0)
    col = lax.broadcasted_iota(jnp.int32, shape, 1)
    mat = row // RANK
    seed = jnp.full(shape, seeds_ref[0], jnp.int32)
    for index in range(1, mats):
        seed = jnp.where(mat == index, seeds_ref[index], seed)
    mixed = ((row - mat * RANK) * cols + col) * 747796405 + seed * 277803737 + 12345
    mixed = mixed ^ (mixed >> 15)
    mixed = mixed * 1274126177
    mixed = mixed ^ (mixed >> 13)
    lowbits = jnp.bitwise_and(mixed, 65535)
    return (lowbits.astype(F32) - 32767.5) / 32768.0


def fold(mat, value, product):
    part = product[: value.shape[0]] + product[value.shape[0] :]
    row = lax.broadcasted_iota(jnp.int32, value.shape, 0)
    return jnp.where(row // RANK == mat, part, value)


def project_body(seeds_ref, grads_ref, errors_ref, left_ref, gbuf, ebuf, seed, seed_sem, sems):
    _, mats, rows, cols = grads_ref.shape
    size = rows // CHUNKS
    seed_copy = pltpu.make_async_copy(seeds_ref, seed, seed_sem)
    seed_copy.start()
    copies = []
    for chunk in range(CHUNKS):
        at = pl.ds(chunk * size, size)
        for mat in range(mats):
            slot = chunk * mats + mat
            copies.append(pltpu.make_async_copy(grads_ref.at[0, mat, at], gbuf.at[mat, at], sems.at[0, slot]))
            copies.append(pltpu.make_async_copy(errors_ref.at[0, mat, at], ebuf.at[mat, at], sems.at[1, slot]))
    for copy in copies:
        copy.start()
    seed_copy.wait()
    start = start_rows(seed, mats, cols)
    weights = jnp.concatenate(halves(start), axis=0).astype(BF16)
    dims = (((1,), (1,)), ((), ()))
    for chunk in range(CHUNKS):
        at = pl.ds(chunk * size, size)
        left = jnp.zeros((mats * RANK, size), F32)
        for copy in copies[2 * mats * chunk : 2 * mats * (chunk + 1)]:
            copy.wait()
        for mat in range(mats):
            value = gbuf[mat, at].astype(F32) + ebuf[mat, at]
            high = value.astype(BF16)
            low = (value - high.astype(F32)).astype(BF16)
            product = lax.dot_general(weights, high, dims, preferred_element_type=F32)
            product = product + lax.dot_general(weights, low, dims, preferred_element_type=F32)
            left = fold(mat, left, product)
        left_ref[:, at] = left


def project(seeds, grads, errors):
    _, mats, rows, cols = grads.shape
    return pl.pallas_call(
        project_body,
        out_shape=(
            jax.ShapeDtypeStruct((mats * RANK, rows), F32),
            pltpu.VMEM((mats, rows, cols), BF16),
            pltpu.VMEM((mats, rows, cols), F32),
        ),
        in_specs=[pl.BlockSpec(memory_space=pltpu.HBM)] * 3,
        out_specs=[pl.BlockSpec(memory_space=pltpu.VMEM)] * 3,
        scratch_shapes=[
            pltpu.SMEM(seeds.shape, seeds.dtype),
            pltpu.SemaphoreType.DMA,
            pltpu.SemaphoreType.DMA((2, mats * CHUNKS)),
        ],
        compiler_params=pltpu.CompilerParams(vmem_limit_bytes=16 * 2**20),
        name="project",
    )(*[pltpu.with_memory_space_constraint(value, pltpu.HBM) for value in (seeds, grads, errors)])


def merge_body(grads_ref, errors_ref, merged_ref, high_ref, low_ref, zero_ref):
    mats, rows, cols = grads_ref.shape
    size = 64
    zero_ref[...] = jnp.zeros_like(zero_ref)

    @pl.loop(0, rows // size)
    def _(step):
        at = pl.ds(pl.multiple_of(step * size, size), size)
        for mat in range(mats):
            value = grads_ref[mat, at].astype(F32) + errors_ref[mat, at]
            high = value.astype(BF16)
            merged_ref[mat, at] = value
            high_ref[mat, at] = high
            low_ref[mat, at] = (value - high.astype(F32)).astype(BF16)


def merge(grads, errors):
    shape = grads.shape
    return pl.pallas_call(
        merge_body,
        out_shape=(
            pltpu.VMEM(shape, F32),
            pltpu.VMEM(shape, BF16),
            pltpu.VMEM(shape, BF16),
            jax.ShapeDtypeStruct((shape[0] * RANK, shape[1]), F32),
        ),
        in_specs=[pl.BlockSpec(memory_space=pltpu.VMEM)] * 2,
        out_specs=[pl.BlockSpec(memory_space=pltpu.VMEM)] * 4,
        compiler_params=pltpu.CompilerParams(vmem_limit_bytes=16 * 2**20),
        cost_estimate=pl.CostEstimate(flops=3 * grads.size, bytes_accessed=14 * grads.size, transcendentals=0),
        name="merge",
    )(*[pltpu.with_memory_space_constraint(value, pltpu.VMEM) for value in (grads, errors)])


def pick(rows, index, count):
    return jnp.concatenate(
        [
            jnp.broadcast_to(rows[start + index : start + index + 1], (RANK, rows.shape[1]))
            for start in range(0, count, RANK)
        ],
        axis=0,
    )


def orthogonal(mine, other):
    count = mine.shape[0]
    rank = lax.broadcasted_iota(jnp.int32, (count, 1), 0) % RANK
    steps = []
    for index in range(RANK):
        current = pick(mine, index, count)
        partner = pick(other, index, count)
        products = jnp.sum(mine * current + other * partner, axis=1, keepdims=True)
        inverse = 1.0 / (jnp.sqrt(pick(products, index, count)) + EPSILON)
        weight = jnp.where(rank > index, products * inverse * inverse, 0.0)
        steps.append(jnp.where(rank == index, inverse, weight))
        mine = row_step(mine, current, steps[-1], index)
        if index < RANK - 1:
            other = row_step(other, partner, steps[-1], index)
    return mine, steps


def row_step(rows, current, step, index):
    rank = lax.broadcasted_iota(jnp.int32, (rows.shape[0], 1), 0) % RANK
    return jnp.where(rank == index, rows * step, rows - step * current)


def reflect_body(scale, mine_ref, high_ref, low_ref, right_ref):
    mats, rows, cols = high_ref.shape
    weights = jnp.concatenate(halves(mine_ref[...] * scale), axis=0).astype(BF16)
    right = jnp.zeros((mats * RANK, cols), F32)
    for mat in range(mats):
        product = jnp.dot(weights, high_ref[mat], preferred_element_type=F32)
        product = product + jnp.dot(weights, low_ref[mat], preferred_element_type=F32)
        right = fold(mat, right, product)
    right_ref[...] = right


def reflect(mine, high, low, scale):
    mats, rows, cols = high.shape
    return pl.pallas_call(
        functools.partial(reflect_body, scale),
        out_shape=jax.ShapeDtypeStruct((mats * RANK, cols), F32),
        in_specs=[pl.BlockSpec(memory_space=pltpu.VMEM)] * 3,
        out_specs=pl.BlockSpec(memory_space=pltpu.VMEM),
        compiler_params=pltpu.CompilerParams(vmem_limit_bytes=16 * 2**20),
        cost_estimate=pl.CostEstimate(flops=64 * high.size, bytes_accessed=4 * high.size, transcendentals=0),
        name="reflect",
    )(mine, pltpu.with_memory_space_constraint(high, pltpu.VMEM), pltpu.with_memory_space_constraint(low, pltpu.VMEM))


def turn_body(scale, mine_ref, other_ref, turned_ref, steps_ref, zero_ref):
    zero_ref[...] = jnp.zeros_like(zero_ref)
    left, steps = orthogonal(mine_ref[...] * scale, other_ref[...] * scale)
    for index in range(RANK):
        steps_ref[index] = jnp.broadcast_to(steps[index], steps_ref.shape[1:])
    high, middle, low = thirds(left)
    turned_ref[...] = jnp.concatenate([high, high, high, middle, middle, low], axis=0).T.astype(BF16)


def turn(mine, other, cols, scale):
    count, rows = mine.shape
    return pl.pallas_call(
        functools.partial(turn_body, scale),
        out_shape=(
            pltpu.VMEM((rows, 6 * count), BF16),
            jax.ShapeDtypeStruct((RANK, count, cols), F32),
            jax.ShapeDtypeStruct((count, cols), F32),
        ),
        in_specs=[pl.BlockSpec(memory_space=pltpu.VMEM)] * 2,
        out_specs=[pl.BlockSpec(memory_space=pltpu.VMEM)] * 3,
        compiler_params=pltpu.CompilerParams(vmem_limit_bytes=16 * 2**20),
        cost_estimate=pl.CostEstimate(flops=64 * mine.size, bytes_accessed=128 * mine.size, transcendentals=0),
        name="turn",
    )(mine, other)


def total(own_ref, both_ref, taken_refs, given_refs):
    first = lax.axis_index("tensor") == 0
    terms = {0: own_ref[...], SHARED: both_ref[...]}
    for masks, taken_ref, given_ref in zip(SPLIT, taken_refs, given_refs):
        taken, given = taken_ref[...], given_ref[...]
        terms[masks[0]] = jnp.where(first, taken, given)
        terms[masks[1]] = jnp.where(first, given, taken)
    sums = [terms[index] for index in range(len(terms))]
    while len(sums) > 1:
        sums = [sums[at] + sums[at + 1] for at in range(0, len(sums), 2)]
    return sums[0]


def finish_body(scale, count, left_ref, steps_ref, merged_ref, own_ref, both_ref, *refs):
    taken_refs, given_refs = refs[:count], refs[count : 2 * count]
    update_ref, errors_ref, ubuf, ebuf, sems = refs[2 * count :]
    right = total(own_ref, both_ref, taken_refs, given_refs) * scale
    for index in range(RANK):
        right = row_step(right, pick(right, index, right.shape[0]), steps_ref[index], index)
    finish_rows(right, left_ref, merged_ref, update_ref, errors_ref, ubuf, ebuf, sems)


def finish_rows(right, left_ref, merged_ref, update_ref, errors_ref, ubuf, ebuf, sems):
    mats, rows, cols = merged_ref.shape
    high, middle, low = thirds(right)
    right = jnp.concatenate([high, middle, low, high, middle, high], axis=0)
    row = lax.broadcasted_iota(jnp.int32, right.shape, 0) % (mats * RANK)
    copies = []
    for mat in range(mats):
        weights = jnp.where(row // RANK == mat, right, 0.0).astype(BF16)
        parts = (8, 8, 4, 2) if mat == 0 else (2, 2)
        start = 0
        for chunk, part in enumerate(parts):
            at = pl.ds(start, rows // part)
            start += rows // part
            slot = mat * CHUNKS + chunk
            approx = jnp.dot(left_ref[at], weights, preferred_element_type=F32)
            ubuf[mat, at] = approx.astype(BF16)
            ebuf[mat, at] = merged_ref[mat, at] - approx
            for copy in (
                pltpu.make_async_copy(ubuf.at[mat, at], update_ref.at[mat, at], sems.at[0, slot]),
                pltpu.make_async_copy(ebuf.at[mat, at], errors_ref.at[0, mat, at], sems.at[1, slot]),
            ):
                copy.start()
                copies.append(copy)
    for copy in copies:
        copy.wait()


def finish(left, steps, merged, own, both, taken, given, scale):
    mats, rows, cols = merged.shape
    return pl.pallas_call(
        functools.partial(finish_body, scale, len(taken)),
        out_shape=(
            jax.ShapeDtypeStruct((mats, rows, cols), BF16),
            jax.ShapeDtypeStruct((1, mats, rows, cols), F32),
        ),
        in_specs=[pl.BlockSpec(memory_space=pltpu.VMEM)] * (5 + 2 * len(taken)),
        out_specs=[pl.BlockSpec(memory_space=pltpu.HBM)] * 2,
        scratch_shapes=[
            pltpu.VMEM((mats, rows, cols), BF16),
            pltpu.VMEM((mats, rows, cols), F32),
            pltpu.SemaphoreType.DMA((2, mats * CHUNKS)),
        ],
        compiler_params=pltpu.CompilerParams(vmem_limit_bytes=16 * 2**20),
        name="finish",
    )(
        pltpu.with_memory_space_constraint(left, pltpu.VMEM),
        steps,
        pltpu.with_memory_space_constraint(merged, pltpu.VMEM),
        own,
        both,
        *taken,
        *given,
    )


def swap(value, axes, pairs):
    return lax.ppermute(value, axes, pairs + [(target, source) for source, target in pairs])


def swap_cores(value):
    return swap(value, "tensor", [(0, 1)])


def swap_chips(value, masks, cross=0):
    pairs = []
    for core in range(2):
        for at in range(lax.axis_size("dp")):
            partner = at ^ masks[core]
            if at < partner:
                pairs.append((2 * at + core, 2 * partner + (core ^ cross)))
    return swap(value, ("dp", "tensor"), pairs)


def chips_sum(value, zero):
    count = lax.axis_size("dp")
    last = max(count // 4, 1)
    step = 1
    while step < last:
        value = value + (zero + swap_chips(value, (step, step)))
        zero = 0.0
        step *= 2
    terms = [value] + [swap_chips(value, (offset, offset)) for offset in range(last, count, last)]
    while len(terms) > 1:
        terms = [terms[at] + terms[at + 1] for at in range(0, len(terms), 2)]
    return terms[0]


def chips_terms(value):
    count = lax.axis_size("dp")
    last = count // 8
    step = 1
    while step < last:
        value = value + swap_chips(value, (step, step), 1)
        step *= 2
    both = swap_chips(value, (SHARED * last, SHARED * last), 1)
    taken = [swap_chips(value, (lower * last, upper * last)) for lower, upper in SPLIT[::-1]][::-1]
    return value, both, taken, [swap_cores(term) for term in taken]


def body(grads, errors, seeds):
    replicas = lax.axis_size("dp")
    left_part, grads, errors = project(seeds, grads, errors)
    merged, high, low, zero = merge(grads, errors)
    mine = chips_sum(left_part, zero)
    other = swap_cores(mine)
    right_part = reflect(mine, high, low, 1.0 / replicas)
    left, steps, zero = turn(mine, other, right_part.shape[1], 1.0 / replicas)
    terms = chips_terms(right_part + (zero + swap_cores(right_part)))
    return finish(left, steps, merged, *terms, 1.0 / replicas)


def solution(mesh):
    in_specs = (
        P(("groups", "dp"), None, "tensor", None),
        P(("groups", "dp"), None, "tensor", None),
        P(),
    )
    out_specs = (P("groups", "tensor", None), P(("groups", "dp"), None, "tensor", None))
    return jax.shard_map(body, mesh=mesh, in_specs=in_specs, out_specs=out_specs, check_vma=False)
```

```python
import functools

import jax
import jax.numpy as jnp
from jax import lax
from jax.experimental import pallas as pl
from jax.experimental.pallas import tpu as pltpu
from jax.sharding import PartitionSpec as P

RANK = 4
EPSILON = 1e-08
CHUNKS = 4
SPLIT = ((1, 7), (5, 4), (2, 6))
SHARED = 3
BF16 = jnp.bfloat16
F32 = jnp.float32


def halves(value):
    high = value.astype(BF16).astype(F32)
    return high, value - high


def thirds(value):
    high, rest = halves(value)
    middle, low = halves(rest)
    return high, middle, low


def start_rows(seeds_ref, mats, cols):
    shape = (mats * RANK, cols)
    row = lax.broadcasted_iota(jnp.int32, shape, 0)
    col = lax.broadcasted_iota(jnp.int32, shape, 1)
    mat = row // RANK
    seed = jnp.full(shape, seeds_ref[0], jnp.int32)
    for index in range(1, mats):
        seed = jnp.where(mat == index, seeds_ref[index], seed)
    mixed = ((row - mat * RANK) * cols + col) * 747796405 + seed * 277803737 + 12345
    mixed = mixed ^ (mixed >> 15)
    mixed = mixed * 1274126177
    mixed = mixed ^ (mixed >> 13)
    lowbits = jnp.bitwise_and(mixed, 65535)
    return (lowbits.astype(F32) - 32767.5) / 32768.0


def fold(mat, value, product):
    part = product[: value.shape[0]] + product[value.shape[0] :]
    row = lax.broadcasted_iota(jnp.int32, value.shape, 0)
    return jnp.where(row // RANK == mat, part, value)


def project_body(seeds_ref, grads_ref, errors_ref, left_ref, gbuf, ebuf, seed, seed_sem, sems):
    _, mats, rows, cols = grads_ref.shape
    size = rows // CHUNKS
    seed_copy = pltpu.make_async_copy(seeds_ref, seed, seed_sem)
    seed_copy.start()
    copies = []
    for chunk in range(CHUNKS):
        at = pl.ds(chunk * size, size)
        for mat in range(mats):
            slot = chunk * mats + mat
            copies.append(pltpu.make_async_copy(grads_ref.at[0, mat, at], gbuf.at[mat, at], sems.at[0, slot]))
            copies.append(pltpu.make_async_copy(errors_ref.at[0, mat, at], ebuf.at[mat, at], sems.at[1, slot]))
    for copy in copies:
        copy.start()
    seed_copy.wait()
    start = start_rows(seed, mats, cols)
    weights = jnp.concatenate(halves(start), axis=0).astype(BF16)
    dims = (((1,), (1,)), ((), ()))
    for chunk in range(CHUNKS):
        at = pl.ds(chunk * size, size)
        left = jnp.zeros((mats * RANK, size), F32)
        for copy in copies[2 * mats * chunk : 2 * mats * (chunk + 1)]:
            copy.wait()
        for mat in range(mats):
            value = gbuf[mat, at].astype(F32) + ebuf[mat, at]
            high = value.astype(BF16)
            low = (value - high.astype(F32)).astype(BF16)
            product = lax.dot_general(weights, high, dims, preferred_element_type=F32)
            product = product + lax.dot_general(weights, low, dims, preferred_element_type=F32)
            left = fold(mat, left, product)
        left_ref[:, at] = left


def project(seeds, grads, errors):
    _, mats, rows, cols = grads.shape
    return pl.pallas_call(
        project_body,
        out_shape=(
            jax.ShapeDtypeStruct((mats * RANK, rows), F32),
            pltpu.VMEM((mats, rows, cols), BF16),
            pltpu.VMEM((mats, rows, cols), F32),
        ),
        in_specs=[pl.BlockSpec(memory_space=pltpu.HBM)] * 3,
        out_specs=[pl.BlockSpec(memory_space=pltpu.VMEM)] * 3,
        scratch_shapes=[
            pltpu.SMEM(seeds.shape, seeds.dtype),
            pltpu.SemaphoreType.DMA,
            pltpu.SemaphoreType.DMA((2, mats * CHUNKS)),
        ],
        compiler_params=pltpu.CompilerParams(vmem_limit_bytes=16 * 2**20),
        name="project",
    )(*[pltpu.with_memory_space_constraint(value, pltpu.HBM) for value in (seeds, grads, errors)])


def merge_body(grads_ref, errors_ref, merged_ref, high_ref, low_ref, zero_ref):
    mats, rows, cols = grads_ref.shape
    size = 64
    zero_ref[...] = jnp.zeros_like(zero_ref)

    @pl.loop(0, rows // size)
    def _(step):
        at = pl.ds(pl.multiple_of(step * size, size), size)
        for mat in range(mats):
            value = grads_ref[mat, at].astype(F32) + errors_ref[mat, at]
            high = value.astype(BF16)
            merged_ref[mat, at] = value
            high_ref[mat, at] = high
            low_ref[mat, at] = (value - high.astype(F32)).astype(BF16)


def merge(grads, errors):
    shape = grads.shape
    return pl.pallas_call(
        merge_body,
        out_shape=(
            pltpu.VMEM(shape, F32),
            pltpu.VMEM(shape, BF16),
            pltpu.VMEM(shape, BF16),
            jax.ShapeDtypeStruct((shape[0] * RANK, shape[1]), F32),
        ),
        in_specs=[pl.BlockSpec(memory_space=pltpu.VMEM)] * 2,
        out_specs=[pl.BlockSpec(memory_space=pltpu.VMEM)] * 4,
        compiler_params=pltpu.CompilerParams(vmem_limit_bytes=16 * 2**20),
        cost_estimate=pl.CostEstimate(flops=3 * grads.size, bytes_accessed=14 * grads.size, transcendentals=0),
        name="merge",
    )(*[pltpu.with_memory_space_constraint(value, pltpu.VMEM) for value in (grads, errors)])


def pick(rows, index, count):
    return jnp.concatenate(
        [
            jnp.broadcast_to(rows[start + index : start + index + 1], (RANK, rows.shape[1]))
            for start in range(0, count, RANK)
        ],
        axis=0,
    )


def orthogonal(mine, other):
    count = mine.shape[0]
    rank = lax.broadcasted_iota(jnp.int32, (count, 1), 0) % RANK
    steps = []
    for index in range(RANK):
        current = pick(mine, index, count)
        partner = pick(other, index, count)
        products = jnp.sum(mine * current + other * partner, axis=1, keepdims=True)
        inverse = 1.0 / (jnp.sqrt(pick(products, index, count)) + EPSILON)
        weight = jnp.where(rank > index, products * inverse * inverse, 0.0)
        steps.append(jnp.where(rank == index, inverse, weight))
        mine = row_step(mine, current, steps[-1], index)
        if index < RANK - 1:
            other = row_step(other, partner, steps[-1], index)
    return mine, steps


def row_step(rows, current, step, index):
    rank = lax.broadcasted_iota(jnp.int32, (rows.shape[0], 1), 0) % RANK
    return jnp.where(rank == index, rows * step, rows - step * current)


def reflect_body(scale, mine_ref, high_ref, low_ref, right_ref):
    mats, rows, cols = high_ref.shape
    weights = jnp.concatenate(halves(mine_ref[...] * scale), axis=0).astype(BF16)
    right = jnp.zeros((mats * RANK, cols), F32)
    for mat in range(mats):
        product = jnp.dot(weights, high_ref[mat], preferred_element_type=F32)
        product = product + jnp.dot(weights, low_ref[mat], preferred_element_type=F32)
        right = fold(mat, right, product)
    right_ref[...] = right


def reflect(mine, high, low, scale):
    mats, rows, cols = high.shape
    return pl.pallas_call(
        functools.partial(reflect_body, scale),
        out_shape=jax.ShapeDtypeStruct((mats * RANK, cols), F32),
        in_specs=[pl.BlockSpec(memory_space=pltpu.VMEM)] * 3,
        out_specs=pl.BlockSpec(memory_space=pltpu.VMEM),
        compiler_params=pltpu.CompilerParams(vmem_limit_bytes=16 * 2**20),
        cost_estimate=pl.CostEstimate(flops=64 * high.size, bytes_accessed=4 * high.size, transcendentals=0),
        name="reflect",
    )(mine, pltpu.with_memory_space_constraint(high, pltpu.VMEM), pltpu.with_memory_space_constraint(low, pltpu.VMEM))


def turn_body(scale, mine_ref, other_ref, turned_ref, steps_ref, zero_ref):
    zero_ref[...] = jnp.zeros_like(zero_ref)
    left, steps = orthogonal(mine_ref[...] * scale, other_ref[...] * scale)
    for index in range(RANK):
        steps_ref[index] = jnp.broadcast_to(steps[index], steps_ref.shape[1:])
    high, middle, low = thirds(left)
    turned_ref[...] = jnp.concatenate([high, high, high, middle, middle, low], axis=0).T.astype(BF16)


def turn(mine, other, cols, scale):
    count, rows = mine.shape
    return pl.pallas_call(
        functools.partial(turn_body, scale),
        out_shape=(
            pltpu.VMEM((rows, 6 * count), BF16),
            jax.ShapeDtypeStruct((RANK, count, cols), F32),
            jax.ShapeDtypeStruct((count, cols), F32),
        ),
        in_specs=[pl.BlockSpec(memory_space=pltpu.VMEM)] * 2,
        out_specs=[pl.BlockSpec(memory_space=pltpu.VMEM)] * 3,
        compiler_params=pltpu.CompilerParams(vmem_limit_bytes=16 * 2**20),
        cost_estimate=pl.CostEstimate(flops=64 * mine.size, bytes_accessed=128 * mine.size, transcendentals=0),
        name="turn",
    )(mine, other)


def total(own_ref, both_ref, taken_refs, given_refs):
    first = lax.axis_index("tensor") == 0
    terms = {0: own_ref[...], SHARED: both_ref[...]}
    for masks, taken_ref, given_ref in zip(SPLIT, taken_refs, given_refs):
        taken, given = taken_ref[...], given_ref[...]
        terms[masks[0]] = jnp.where(first, taken, given)
        terms[masks[1]] = jnp.where(first, given, taken)
    sums = [terms[index] for index in range(len(terms))]
    while len(sums) > 1:
        sums = [sums[at] + sums[at + 1] for at in range(0, len(sums), 2)]
    return sums[0]


def finish_body(scale, count, left_ref, steps_ref, merged_ref, own_ref, both_ref, *refs):
    taken_refs, given_refs = refs[:count], refs[count : 2 * count]
    update_ref, errors_ref, ubuf, ebuf, sems = refs[2 * count :]
    right = total(own_ref, both_ref, taken_refs, given_refs) * scale
    for index in range(RANK):
        right = row_step(right, pick(right, index, right.shape[0]), steps_ref[index], index)
    finish_rows(right, left_ref, merged_ref, update_ref, errors_ref, ubuf, ebuf, sems)


def finish_rows(right, left_ref, merged_ref, update_ref, errors_ref, ubuf, ebuf, sems):
    mats, rows, cols = merged_ref.shape
    high, middle, low = thirds(right)
    right = jnp.concatenate([high, middle, low, high, middle, high], axis=0)
    row = lax.broadcasted_iota(jnp.int32, right.shape, 0) % (mats * RANK)
    copies = []
    for mat in range(mats):
        weights = jnp.where(row // RANK == mat, right, 0.0).astype(BF16)
        parts = (8, 8, 4, 2) if mat == 0 else (2, 2)
        start = 0
        for chunk, part in enumerate(parts):
            at = pl.ds(start, rows // part)
            start += rows // part
            slot = mat * CHUNKS + chunk
            approx = jnp.dot(left_ref[at], weights, preferred_element_type=F32)
            ubuf[mat, at] = approx.astype(BF16)
            ebuf[mat, at] = merged_ref[mat, at] - approx
            for copy in (
                pltpu.make_async_copy(ubuf.at[mat, at], update_ref.at[mat, at], sems.at[0, slot]),
                pltpu.make_async_copy(ebuf.at[mat, at], errors_ref.at[0, mat, at], sems.at[1, slot]),
            ):
                copy.start()
                copies.append(copy)
    for copy in copies:
        copy.wait()


def finish(left, steps, merged, own, both, taken, given, scale):
    mats, rows, cols = merged.shape
    return pl.pallas_call(
        functools.partial(finish_body, scale, len(taken)),
        out_shape=(
            jax.ShapeDtypeStruct((mats, rows, cols), BF16),
            jax.ShapeDtypeStruct((1, mats, rows, cols), F32),
        ),
        in_specs=[pl.BlockSpec(memory_space=pltpu.VMEM)] * (5 + 2 * len(taken)),
        out_specs=[pl.BlockSpec(memory_space=pltpu.HBM)] * 2,
        scratch_shapes=[
            pltpu.VMEM((mats, rows, cols), BF16),
            pltpu.VMEM((mats, rows, cols), F32),
            pltpu.SemaphoreType.DMA((2, mats * CHUNKS)),
        ],
        compiler_params=pltpu.CompilerParams(vmem_limit_bytes=16 * 2**20),
        name="finish",
    )(
        pltpu.with_memory_space_constraint(left, pltpu.VMEM),
        steps,
        pltpu.with_memory_space_constraint(merged, pltpu.VMEM),
        own,
        both,
        *taken,
        *given,
    )


def swap(value, axes, pairs):
    return lax.ppermute(value, axes, pairs + [(target, source) for source, target in pairs])


def swap_cores(value):
    return swap(value, "tensor", [(0, 1)])


def swap_chips(value, masks, cross=0):
    pairs = []
    for core in range(2):
        for at in range(lax.axis_size("dp")):
            partner = at ^ masks[core]
            if at < partner:
                pairs.append((2 * at + core, 2 * partner + (core ^ cross)))
    return swap(value, ("dp", "tensor"), pairs)


def chips_sum(value, zero):
    count = lax.axis_size("dp")
    last = max(count // 4, 1)
    step = 1
    while step < last:
        value = value + (swap_chips(value, (step, step)) + zero)
        zero = 0.0
        step *= 2
    terms = [value] + [swap_chips(value, (offset, offset)) for offset in range(last, count, last)]
    while len(terms) > 1:
        terms = [terms[at + 1] + terms[at] for at in range(0, len(terms), 2)]
    return terms[0]


def chips_terms(value):
    count = lax.axis_size("dp")
    last = count // 8
    step = 1
    while step < last:
        value = value + swap_chips(value, (step, step), 1)
        step *= 2
    both = swap_chips(value, (SHARED * last, SHARED * last), 1)
    taken = [swap_chips(value, (lower * last, upper * last)) for lower, upper in SPLIT[::-1]][::-1]
    return value, both, taken, [swap_cores(term) for term in taken]


def body(grads, errors, seeds):
    replicas = lax.axis_size("dp")
    left_part, grads, errors = project(seeds, grads, errors)
    merged, high, low, zero = merge(grads, errors)
    mine = chips_sum(left_part, zero)
    other = swap_cores(mine)
    right_part = reflect(mine, high, low, 1.0 / replicas)
    left, steps, zero = turn(mine, other, right_part.shape[1], 1.0 / replicas)
    terms = chips_terms(right_part + (zero + swap_cores(right_part)))
    return finish(left, steps, merged, *terms, 1.0 / replicas)


def solution(mesh):
    in_specs = (
        P(("groups", "dp"), None, "tensor", None),
        P(("groups", "dp"), None, "tensor", None),
        P(),
    )
    out_specs = (P("groups", "tensor", None), P(("groups", "dp"), None, "tensor", None))
    return jax.shard_map(body, mesh=mesh, in_specs=in_specs, out_specs=out_specs, check_vma=False)
```
